32 devices in a mesh: segment: 4 (over y, x), dom: 8 (over z, core).
Axes of the slice: x: 2, y: 2, z: 4, core: 2. Of those that a mesh axis runs over, the one named last changes fastest.
Arguments:
- features: bfloat16 [4, 4096, 512], P(None, 'dom'), may hold values from -6 to 6
- layer_weights: bfloat16 [8, 1024, 512], P('segment'), may hold values from -0.1875 to 0.1875
- layer_bias: float32 [8, 512], P('segment'), may hold values from -3 to 3
- layer_gain: float32 [8, 512], P('segment'), may hold values from 0.1 to 1.9
- tile_val: bfloat16 [32, 4, 128, 128], P('dom'), may hold values from -0.25 to 0.25
- tile_col: int32 [32, 4], P('dom'), may hold values from 0 to 3
- tile_count: int32 [32], P('dom'), may hold values from 1 to 4, as said below
- cross_val: bfloat16 [8, 32, 128, 128], P('segment', 'dom'), may hold values from -0.5 to 0.5
- send_rows: int32 [8, 1024], P('segment', 'dom'), may hold values from 0 to 511, as said below
Outputs:
- segment_out: bfloat16 [4, 4, 4096, 512], P('segment', None, 'dom')
The draws below stay inside these ranges and needn't reach their ends.
Inputs may be any that keep to these rules, and one draw needn't show every extreme that they name: `tile_count`: in some row block of the graph all 4 slots are live. `send_rows`: each partition's list at a layer holds 128 distinct local node indices and contains 512 - 1.
All inputs are finite; a program needn't handle non-finite values.
Results may differ from the reference program's by a relative error of at most 0.012.
Values may be sent and summed in bfloat16 or wider, within the bound.
No kernel may reach another device: no remote copies, remote signals or barrier semaphores. Data moves between devices by JAX's collectives and lax.ppermute only.
A program may use at most 64 MiB of HBM per device.

```python
import jax
import jax.numpy as jnp
import numpy as np
from jax import lax

D = 512
TILE = 128
SLOTS = 4
LS = 2
BOUND_ROWS = 128
NODES_DEV = 512
MICRO = 4
BLK_DEV = 4
NODES = 4096
NBLK = 32
LAYERS = 8
BOUND = 1024
N_DOM = 8


def draw_tile_count(key, part):
    parts_n = NBLK // BLK_DEV
    key_a = jax.random.fold_in(key, 11)
    key_b = jax.random.fold_in(key, 12)
    key_c = jax.random.fold_in(key, 13)
    key_d = jax.random.fold_in(key, 14)
    level = jax.random.randint(key_a, (parts_n,), 1, SLOTS + 1)
    chosen = jax.random.randint(key_b, (), 0, parts_n)
    level = jnp.where(jnp.arange(parts_n) == chosen, SLOTS, level)
    counts = jax.random.randint(key_c, (parts_n, BLK_DEV), 1, SLOTS + 1)
    counts = jnp.minimum(counts, level[:, None])
    place = jax.random.randint(key_d, (parts_n,), 0, BLK_DEV)
    counts = jnp.where(jnp.arange(BLK_DEV)[None, :] == place[:, None], level[:, None], counts)
    return counts.reshape(NBLK).astype(jnp.int32)


def draw_send_rows(key, part):
    parts_n = BOUND // BOUND_ROWS
    key_a = jax.random.fold_in(key, 21)
    key_b = jax.random.fold_in(key, 22)
    scores = jax.random.randint(key_a, (LAYERS, parts_n, NODES_DEV - 1), 0, 2 ** 16)
    scores = scores * NODES_DEV + jnp.arange(NODES_DEV - 1, dtype=jnp.int32)
    order = jnp.argsort(scores, axis=-1).astype(jnp.int32)
    picked = order[:, :, :BOUND_ROWS - 1]
    last_row = jnp.full((LAYERS, parts_n, 1), NODES_DEV - 1, jnp.int32)
    listed = jnp.concatenate([picked, last_row], axis=-1)
    offset = jax.random.randint(key_b, (LAYERS, parts_n, 1), 0, BOUND_ROWS)
    where_from = (jnp.arange(BOUND_ROWS, dtype=jnp.int32)[None, None, :] + offset) % BOUND_ROWS
    listed = jnp.take_along_axis(listed, where_from, axis=-1)
    return listed.reshape(LAYERS, BOUND).astype(jnp.int32)


def touch_ends(array, key, least, largest):
    longest = array.shape.index(max(array.shape))
    spots = []
    for shift in (0, 1):
        where = [jax.random.randint(jax.random.fold_in(key, axis), (), 0, length) for axis, length in enumerate(array.shape)]
        where[longest] = (where[longest] + shift) % array.shape[longest]
        spots.append(tuple(where))
    return array.at[spots[0]].set(least).at[spots[1]].set(largest)


def steps_of(rng, dims, cuts, low, high):
    def one(axis_at, shards_of):
        draws = jax.random.uniform(jax.random.fold_in(jax.random.fold_in(rng, 6), axis_at), (shards_of,), jnp.float32, low / len(cuts), high / len(cuts))
        return jnp.repeat(jnp.exp(draws), dims[axis_at] // shards_of).reshape((-1,) + (1,) * (len(dims) - axis_at - 1))

    factor_of = one(*cuts[0])
    for cut in cuts[1:]:
        factor_of = factor_of * one(*cut)
    return factor_of


def normal_values(stream_key, shape, scale, reach, pieces=(), kind=jnp.bfloat16):
    drawn = scale * jax.random.normal(stream_key, shape, jnp.float32)
    if pieces:
        drawn = drawn * steps_of(stream_key, shape, pieces, -0.22, 0.18)
    return jnp.clip(drawn, -reach, reach).astype(kind)


def setup_inputs(seed: int = 0) -> dict:
    key_of = jax.random.split(jax.random.key(seed), 10)
    features = normal_values(key_of[0], (MICRO, NODES, D), 1.0, 6.0, ((1, 8),))
    layer_weights = normal_values(key_of[1], (LAYERS, 2 * D, D), (2 * D) ** -0.5, 0.1875, ((0, 4),))
    layer_bias = normal_values(key_of[2], (LAYERS, D), 0.5, 3.0, ((0, 4),), jnp.float32)
    layer_gain = jnp.clip(1.0 + 0.18 * jax.random.normal(key_of[3], (LAYERS, D), jnp.float32), 0.1, 1.9)
    tile_val = normal_values(key_of[4], (NBLK, SLOTS, TILE, TILE), (TILE * SLOTS) ** -0.5, 0.25, ((0, 8),))
    tile_col = touch_ends(jax.random.randint(key_of[5], (NBLK, SLOTS), 0, BLK_DEV), jax.random.fold_in(key_of[5], 1), 0, BLK_DEV - 1).astype(jnp.int32)
    tile_count = draw_tile_count(jax.random.fold_in(key_of[9], 71), 0)
    cross_val = normal_values(key_of[7], (LAYERS, NBLK, TILE, BOUND_ROWS), BOUND_ROWS ** -0.5, 0.5, ((0, 4), (1, 8)))
    send_rows = draw_send_rows(jax.random.fold_in(key_of[9], 71), 0)
    return {"features": features, "layer_weights": layer_weights, "layer_bias": layer_bias, "layer_gain": layer_gain, "tile_val": tile_val, "tile_col": tile_col, "tile_count": tile_count, "cross_val": cross_val, "send_rows": send_rows}


def one_layer(h, layer, layer_weights, layer_bias, layer_gain, tile_val, gidx, tile_count, cross_val, send_rows):
    hf = h.astype(jnp.float32)
    meansq = lax.optimization_barrier(jnp.mean(hf * hf, axis=-1, keepdims=True))
    x = (hf * lax.rsqrt(meansq + 1e-05) * layer_gain[layer]).astype(jnp.bfloat16)
    nbits = N_DOM.bit_length() - 1
    slot_pos = layer % LS
    bit = slot_pos * (nbits - 1) // max(LS - 1, 1)
    partner = np.arange(N_DOM) ^ 1 << bit
    parted = x.reshape(N_DOM, NODES_DEV, D)
    rows = send_rows[layer].reshape(N_DOM, BOUND_ROWS).astype(jnp.int32)
    sent = jnp.take_along_axis(parted, rows[:, :, None], axis=1)
    recv = sent[partner]
    blocks = x.reshape(NBLK, TILE, D)
    acc = jnp.zeros((NBLK, TILE, D), jnp.float32)
    for slot in range(SLOTS):
        source = blocks[gidx[:, slot]].astype(jnp.float32)
        tiles = tile_val[:, slot].astype(jnp.float32)
        live = (slot < tile_count)[:, None, None]
        prod = jnp.einsum('bij,bjd->bid', tiles, source)
        acc = acc + jnp.where(live, prod, jnp.float32(0.0))
    cross = cross_val[layer].reshape(N_DOM, BLK_DEV, TILE, BOUND_ROWS).astype(jnp.float32)
    remote = jnp.einsum('pbir,prd->pbid', cross, recv.astype(jnp.float32))
    acc = acc + remote.reshape(NBLK, TILE, D)
    agg = acc.reshape(NODES, D).astype(jnp.bfloat16)
    z = jnp.dot(x, layer_weights[layer, :D], preferred_element_type=jnp.float32)
    z = z + jnp.dot(agg, layer_weights[layer, D:], preferred_element_type=jnp.float32)
    z = z + layer_bias[layer]
    return (hf + jax.nn.silu(z)).astype(jnp.bfloat16)

def reference(features, layer_weights, layer_bias, layer_gain, tile_val, tile_col, tile_count, cross_val, send_rows):
    base = jnp.arange(NBLK, dtype=jnp.int32) // BLK_DEV * BLK_DEV
    gidx = (base[:, None] + tile_col).astype(jnp.int32)
    per_micro = []
    for micro_id in range(MICRO):
        h = features[micro_id]
        per_segment = []
        for layer in range(LAYERS):
            h = one_layer(h, layer, layer_weights, layer_bias, layer_gain, tile_val, gidx, tile_count, cross_val, send_rows)
            if layer % LS == LS - 1:
                per_segment.append(h)
        per_micro.append(jnp.stack(per_segment))
    return jnp.stack(per_micro, axis=1)
```

```python
import functools

import jax
import jax.numpy as jnp
from jax import lax
from jax.experimental import pallas as pl
from jax.experimental.pallas import tpu as pltpu
from jax.sharding import PartitionSpec as P

F32 = jnp.float32
BF16 = jnp.bfloat16
VMEM_BYTES = 24 * 2**20


def call(body, outs, in_specs, scratch=(), flops=0, moved=0):
    return pl.pallas_call(
        body,
        out_shape=outs,
        in_specs=in_specs,
        out_specs=jax.tree.map(lambda _: pl.BlockSpec(memory_space=pltpu.VMEM), outs),
        scratch_shapes=scratch,
        compiler_params=pltpu.CompilerParams(vmem_limit_bytes=VMEM_BYTES),
        cost_estimate=pl.CostEstimate(flops=flops, bytes_accessed=moved, transcendentals=0),
    )


VM = pl.BlockSpec(memory_space=pltpu.VMEM)
SM = pl.BlockSpec(memory_space=pltpu.SMEM)
ANY = pl.BlockSpec(memory_space=pl.ANY)


def normed(h, gain):
    hf = h.astype(F32)
    meansq = jnp.mean(hf * hf, axis=-1, keepdims=True)
    return (hf * lax.rsqrt(meansq + 1e-05) * gain).astype(BF16)


def picked_rows(small_ref, layer, width, x):
    rows = small_ref[layer : layer + 1, 2 * width :]
    count = x.shape[0]
    index = lax.broadcasted_iota(jnp.int32, (count, rows.shape[1]), 0).astype(F32)
    chosen = (index == rows).astype(BF16)
    return lax.dot_general(chosen, x, (((0,), (0,)), ((), ())), preferred_element_type=F32).astype(BF16)


def first_kernel(ids, cols, counts, feat_ref, tiles_ref, small_ref, h_ref, adj_ref, x_ref, sent_ref):
    nblk, slots, tile, _ = tiles_ref.shape
    width = h_ref.shape[1]
    h = feat_ref[ids[0]]
    h_ref[...] = h
    x = normed(h, small_ref[0:1, width : 2 * width])
    x_ref[...] = x
    sent_ref[...] = picked_rows(small_ref, 0, width, x)
    for r in range(nblk):
        for j in range(nblk):
            total = jnp.zeros((tile, tile), F32)
            for k in range(slots):
                used = jnp.logical_and(k < counts[r], cols[r, k] == j)
                total = total + jnp.where(used, tiles_ref[r, k].astype(F32), 0.0)
            adj_ref[r * tile : (r + 1) * tile, j * tile : (j + 1) * tile] = total.astype(BF16)


def fetch_half(top, ids, mine_ref, other_ref, w_ref, sem):
    @pl.when(ids[1] == (0 if top else 1))
    def _():
        pltpu.make_async_copy(mine_ref, w_ref, sem).start()

    @pl.when(ids[1] != (0 if top else 1))
    def _():
        pltpu.make_async_copy(other_ref, w_ref, sem).start()

    return pltpu.make_async_copy(mine_ref, w_ref, sem)


def local_kernel(layer, ids, x_ref, adj_ref, mine_ref, other_ref, small_ref, agg_ref, z_ref, w_ref, sem):
    width = x_ref.shape[1]
    weights = fetch_half(True, ids, mine_ref, other_ref, w_ref, sem)
    x = x_ref[...]
    agg_ref[...] = jnp.dot(adj_ref[...], x, preferred_element_type=F32)
    weights.wait()
    z_ref[...] = jnp.dot(x, w_ref[...], preferred_element_type=F32) + small_ref[layer : layer + 1, :width]


def finish_kernel(section, layer, last, ids, agg_ref, z_ref, recv_ref, cross_ref, mine_ref, other_ref, h_ref, small_ref, *rest):
    if last:
        h_out, w_ref, c_ref, sem, c_sem = rest
    else:
        h_out, x_ref, sent_ref, w_ref, c_ref, sem, c_sem = rest
    width = h_ref.shape[1]
    tiles = pltpu.make_async_copy(cross_ref.at[section], c_ref, c_sem)
    tiles.start()
    weights = fetch_half(False, ids, mine_ref, other_ref, w_ref, sem)
    tiles.wait()
    agg = agg_ref[...] + jnp.dot(c_ref[...], recv_ref[...], preferred_element_type=F32)
    agg = agg.astype(BF16)
    weights.wait()
    z = z_ref[...] + jnp.dot(agg, w_ref[...], preferred_element_type=F32)
    h = (h_ref[...].astype(F32) + z / (1.0 + jnp.exp(-z))).astype(BF16)
    h_out[...] = h
    if not last:
        x = normed(h, small_ref[layer + 1 : layer + 2, width : 2 * width])
        x_ref[...] = x
        sent_ref[...] = picked_rows(small_ref, layer + 1, width, x)


def shards(features, weights, bias, gain, tile_val, tile_col, tile_count, cross_val, send_rows):
    sections = lax.axis_size("segment")
    doms = lax.axis_size("dom")
    seg = lax.axis_index("segment")
    core = lax.axis_index("dom") & 1
    steps, _, width = weights.shape
    nodes = features.shape[1]
    bound = send_rows.shape[1]
    layers = steps * sections
    nbits = doms.bit_length() - 1
    ids = jnp.stack([seg, core]).astype(jnp.int32)

    def moved(value, target):
        pairs = []
        for s in range(sections):
            for d in range(doms):
                t, e = target(s, d)
                pairs.append((s * doms + d, t * doms + e))
        return lax.ppermute(value, ("segment", "dom"), pairs)

    def near(s, d):
        return s ^ (1 + (d & 1)), d

    def far(s, d):
        return s ^ (2 - (d & 1)), d

    def sibling(s, d):
        return s, d ^ 1

    small = jnp.concatenate([bias, gain, send_rows.astype(F32)], axis=1)
    small = lax.all_gather(small, "segment", axis=0, tiled=True)
    cross = cross_val.reshape(steps, nodes, bound)
    crosses = [lax.all_gather(cross[p], "segment", axis=0) for p in range(steps)]

    own, first, second, third = [], [], [], []
    middle = (seg == 1) | (seg == 2)
    for p in range(steps):
        u = lax.dynamic_slice(weights, (p, core * width, 0), (1, width, width))[0]
        a = moved(u, near)
        b = moved(jnp.where(middle, a, u), far)
        own.append(u)
        first.append(a)
        second.append(b)
    for p in range(steps):
        third.append(moved(jnp.where(middle, own[p], first[p]), far))
    near_to = seg ^ (1 + core)
    far_to = seg ^ (2 - core)
    in_second = jnp.where((far_to == 1) | (far_to == 2), seg ^ 3, far_to)

    halves = []
    for layer in range(layers):
        k, p = divmod(layer, steps)
        rest = second[p] if k == 0 else jnp.where(in_second == k, second[p], third[p])
        mine = jnp.where(seg == k, own[p], jnp.where(near_to == k, first[p], rest))
        halves.append((mine, moved(mine, sibling)))

    mat = jax.ShapeDtypeStruct((nodes, width), BF16)
    mat32 = jax.ShapeDtypeStruct((nodes, width), F32)
    edge = jax.ShapeDtypeStruct((bound, width), BF16)
    adj_shape = jax.ShapeDtypeStruct((nodes, nodes), BF16)
    h, adj, x, sent = call(
        first_kernel,
        (mat, adj_shape, mat, edge),
        [SM, SM, SM, VM, VM, VM],
        flops=2 * bound * nodes * width,
        moved=2**22,
    )(ids, tile_col, tile_count, features, tile_val, small)

    ends = []
    for layer in range(layers):
        k, p = divmod(layer, steps)
        bit = p * (nbits - 1) // max(steps - 1, 1)
        recv = lax.ppermute(sent, "dom", [(i, i ^ 1 << bit) for i in range(doms)])
        mine, other = halves[layer]
        agg, z = call(
            functools.partial(local_kernel, layer),
            (mat32, mat32),
            [SM, VM, VM, ANY, ANY, VM],
            scratch=[pltpu.VMEM((width, width), BF16), pltpu.SemaphoreType.DMA],
            flops=4 * nodes * nodes * width,
            moved=2**22,
        )(ids, x, adj, mine, other, small)
        last = layer == layers - 1
        out = call(
            functools.partial(finish_kernel, k, layer, last),
            (mat,) if last else (mat, mat, edge),
            [SM, VM, VM, VM, ANY, ANY, ANY, VM, VM],
            scratch=[
                pltpu.VMEM((width, width), BF16),
                pltpu.VMEM((nodes, bound), BF16),
                pltpu.SemaphoreType.DMA,
                pltpu.SemaphoreType.DMA,
            ],
            flops=3 * nodes * nodes * width,
            moved=2**22,
        )(ids, agg, z, recv, crosses[p], mine, other, h, small)
        h = out[0]
        if not last:
            x, sent = out[1:]
        if p == steps - 1:
            ends.append(h)
    stacked = jnp.stack(ends)
    got = lax.all_to_all(stacked, "segment", 0, 0)
    return got[None]


def solution(mesh):
    in_specs = (
        P(None, "dom", None),
        P("segment", None, None),
        P("segment", None),
        P("segment", None),
        P("dom", None, None, None),
        P("dom", None),
        P("dom"),
        P("segment", "dom", None, None),
        P("segment", "dom"),
    )
    out_specs = P("segment", None, "dom", None)
    return jax.shard_map(shards, mesh=mesh, in_specs=in_specs, out_specs=out_specs, check_vma=False)
```

```python
import functools

import jax
import jax.numpy as jnp
from jax import lax
from jax.experimental import pallas as pl
from jax.experimental.pallas import tpu as pltpu
from jax.sharding import PartitionSpec as P

F32 = jnp.float32
BF16 = jnp.bfloat16
VMEM_BYTES = 24 * 2**20
VM = pl.BlockSpec(memory_space=pltpu.VMEM)
SM = pl.BlockSpec(memory_space=pltpu.SMEM)
ANY = pl.BlockSpec(memory_space=pl.ANY)


def call(body, outs, in_specs, scratch=(), flops=0, moved=0, out_specs=None):
    if out_specs is None:
        out_specs = jax.tree.map(lambda _: VM, outs)
    return pl.pallas_call(
        body,
        out_shape=outs,
        in_specs=in_specs,
        out_specs=out_specs,
        scratch_shapes=scratch,
        compiler_params=pltpu.CompilerParams(vmem_limit_bytes=VMEM_BYTES),
        cost_estimate=pl.CostEstimate(flops=flops, bytes_accessed=moved, transcendentals=0),
    )


def dot(a, b):
    return jnp.dot(a, b, preferred_element_type=F32)


def normed(hf, gain):
    meansq = jnp.mean(hf * hf, axis=-1, keepdims=True)
    return (hf * lax.rsqrt(meansq + 1e-05) * gain).astype(BF16)


def stepped(h, z):
    return (h.astype(F32) + z / (1.0 + jnp.exp(-z))).astype(BF16)


def start_one(choices, dst, sem):
    for condition, source in choices:

        @pl.when(condition)
        def _():
            pltpu.make_async_copy(source, dst, sem).start()

    return pltpu.make_async_copy(choices[0][1], dst, sem)


def fetch_half(seg, core, section, step, half, own, mine, theirs, dst, sem):
    width = dst.shape[1]
    near, far = 1 + half, 2 - half
    via = seg ^ far
    passed = jnp.logical_or(via == 1, via == 2)
    second = jnp.where(passed, seg ^ 3, via)
    home = seg == section
    in_first = (seg ^ near) == section
    in_second = second == section
    choices = [(home, own.at[step, pl.ds(half * width, width), :])]
    for here, refs in ((core == half, mine), (core != half, theirs)):
        choices.append((jnp.logical_and(here, in_first), refs[0]))
        if len(refs) == 2:
            left = jnp.logical_not(jnp.logical_or(home, in_first))
            choices.append((jnp.logical_and(here, left), refs[1]))
        else:
            choices.append((jnp.logical_and(here, in_second), refs[1]))
            left = jnp.logical_not(jnp.logical_or(jnp.logical_or(home, in_first), in_second))
            choices.append((jnp.logical_and(here, left), refs[2]))
    return start_one(choices, dst, sem)


def fetch_cross(seg, section, step, own, others, dst, sem):
    apart = seg ^ section
    choices = [(apart == 0, own.at[step])]
    for r, ref in enumerate(others):
        choices.append((apart == r + 1, ref))
    return start_one(choices, dst, sem)


def fetch_layer(section, step, ids, cands, top, bottom, cross, sems):
    own, mine, theirs, own_cross, crosses = cands
    seg, core = ids[0], ids[1]
    return (
        fetch_half(seg, core, section, step, 0, own, mine, theirs, top, sems.at[0]),
        fetch_half(seg, core, section, step, 1, own, mine, theirs, bottom, sems.at[1]),
        fetch_cross(seg, section, step, own_cross, crosses, cross, sems.at[2]),
    )


def cands_of(refs, section):
    n = 2 if section == 0 else 3
    return refs[0], refs[1 : 1 + n], refs[1 + n : 1 + 2 * n], refs[1 + 2 * n], refs[2 + 2 * n :]


def first_kernel(ids, cols, counts, feat_ref, tiles_ref, s0, s1, s2, s3, h_ref, adj_ref, x_ref, sent_ref, small_ref, pick_ref, sem):
    nblk, slots, tile, _ = tiles_ref.shape
    nodes, width = h_ref.shape
    seg = ids[0]
    copy = pltpu.make_async_copy(feat_ref.at[seg], h_ref, sem)
    copy.start()
    for r in range(nblk):
        for j in range(nblk):
            total = jnp.zeros((tile, tile), F32)
            for k in range(slots):
                used = jnp.logical_and(k < counts[r], cols[r, k] == j)
                total = total + jnp.where(used, tiles_ref[r, k].astype(F32), 0.0)
            adj_ref[r * tile : (r + 1) * tile, j * tile : (j + 1) * tile] = total.astype(BF16)
    for r, ref in enumerate((s0, s1, s2, s3)):
        small_ref[seg ^ r] = ref[...]
    sections, steps = small_ref.shape[:2]
    bound = small_ref.shape[2] - 2 * width
    for k in range(sections):
        for p in range(steps):
            rows = small_ref[k, p : p + 1, 2 * width :]
            index = lax.broadcasted_iota(jnp.int32, (nodes, bound), 0).astype(F32)
            pick_ref[k, p] = jnp.where(index == rows, 1.0, 0.0).T.astype(BF16)
    copy.wait()
    x = normed(h_ref[...].astype(F32), small_ref[0, 0:1, width : 2 * width])
    x_ref[...] = x
    sent_ref[...] = dot(pick_ref[0, 0], x).astype(BF16)


def load_kernel(ids, *refs):
    cands, (w_ref, c_ref, sems) = cands_of(refs[:-3], 0), refs[-3:]
    width = w_ref.shape[1]
    for copy in fetch_layer(0, 0, ids, cands, w_ref.at[pl.ds(0, width), :], w_ref.at[pl.ds(width, width), :], c_ref, sems):
        copy.wait()


def edge_kernel(section, x_ref, h_ref, adj_ref, w_ref, c_ref, small_ref, pick_ref, agg_ref, z_ref, cross_ref, h_out):
    width = x_ref.shape[1]
    pick = pick_ref[section, 1]
    x = x_ref[...]
    adj = dot(pick, adj_ref[...]).astype(BF16)
    agg_ref[...] = dot(adj, x)
    xb = dot(pick, x).astype(BF16)
    z_ref[...] = dot(xb, w_ref[:width, :]) + small_ref[section, 0:1, :width]
    cross_ref[...] = dot(pick, c_ref[...]).astype(BF16)
    h_out[...] = dot(pick, h_ref[...]).astype(BF16)


def send_kernel(section, recv_ref, agg_ref, z_ref, cross_ref, h_ref, w_ref, small_ref, sent_ref):
    width = h_ref.shape[1]
    agg = (agg_ref[...] + dot(cross_ref[...], recv_ref[...])).astype(BF16)
    z = z_ref[...] + dot(agg, w_ref[width:, :])
    h = stepped(h_ref[...], z)
    sent_ref[...] = normed(h.astype(F32), small_ref[section, 1:2, width : 2 * width])


def middle_kernel(section, ids, x_ref, h_ref, adj_ref, recv_ref, w_ref, c_ref, small_ref, *refs):
    h_out, agg_out, z_out, w2_out, c_out, w1_ref, x2_ref, sems = refs[-8:]
    nodes, width = x_ref.shape
    block = 256
    copies = fetch_layer(section, 1, ids, cands_of(refs[:-8], section), w1_ref, w2_out, c_out, sems)

    def even(i, carry):
        rows = pl.ds(pl.multiple_of(i * block, block), block)
        agg = dot(adj_ref[rows, :], x_ref[...]) + dot(c_ref[rows, :], recv_ref[...])
        z = dot(x_ref[rows, :], w_ref[:width, :]) + small_ref[section, 0:1, :width]
        z = z + dot(agg.astype(BF16), w_ref[width:, :])
        h = stepped(h_ref[rows, :], z)
        h_out[rows, :] = h
        x2_ref[rows, :] = normed(h.astype(F32), small_ref[section, 1:2, width : 2 * width])
        return carry

    lax.fori_loop(0, nodes // block, even, 0)
    copies[0].wait()

    def odd(i, carry):
        rows = pl.ds(pl.multiple_of(i * block, block), block)
        agg_out[rows, :] = dot(adj_ref[rows, :], x2_ref[...])
        z_out[rows, :] = dot(x2_ref[rows, :], w1_ref[...]) + small_ref[section, 1:2, :width]
        return carry

    lax.fori_loop(0, nodes // block, odd, 0)
    copies[1].wait()
    copies[2].wait()


def finish_kernel(section, last, ids, recv_ref, agg_ref, z_ref, w2_ref, c_ref, h_ref, small_ref, pick_ref, *refs):
    if last:
        (h_out,) = refs
    else:
        h_out, x_out, sent_out, w_out, c_out, sems = refs[-6:]
    nodes, width = h_ref.shape
    block = 256
    if not last:
        tops = w_out.at[pl.ds(0, width), :], w_out.at[pl.ds(width, width), :]
        copies = fetch_layer(section + 1, 0, ids, cands_of(refs[:-6], section + 1), *tops, c_out, sems)

    def odd(i, carry):
        rows = pl.ds(pl.multiple_of(i * block, block), block)
        agg = agg_ref[rows, :] + dot(c_ref[rows, :], recv_ref[...])
        z = z_ref[rows, :] + dot(agg.astype(BF16), w2_ref[...])
        h = stepped(h_ref[rows, :], z)
        h_out[rows, :] = h
        if not last:
            x_out[rows, :] = normed(h.astype(F32), small_ref[section + 1, 0:1, width : 2 * width])
        return carry

    lax.fori_loop(0, nodes // block, odd, 0)
    if not last:
        sent_out[...] = dot(pick_ref[section + 1, 0], x_out[...]).astype(BF16)
        for copy in copies:
            copy.wait()


def collect_kernel(sections, ids, *refs):
    ends, got, (out_ref, sems) = refs[:sections], refs[sections:-2], refs[-2:]
    for k in range(sections):

        @pl.when(ids[0] == k)
        def _():
            copies = [pltpu.make_async_copy(ends[k], out_ref.at[0, k], sems.at[0])]
            for r in range(1, sections):
                ref = got[k * (sections - 1) + r - 1]
                copies.append(pltpu.make_async_copy(ref, out_ref.at[0, k ^ r], sems.at[r]))
            for copy in copies:
                copy.start()
            for copy in copies:
                copy.wait()


def shards(features, weights, bias, gain, tile_val, tile_col, tile_count, cross_val, send_rows):
    sections = lax.axis_size("segment")
    doms = lax.axis_size("dom")
    seg = lax.axis_index("segment")
    core = lax.axis_index("dom") & 1
    steps, _, width = weights.shape
    nodes = features.shape[1]
    bound = send_rows.shape[1]
    nbits = doms.bit_length() - 1
    ids = jnp.stack([seg, core]).astype(jnp.int32)

    def moved(value, target, sources=range(sections)):
        pairs = []
        for s in sources:
            for d in range(doms):
                t, e = target(s, d)
                pairs.append((s * doms + d, t * doms + e))
        return lax.ppermute(value, ("segment", "dom"), pairs)

    def near(s, d):
        return s ^ (1 + (d & 1)), d

    def far(s, d):
        return s ^ (2 - (d & 1)), d

    def sibling(s, d):
        return s, d ^ 1

    def across(r):
        return lambda s, d: (s ^ r, d)

    def exchange(sent, step):
        bit = step * (nbits - 1) // max(steps - 1, 1)
        return lax.ppermute(sent, "dom", [(i, i ^ 1 << bit) for i in range(doms)])

    after = lax.optimization_barrier

    small = jnp.concatenate([bias, gain, send_rows.astype(F32)], axis=1)
    smalls = [small] + [moved(small, across(r)) for r in range(1, sections)]

    middle = (seg == 1) | (seg == 2)
    cross = cross_val.reshape(steps, nodes, bound)
    own = [lax.dynamic_slice(weights, (p, core * width, 0), (1, width, width))[0] for p in range(steps)]
    first, second, third, crosses = [], [], [], []
    first.append(moved(own[0], near))
    for p in range(steps):
        u, a = own[p], first[p]
        b = moved(jnp.where(middle, a, u), far)
        second.append(b)
        cross_p, a = after((cross[p], a))
        crosses.append([moved(cross_p, across(r)) for r in range(1, sections)])
        if p + 1 < steps:
            nxt, a = after((own[p + 1], a))
            first.append(moved(nxt, near))
    for p in range(steps):
        pay, _ = after((jnp.where(middle, own[p], first[p]), second[-1] if p == 0 else third[-1]))
        third.append(moved(pay, far))

    brought = [(first[p], second[p], third[p]) for p in range(steps)]
    swapped = [tuple(moved(v, sibling) for v in brought[p]) for p in range(steps)]

    def candidates(section, p):
        n = 2 if section == 0 else 3
        return [weights, *brought[p][:n], *swapped[p][:n], cross, *crosses[p]]

    mat = jax.ShapeDtypeStruct((nodes, width), BF16)
    mat32 = jax.ShapeDtypeStruct((nodes, width), F32)
    edge = jax.ShapeDtypeStruct((bound, width), BF16)
    edge32 = jax.ShapeDtypeStruct((bound, width), F32)
    half = jax.ShapeDtypeStruct((width, width), BF16)
    both = jax.ShapeDtypeStruct((2 * width, width), BF16)
    tiles = jax.ShapeDtypeStruct((nodes, bound), BF16)
    picks = jax.ShapeDtypeStruct((sections, steps, bound, nodes), BF16)
    dma3 = pltpu.SemaphoreType.DMA((3,))
    unit = 2 * nodes * width * width

    h, adj, x, sent, small, pick = call(
        first_kernel,
        (mat, jax.ShapeDtypeStruct((nodes, nodes), BF16), mat, edge, jax.ShapeDtypeStruct((sections,) + small.shape, F32), picks),
        [SM, SM, SM, ANY, VM] + [VM] * sections,
        scratch=[pltpu.SemaphoreType.DMA],
        flops=unit,
    )(ids, tile_col, tile_count, features, tile_val, *smalls)
    cands = candidates(0, 0)
    w, c = call(load_kernel, (both, tiles), [SM] + [ANY] * len(cands), scratch=[dma3], flops=unit)(ids, *cands)

    ends, got = [], []
    for k in range(sections):
        last = k == sections - 1
        recv = exchange(sent, 0)
        edges = call(
            functools.partial(edge_kernel, k),
            (edge32, edge32, jax.ShapeDtypeStruct((bound, bound), BF16), edge),
            [VM] * 7,
            flops=unit,
        )(x, h, adj, w, c, small, pick)
        sent = call(functools.partial(send_kernel, k), edge, [VM] * 7, flops=unit)(recv, *edges[:3], edges[3], w, small)
        recv2 = exchange(sent, 1)
        cands = candidates(k, 1)
        h, agg, z, w2, c2 = call(
            functools.partial(middle_kernel, k),
            (mat, mat32, mat32, half, tiles),
            [SM] + [VM] * 7 + [ANY] * len(cands),
            scratch=[pltpu.VMEM((width, width), BF16), pltpu.VMEM((nodes, width), BF16), dma3],
            flops=4 * unit,
        )(ids, x, h, adj, recv, w, c, small, *cands)
        cands = [] if last else candidates(k + 1, 0)
        out = call(
            functools.partial(finish_kernel, k, last),
            (mat,) if last else (mat, mat, edge, both, tiles),
            [SM] + [VM] * 8 + [ANY] * len(cands),
            scratch=[] if last else [dma3],
            flops=2 * unit,
        )(ids, recv2, agg, z, w2, c2, h, small, pick, *cands)
        h = out[0]
        if not last:
            x, sent, w, c = out[1:]
        ends.append(h)
        for r in range(1, sections):
            got.append(moved(h, across(r), sources=[k ^ r]))
    return call(
        functools.partial(collect_kernel, sections),
        jax.ShapeDtypeStruct((1, sections, nodes, width), BF16),
        [SM] + [ANY] * (len(ends) + len(got)),
        scratch=[pltpu.SemaphoreType.DMA((sections,))],
        out_specs=ANY,
    )(ids, *ends, *got)


def solution(mesh):
    in_specs = (
        P(None, "dom", None),
        P("segment", None, None),
        P("segment", None),
        P("segment", None),
        P("dom", None, None, None),
        P("dom", None),
        P("dom"),
        P("segment", "dom", None, None),
        P("segment", "dom"),
    )
    out_specs = P("segment", None, "dom", None)
    return jax.shard_map(shards, mesh=mesh, in_specs=in_specs, out_specs=out_specs, check_vma=False)
```

```python
import functools

import jax
import jax.numpy as jnp
from jax import lax
from jax.experimental import pallas as pl
from jax.experimental.pallas import tpu as pltpu
from jax.sharding import PartitionSpec as P

F32 = jnp.float32
BF16 = jnp.bfloat16
VMEM_BYTES = 24 * 2**20
LOAD = 4
VM = pl.BlockSpec(memory_space=pltpu.VMEM)
SM = pl.BlockSpec(memory_space=pltpu.SMEM)
ANY = pl.BlockSpec(memory_space=pl.ANY)
HBM = pl.BlockSpec(memory_space=pltpu.HBM)


def call(body, outs, in_specs, scratch=(), out_specs=None, flops=0):
    if out_specs is None:
        out_specs = jax.tree.map(lambda _: VM, outs)
    inner = body.func if isinstance(body, functools.partial) else body
    return pl.pallas_call(
        body,
        name=inner.__name__,
        out_shape=outs,
        in_specs=in_specs,
        out_specs=out_specs,
        scratch_shapes=scratch,
        compiler_params=pltpu.CompilerParams(vmem_limit_bytes=VMEM_BYTES),
        cost_estimate=pl.CostEstimate(flops=int(flops), bytes_accessed=0, transcendentals=0),
    )


def dot(a, b):
    return jnp.dot(a, b, preferred_element_type=F32)


def aligned(start, unit):
    return start if isinstance(start, int) else pl.multiple_of(start, unit)


def normed(hf, gain):
    meansq = jnp.mean(hf * hf, axis=-1, keepdims=True)
    return (hf * lax.rsqrt(meansq + 1e-05) * gain).astype(BF16)


def stepped(h, z):
    return (h.astype(F32) + z / (1.0 + jnp.exp(-z))).astype(BF16)


def start_one(choices, dst, sem):
    for condition, source in choices:

        @pl.when(condition)
        def _():
            pltpu.make_async_copy(source, dst, sem).start()

    return pltpu.make_async_copy(choices[0][1], dst, sem)


def source_of(seg, section, half):
    near, far = 1 + half, 2 - half
    via = seg ^ far
    passed = jnp.logical_or(via == 1, via == 2)
    second = jnp.where(passed, seg ^ 3, via)
    return jnp.where(seg == section, 0, jnp.where((seg ^ near) == section, 1, jnp.where(second == section, 2, 3)))


def fetch_half(seg, core, section, half, own, mine, theirs, dst, sem):
    width = dst.shape[1]
    source = source_of(seg, section, half)
    choices = [(source == 0, own.at[pl.ds(half * width, width), :])]
    for here, refs in ((core == half, mine), (core != half, theirs)):
        for i, (ref, row) in enumerate(refs):
            choices.append((jnp.logical_and(here, source == i + 1), ref.at[pl.ds(row, width), :]))
    return [start_one(choices, dst, sem)]


def fetch_cross(seg, core, section, own, mine, dst, sems):
    tile = dst.shape[0]
    width = dst.shape[1]
    blocks = own.shape[0]
    source = jnp.where(core == 0, source_of(seg, section, 0), source_of(seg, section, 1))
    for i, (ref, _) in enumerate(mine):

        @pl.when(source == i + 1)
        def _():
            for b in range(blocks):
                part = ref.at[pl.ds(width, tile), pl.ds(b * tile, tile)]
                pltpu.make_async_copy(part, dst.at[:, pl.ds(b * tile, tile)], sems.at[b]).start()

    @pl.when(source == 0)
    def _():
        for b in range(blocks):
            pltpu.make_async_copy(own.at[b], dst.at[:, pl.ds(b * tile, tile)], sems.at[b]).start()

    return [pltpu.make_async_copy(own.at[b], dst.at[:, pl.ds(b * tile, tile)], sems.at[b]) for b in range(blocks)]


def fetch_layer(section, step, ids, cands, top, bottom, cross, sems):
    own, own_cross, mine, theirs = cands
    seg, core = ids[0], ids[1]
    return (
        fetch_half(seg, core, section, 0, own.at[step], mine, theirs, top, sems.at[0])
        + fetch_half(seg, core, section, 1, own.at[step], mine, theirs, bottom, sems.at[1])
        + fetch_cross(seg, core, section, own_cross.at[step], mine, cross, sems.at[pl.ds(2, own_cross.shape[1])])
    )


def cands_of(refs, step, width):
    own, cross, rest = refs[0], refs[1], refs[2:]
    if step == 0:
        n = len(rest) // 2
        theirs = [(ref, 0) for ref in rest[n:]]
    else:
        n = 2 if len(rest) == 3 else 3
        theirs = [(rest[n], 0), (rest[n], width)] + [(ref, 0) for ref in rest[n + 1 :]]
    return own, cross, [(ref, 0) for ref in rest[:n]], theirs


def first_kernel(ids, cols, counts, feat_ref, tiles_ref, s0, s1, s2, s3, h_ref, adj_ref, x_ref, sent_ref, small_ref, pick_ref, sem):
    nblk, slots, tile, _ = tiles_ref.shape
    nodes, width = h_ref.shape
    seg = ids[0]
    copy = pltpu.make_async_copy(feat_ref.at[seg], h_ref, sem)
    copy.start()
    for r in range(nblk):
        for j in range(nblk):
            total = jnp.zeros((tile, tile), F32)
            for k in range(slots):
                used = jnp.logical_and(k < counts[r], cols[r, k] == j)
                total = total + jnp.where(used, tiles_ref[r, k].astype(F32), 0.0)
            adj_ref[r * tile : (r + 1) * tile, j * tile : (j + 1) * tile] = total.astype(BF16)
    for r, ref in enumerate((s0, s1, s2, s3)):
        small_ref[seg ^ r] = ref[...]
    sections, steps = small_ref.shape[:2]
    bound = small_ref.shape[2] - 2 * width
    for k in range(sections):
        for p in range(steps):
            rows = small_ref[k, p : p + 1, 2 * width :]
            index = lax.broadcasted_iota(jnp.int32, (nodes, bound), 0).astype(F32)
            pick_ref[k, p] = jnp.where(index == rows, 1.0, 0.0).T.astype(BF16)
    copy.wait()
    x = normed(h_ref[...].astype(F32), small_ref[0, 0:1, width : 2 * width])
    x_ref[...] = x
    sent_ref[...] = dot(pick_ref[0, 0], x).astype(BF16)


def payload_kernel(ids, own, cross, *refs):
    outs, sems = refs[:-1], refs[-1]
    copies = []
    for p, out_ref in enumerate(outs):
        width = out_ref.shape[1]
        tile = cross.shape[-1]
        half = own.at[p, pl.ds(pl.multiple_of(ids[1] * width, width), width), :]
        copies.append(pltpu.make_async_copy(half, out_ref.at[pl.ds(0, width), :], sems.at[p, 0]))
        for b in range(cross.shape[1]):
            dst = out_ref.at[pl.ds(width, tile), pl.ds(b * tile, tile)]
            copies.append(pltpu.make_async_copy(cross.at[p, b], dst, sems.at[p, b + 1]))
    for copy in copies:
        copy.start()
    for copy in copies:
        copy.wait()


def select_kernel(wanted, ids, *refs):
    count = len(wanted)
    outs, sources = refs[-count:], refs
    for out_ref, rule in zip(outs, wanted):
        for i, segments in enumerate(rule):
            here = functools.reduce(jnp.logical_or, [ids[0] == s for s in segments])

            @pl.when(here)
            def _():
                out_ref[...] = sources[i][...]


def stack_kernel(a_ref, b_ref, *refs):
    out_ref = refs[-1]
    rows = out_ref.shape[0] // 2
    out_ref[:rows, :] = a_ref[:rows, :]
    out_ref[rows:, :] = b_ref[:rows, :]


def select(ids, sources, wanted, deps=()):
    shape = jax.ShapeDtypeStruct(sources[0].shape, sources[0].dtype)
    specs = [SM] + [VM] * len(sources) + [ANY] * len(deps)
    return call(functools.partial(select_kernel, wanted), [shape] * len(wanted), specs)(ids, *sources, *deps)


def tie(value, *deps):
    return pl.pallas_call(
        lambda *refs: None,
        name="tie",
        out_shape=jax.ShapeDtypeStruct(value.shape, value.dtype),
        in_specs=[ANY] * (1 + len(deps)),
        out_specs=ANY,
        input_output_aliases={0: 0},
    )(value, *deps)


def load_kernel(section, ids, dep, *refs):
    w_ref, c_ref, sems = refs[-3:]
    width = w_ref.shape[1]
    parts = w_ref.at[pl.ds(0, width), :], w_ref.at[pl.ds(width, width), :]
    for copy in fetch_layer(section, 0, ids, cands_of(refs[:-3], 0, width), *parts, c_ref, sems):
        copy.wait()


def edge_kernel(section, x_ref, h_ref, adj_ref, w_ref, c_ref, small_ref, pick_ref, agg_ref, z_ref, cross_ref, h_out):
    width = x_ref.shape[1]
    pick = pick_ref[section, 1]
    x = x_ref[...]
    adj = dot(pick, adj_ref[...]).astype(BF16)
    agg_ref[...] = dot(adj, x)
    xb = dot(pick, x).astype(BF16)
    z_ref[...] = dot(xb, w_ref[:width, :]) + small_ref[section, 0:1, :width]
    tile = c_ref.shape[0]
    cross = jnp.zeros((pick.shape[0], tile), F32)
    for b in range(c_ref.shape[1] // tile):
        lanes = slice(b * tile, (b + 1) * tile)
        cross = cross + dot(pick[:, lanes], c_ref[:, lanes])
    cross_ref[...] = cross.astype(BF16)
    h_out[...] = dot(pick, h_ref[...]).astype(BF16)


def send_kernel(section, recv_ref, agg_ref, z_ref, cross_ref, h_ref, w_ref, small_ref, sent_ref):
    width = h_ref.shape[1]
    agg = (agg_ref[...] + dot(cross_ref[...], recv_ref[...])).astype(BF16)
    z = z_ref[...] + dot(agg, w_ref[width:, :])
    h = stepped(h_ref[...], z)
    sent_ref[...] = normed(h.astype(F32), small_ref[section, 1:2, width : 2 * width])


def remote(c_ref, recv_ref, i, block):
    tile = c_ref.shape[0]
    parts = []
    for b in range(block // tile):
        lanes = pl.ds(aligned(i * block + b * tile, tile), tile)
        parts.append(dot(c_ref[:, lanes], recv_ref[...]))
    return jnp.concatenate(parts, axis=0)


def even_kernel(section, x_ref, h_ref, adj_ref, recv_ref, w_ref, c_ref, small_ref, dep, h_out, x_out):
    nodes, width = x_ref.shape
    block = 256

    def even(i, carry):
        rows = pl.ds(aligned(i * block, block), block)
        agg = dot(adj_ref[rows, :], x_ref[...]) + remote(c_ref, recv_ref, i, block)
        z = dot(x_ref[rows, :], w_ref[:width, :]) + small_ref[section, 0:1, :width]
        z = z + dot(agg.astype(BF16), w_ref[width:, :])
        h = stepped(h_ref[rows, :], z)
        h_out[rows, :] = h
        x_out[rows, :] = normed(h.astype(F32), small_ref[section, 1:2, width : 2 * width])
        return carry

    lax.fori_loop(0, nodes // block, even, 0)


def odd_kernel(section, ids, x_ref, adj_ref, small_ref, *refs):
    agg_out, z_out, w2_out, c_out, w1_ref, sems = refs[-6:]
    nodes, width = x_ref.shape
    block = 256
    copies = fetch_layer(section, 1, ids, cands_of(refs[:-6], 1, width), w1_ref, w2_out, c_out, sems)
    copies[0].wait()

    def odd(i, carry):
        rows = pl.ds(aligned(i * block, block), block)
        agg_out[rows, :] = dot(adj_ref[rows, :], x_ref[...])
        z_out[rows, :] = dot(x_ref[rows, :], w1_ref[...]) + small_ref[section, 1:2, :width]
        return carry

    lax.fori_loop(0, nodes // block, odd, 0)
    for copy in copies[1:]:
        copy.wait()


def finish_kernel(section, last, deps, ids, recv_ref, agg_ref, z_ref, w2_ref, c_ref, h_ref, small_ref, pick_ref, *refs):
    nodes, width = h_ref.shape
    block = 256
    refs = refs[deps:]
    fetch = len(refs) > 3
    if last:
        (h_out,) = refs
    elif not fetch:
        h_out, x_out, sent_out = refs
    else:
        h_out, x_out, sent_out, w_out, c_out, sems = refs[-6:]
        parts = w_out.at[pl.ds(0, width), :], w_out.at[pl.ds(width, width), :]
        copies = fetch_layer(section + 1, 0, ids, cands_of(refs[:-6], 0, width), *parts, c_out, sems)

    def odd(i, carry):
        rows = pl.ds(aligned(i * block, block), block)
        agg = agg_ref[rows, :] + remote(c_ref, recv_ref, i, block)
        z = z_ref[rows, :] + dot(agg.astype(BF16), w2_ref[...])
        h = stepped(h_ref[rows, :], z)
        h_out[rows, :] = h
        if not last:
            x_out[rows, :] = normed(h.astype(F32), small_ref[section + 1, 0:1, width : 2 * width])
        return carry

    lax.fori_loop(0, nodes // block, odd, 0)
    if not last:
        sent_out[...] = dot(pick_ref[section + 1, 0], x_out[...]).astype(BF16)
    if fetch:
        for copy in copies:
            copy.wait()


def collect_kernel(sections, ids, *refs):
    out_ref, sems = refs[-2:]
    for k in range(sections):

        @pl.when(ids[0] == k)
        def _():
            made = []
            for r in range(sections):
                made.append(pltpu.make_async_copy(refs[k * sections + r], out_ref.at[0, k ^ r], sems.at[r]))
            for copy in made:
                copy.start()
            for copy in made:
                copy.wait()


def shards(features, weights, bias, gain, tile_val, tile_col, tile_count, cross_val, send_rows):
    sections = lax.axis_size("segment")
    doms = lax.axis_size("dom")
    seg = lax.axis_index("segment")
    core = lax.axis_index("dom") & 1
    steps, _, width = weights.shape
    nodes = features.shape[1]
    bound = send_rows.shape[1]
    nbits = doms.bit_length() - 1
    ids = jnp.stack([seg, core]).astype(jnp.int32)

    def moved(value, target, sources=range(sections)):
        pairs = []
        for s in sources:
            for d in range(doms):
                t, e = target(s, d)
                pairs.append((s * doms + d, t * doms + e))
        return lax.ppermute(value, ("segment", "dom"), pairs)

    def sent_to(value, routes):
        return moved(value, lambda s, d: (routes[s], d), list(routes))

    def near(s, d):
        return s ^ (1 + (d & 1)), d

    def far(s, d):
        return s ^ (2 - (d & 1)), d

    def sibling(s, d):
        return s, d ^ 1

    def across(r):
        return lambda s, d: (s ^ r, d)

    def exchange(sent, step):
        bit = step * (nbits - 1) // max(steps - 1, 1)
        return lax.ppermute(sent, "dom", [(i, i ^ 1 << bit) for i in range(doms)])

    mat = jax.ShapeDtypeStruct((nodes, width), BF16)
    mat32 = jax.ShapeDtypeStruct((nodes, width), F32)
    edge = jax.ShapeDtypeStruct((bound, width), BF16)
    edge32 = jax.ShapeDtypeStruct((bound, width), F32)
    half = jax.ShapeDtypeStruct((width, width), BF16)
    both = jax.ShapeDtypeStruct((2 * width, width), BF16)
    load = jax.ShapeDtypeStruct((width + bound, width), BF16)
    picks = jax.ShapeDtypeStruct((sections, steps, bound, nodes), BF16)
    unit = 2 * nodes * width * width
    dmas = pltpu.SemaphoreType.DMA((2 + cross_val.shape[1],))

    own = call(
        payload_kernel,
        [load] * steps,
        [SM, HBM, HBM],
        scratch=[pltpu.SemaphoreType.DMA((steps, 1 + cross_val.shape[1]))],
    )(ids, weights, cross_val)
    small = jnp.concatenate([bias, gain, send_rows.astype(F32)], axis=1)
    smalls = [small] + [moved(small, across(r)) for r in range(1, sections)]
    h, adj, x, sent, small, pick = call(
        first_kernel,
        (mat, jax.ShapeDtypeStruct((nodes, nodes), BF16), mat, edge, jax.ShapeDtypeStruct((sections,) + small.shape, F32), picks),
        [SM, SM, SM, HBM, VM] + [VM] * sections,
        scratch=[pltpu.SemaphoreType.DMA],
    )(ids, tile_col, tile_count, features, tile_val, *smalls)
    recv = exchange(sent, 0)

    inner, outer = (1, 2), (0, 3)
    a0 = moved(own[0], near)
    a1 = moved(own[1], near)
    (pay,) = select(ids, [a0, own[0]], [(inner, outer)], [sent])
    b0 = moved(pay, far)
    sa0 = moved(a0, sibling)
    (pay,) = select(ids, [a1, own[1]], [(inner, outer)], [sa0])
    b1 = moved(pay, far)
    (pay,) = select(ids, [own[0], a0], [(inner, outer)], [pay])
    c0 = moved(pay, far)
    sb0 = moved(b0, sibling)
    brought, swapped = [[a0, b0], []], [[sa0, sb0], []]

    def candidates(p):
        return [weights, cross_val, *brought[p], *swapped[p]]

    def loaded(section, dep):
        cands = candidates(0)
        specs = [SM, ANY, HBM, HBM] + [ANY] * (len(cands) - 2)
        kernel = functools.partial(load_kernel, section)
        return call(kernel, (both, edge), specs, scratch=[dmas])(ids, dep, *cands)

    w, c = loaded(0, pay)

    ends, got = [], [[] for _ in range(sections)]
    for k in range(sections):
        last = k == sections - 1
        if k > 0:
            recv = exchange(sent, 0)
        if k == 1:
            brought[1].append(tie(c1, x))
            swapped[1].append(moved(brought[1][2], sibling))
            w, c = loaded(1, x)
        edges = call(
            functools.partial(edge_kernel, k),
            (edge32, edge32, jax.ShapeDtypeStruct((bound, bound), BF16), edge),
            [VM] * 7,
            flops=LOAD * unit / 4,
        )(x, h, adj, w, c, small, pick)
        sent = call(functools.partial(send_kernel, k), edge, [VM] * 7, flops=LOAD * unit / 4)(recv, *edges[:3], edges[3], w, small)
        recv2 = exchange(sent, 1)
        h, x = call(functools.partial(even_kernel, k), (mat, mat), [VM] * 7 + [ANY], flops=LOAD * unit)(
            x, h, adj, recv, w, c, small, sent
        )
        if k == 0:
            stacked = jax.ShapeDtypeStruct((2 * width, width), BF16)
            stacked = call(stack_kernel, stacked, [VM, VM, ANY])(a1, b1, sent)
            brought[1] = [a1, b1]
            swapped[1] = [moved(stacked, sibling)]
            (third_pay,) = select(ids, [own[1], a1], [(inner, outer)], [sent])
            c1 = moved(third_pay, far)
        cands = candidates(1)
        agg, z, w2, c2 = call(
            functools.partial(odd_kernel, k),
            (mat32, mat32, half, edge),
            [SM] + [VM] * 3 + [HBM, HBM] + [ANY] * (len(cands) - 2),
            scratch=[pltpu.VMEM((width, width), BF16), dmas],
            flops=LOAD * unit,
        )(ids, x, adj, small, *cands)
        if k == 0:
            brought[0].append(tie(c0, recv2))
            swapped[0].append(moved(brought[0][2], sibling))
        deps = got[0] if last else []
        if k == 2:
            rules = [((r,), (1 ^ r,)) for r in range(1, sections)]
            pays = deps = select(ids, ends, rules, [x])
            for r, pay in enumerate(pays, 1):
                v = sent_to(pay, {r: 0, 1 ^ r: 1})
                got[0].append(v)
                got[1].append(v)
        cands = [] if last or k == 0 else candidates(0)
        extra = [HBM, HBM] + [ANY] * (len(cands) - 2) if cands else []
        out = call(
            functools.partial(finish_kernel, k, last, len(deps)),
            (mat,) if last else (mat, mat, edge, both, edge) if cands else (mat, mat, edge),
            [SM] + [VM] * 8 + [ANY] * len(deps) + extra,
            scratch=[dmas] if cands else [],
            flops=LOAD * unit,
        )(ids, recv2, agg, z, w2, c2, h, small, pick, *deps, *cands)
        if last:
            ends.append(out[0])
        else:
            h, x, sent = out[:3]
            ends.append(h)
        if cands:
            w, c = out[3:]
    pays = [select(ids, ends[2:], [((2 ^ r,), (3 ^ r,))])[0] for r in range(1, sections)]
    for r, pay in enumerate(pays, 1):
        v = sent_to(pay, {2 ^ r: 2, 3 ^ r: 3})
        got[2].append(v)
        got[3].append(v)
    pieces = []
    for k in range(sections):
        pieces += [ends[k], *got[k]]
    return call(
        functools.partial(collect_kernel, sections),
        jax.ShapeDtypeStruct((1, sections, nodes, width), BF16),
        [SM] + [ANY] * len(pieces),
        scratch=[pltpu.SemaphoreType.DMA((sections,))],
        out_specs=ANY,
    )(ids, *pieces)


def solution(mesh):
    in_specs = (
        P(None, "dom", None),
        P("segment", None, None),
        P("segment", None),
        P("segment", None),
        P("dom", None, None, None),
        P("dom", None),
        P("dom"),
        P("segment", "dom", None, None),
        P("segment", "dom"),
    )
    out_specs = P("segment", None, "dom", None)
    return jax.shard_map(shards, mesh=mesh, in_specs=in_specs, out_specs=out_specs, check_vma=False)
```

```python
import functools

import jax
import jax.numpy as jnp
from jax import lax
from jax.experimental import pallas as pl
from jax.experimental.pallas import tpu as pltpu
from jax.sharding import PartitionSpec as P

F32 = jnp.float32
BF16 = jnp.bfloat16
VMEM_BYTES = 12 * 2**20
LOAD = 0.5
VM = pl.BlockSpec(memory_space=pltpu.VMEM)
SM = pl.BlockSpec(memory_space=pltpu.SMEM)
ANY = pl.BlockSpec(memory_space=pl.ANY)
HBM = pl.BlockSpec(memory_space=pltpu.HBM)


def call(body, outs, in_specs, scratch=(), out_specs=None, flops=0, vmem=VMEM_BYTES):
    if out_specs is None:
        out_specs = jax.tree.map(lambda _: VM, outs)
    inner = body.func if isinstance(body, functools.partial) else body
    return pl.pallas_call(
        body,
        name=inner.__name__,
        out_shape=outs,
        in_specs=in_specs,
        out_specs=out_specs,
        scratch_shapes=scratch,
        compiler_params=pltpu.CompilerParams(vmem_limit_bytes=vmem),
        cost_estimate=pl.CostEstimate(flops=int(flops), bytes_accessed=0, transcendentals=0),
    )


def dot(a, b):
    return jnp.dot(a, b, preferred_element_type=F32)


def aligned(start, unit):
    return start if isinstance(start, int) else pl.multiple_of(start, unit)


def normed(hf, gain):
    meansq = jnp.mean(hf * hf, axis=-1, keepdims=True)
    return (hf * lax.rsqrt(meansq + 1e-05) * gain).astype(BF16)


def stepped(h, z):
    return (h.astype(F32) + z / (1.0 + jnp.exp(-z))).astype(BF16)


def start_one(choices, dst, sem):
    for condition, source in choices:

        @pl.when(condition)
        def _():
            pltpu.make_async_copy(source, dst, sem).start()

    return pltpu.make_async_copy(choices[0][1], dst, sem)


def source_of(seg, section, half):
    near, far = 1 + half, 2 - half
    via = seg ^ far
    passed = jnp.logical_or(via == 1, via == 2)
    second = jnp.where(passed, seg ^ 3, via)
    return jnp.where(seg == section, 0, jnp.where((seg ^ near) == section, 1, jnp.where(second == section, 2, 3)))


def fetch_half(seg, core, section, half, own, mine, theirs, dst, sem):
    width = dst.shape[1]
    source = source_of(seg, section, half)
    choices = [(source == 0, own.at[pl.ds(half * width, width), :])]
    for here, refs in ((core == half, mine), (core != half, theirs)):
        for i, (ref, row) in enumerate(refs):
            choices.append((jnp.logical_and(here, source == i + 1), ref.at[pl.ds(row, width), :]))
    return [start_one(choices, dst, sem)]


def fetch_cross(seg, core, section, own, mine, dst, sems):
    tile = dst.shape[0]
    width = dst.shape[1]
    blocks = own.shape[0]
    source = jnp.where(core == 0, source_of(seg, section, 0), source_of(seg, section, 1))
    for i, (ref, _) in enumerate(mine):

        @pl.when(source == i + 1)
        def _():
            for b in range(blocks):
                part = ref.at[pl.ds(width, tile), pl.ds(b * tile, tile)]
                pltpu.make_async_copy(part, dst.at[:, pl.ds(b * tile, tile)], sems.at[b]).start()

    @pl.when(source == 0)
    def _():
        for b in range(blocks):
            pltpu.make_async_copy(own.at[b], dst.at[:, pl.ds(b * tile, tile)], sems.at[b]).start()

    return [pltpu.make_async_copy(own.at[b], dst.at[:, pl.ds(b * tile, tile)], sems.at[b]) for b in range(blocks)]


def fetch_layer(section, step, ids, cands, top, bottom, cross, sems):
    own, own_cross, mine, theirs = cands
    seg, core = ids[0], ids[1]
    return (
        fetch_half(seg, core, section, 0, own.at[step], mine, theirs, top, sems.at[0])
        + fetch_half(seg, core, section, 1, own.at[step], mine, theirs, bottom, sems.at[1])
        + fetch_cross(seg, core, section, own_cross.at[step], mine, cross, sems.at[pl.ds(2, own_cross.shape[1])])
    )


def cands_of(refs, step, width):
    own, cross, rest = refs[0], refs[1], refs[2:]
    if step == 0:
        n = len(rest) // 2
        theirs = [(ref, 0) for ref in rest[n:]]
    else:
        n = 2 if len(rest) == 3 else 3
        theirs = [(rest[n], 0), (rest[n], width)] + [(ref, 0) for ref in rest[n + 1 :]]
    return own, cross, [(ref, 0) for ref in rest[:n]], theirs


def first_kernel(ids, cols, counts, feat_ref, tiles_ref, s0, s1, s2, s3, h_ref, adj_ref, x_ref, sent_ref, small_ref, pick_ref, sem):
    nblk, slots, tile, _ = tiles_ref.shape
    nodes, width = h_ref.shape
    seg = ids[0]
    copy = pltpu.make_async_copy(feat_ref.at[seg], h_ref, sem)
    copy.start()
    for r in range(nblk):
        for j in range(nblk):
            total = jnp.zeros((tile, tile), F32)
            for k in range(slots):
                used = jnp.logical_and(k < counts[r], cols[r, k] == j)
                total = total + jnp.where(used, tiles_ref[r, k].astype(F32), 0.0)
            adj_ref[r * tile : (r + 1) * tile, j * tile : (j + 1) * tile] = total.astype(BF16)
    for r, ref in enumerate((s0, s1, s2, s3)):
        small_ref[seg ^ r] = ref[...]
    sections, steps = small_ref.shape[:2]
    bound = small_ref.shape[2] - 2 * width
    for k in range(sections):
        for p in range(steps):
            rows = small_ref[k, p : p + 1, 2 * width :]
            index = lax.broadcasted_iota(jnp.int32, (nodes, bound), 0).astype(F32)
            pick_ref[k, p] = jnp.where(index == rows, 1.0, 0.0).T.astype(BF16)
    copy.wait()
    x = normed(h_ref[...].astype(F32), small_ref[0, 0:1, width : 2 * width])
    x_ref[...] = x
    sent_ref[...] = dot(pick_ref[0, 0], x).astype(BF16)


def payload_kernel(ids, own, cross, *refs):
    outs, sems = refs[:-1], refs[-1]
    copies = []
    for p, out_ref in enumerate(outs):
        width = out_ref.shape[1]
        tile = cross.shape[-1]
        half = own.at[p, pl.ds(pl.multiple_of(ids[1] * width, width), width), :]
        copies.append(pltpu.make_async_copy(half, out_ref.at[pl.ds(0, width), :], sems.at[p, 0]))
        for b in range(cross.shape[1]):
            dst = out_ref.at[pl.ds(width, tile), pl.ds(b * tile, tile)]
            copies.append(pltpu.make_async_copy(cross.at[p, b], dst, sems.at[p, b + 1]))
    for copy in copies:
        copy.start()
    for copy in copies:
        copy.wait()


def select_kernel(wanted, ids, *refs):
    count = len(wanted)
    outs, sources = refs[-count:], refs
    for out_ref, rule in zip(outs, wanted):
        for i, segments in enumerate(rule):
            here = functools.reduce(jnp.logical_or, [ids[0] == s for s in segments])

            @pl.when(here)
            def _():
                out_ref[...] = sources[i][...]


def stack_kernel(a_ref, b_ref, *refs):
    out_ref = refs[-1]
    rows = out_ref.shape[0] // 2
    out_ref[:rows, :] = a_ref[:rows, :]
    out_ref[rows:, :] = b_ref[:rows, :]


def select(ids, sources, wanted, deps=()):
    shape = jax.ShapeDtypeStruct(sources[0].shape, sources[0].dtype)
    specs = [SM] + [VM] * len(sources) + [ANY] * len(deps)
    return call(functools.partial(select_kernel, wanted), [shape] * len(wanted), specs, vmem=8 * 2**20)(ids, *sources, *deps)


def tie(value, *deps):
    return pl.pallas_call(
        lambda *refs: None,
        name="tie",
        out_shape=jax.ShapeDtypeStruct(value.shape, value.dtype),
        in_specs=[ANY] * (1 + len(deps)),
        out_specs=ANY,
        input_output_aliases={0: 0},
        compiler_params=pltpu.CompilerParams(vmem_limit_bytes=2**20),
    )(value, *deps)


def load_kernel(section, ids, dep, *refs):
    w_ref, c_ref, sems = refs[-3:]
    width = w_ref.shape[1]
    parts = w_ref.at[pl.ds(0, width), :], w_ref.at[pl.ds(width, width), :]
    for copy in fetch_layer(section, 0, ids, cands_of(refs[:-3], 0, width), *parts, c_ref, sems):
        copy.wait()


def edge_kernel(section, x_ref, h_ref, adj_ref, w_ref, c_ref, small_ref, pick_ref, agg_ref, z_ref, cross_ref, h_out):
    width = x_ref.shape[1]
    pick = pick_ref[section, 1]
    x = x_ref[...]
    adj = dot(pick, adj_ref[...]).astype(BF16)
    agg_ref[...] = dot(adj, x)
    xb = dot(pick, x).astype(BF16)
    z_ref[...] = dot(xb, w_ref[:width, :]) + small_ref[section, 0:1, :width]
    tile = c_ref.shape[0]
    cross = jnp.zeros((pick.shape[0], tile), F32)
    for b in range(c_ref.shape[1] // tile):
        lanes = slice(b * tile, (b + 1) * tile)
        cross = cross + dot(pick[:, lanes], c_ref[:, lanes])
    cross_ref[...] = cross.astype(BF16)
    h_out[...] = dot(pick, h_ref[...]).astype(BF16)


def send_kernel(section, recv_ref, agg_ref, z_ref, cross_ref, h_ref, w_ref, small_ref, sent_ref):
    width = h_ref.shape[1]
    agg = (agg_ref[...] + dot(cross_ref[...], recv_ref[...])).astype(BF16)
    z = z_ref[...] + dot(agg, w_ref[width:, :])
    h = stepped(h_ref[...], z)
    sent_ref[...] = normed(h.astype(F32), small_ref[section, 1:2, width : 2 * width])


def remote(c_ref, recv_ref, i, block):
    tile = c_ref.shape[0]
    parts = []
    for b in range(block // tile):
        lanes = pl.ds(aligned(i * block + b * tile, tile), tile)
        parts.append(dot(c_ref[:, lanes], recv_ref[...]))
    return jnp.concatenate(parts, axis=0)


def even_kernel(section, x_ref, h_ref, adj_ref, recv_ref, w_ref, c_ref, small_ref, dep, h_out, x_out):
    nodes, width = x_ref.shape
    block = 256

    def even(i, carry):
        rows = pl.ds(aligned(i * block, block), block)
        agg = dot(adj_ref[rows, :], x_ref[...]) + remote(c_ref, recv_ref, i, block)
        z = dot(x_ref[rows, :], w_ref[:width, :]) + small_ref[section, 0:1, :width]
        z = z + dot(agg.astype(BF16), w_ref[width:, :])
        h = stepped(h_ref[rows, :], z)
        h_out[rows, :] = h
        x_out[rows, :] = normed(h.astype(F32), small_ref[section, 1:2, width : 2 * width])
        return carry

    lax.fori_loop(0, nodes // block, even, 0)


def odd_kernel(section, ids, x_ref, adj_ref, small_ref, *refs):
    agg_out, z_out, w2_out, c_out, w1_ref, sems = refs[-6:]
    nodes, width = x_ref.shape
    block = 256
    copies = fetch_layer(section, 1, ids, cands_of(refs[:-6], 1, width), w1_ref, w2_out, c_out, sems)
    copies[0].wait()

    def odd(i, carry):
        rows = pl.ds(aligned(i * block, block), block)
        agg_out[rows, :] = dot(adj_ref[rows, :], x_ref[...])
        z_out[rows, :] = dot(x_ref[rows, :], w1_ref[...]) + small_ref[section, 1:2, :width]
        return carry

    lax.fori_loop(0, nodes // block, odd, 0)
    for copy in copies[1:]:
        copy.wait()


def finish_kernel(section, last, ids, recv_ref, agg_ref, z_ref, w2_ref, c_ref, h_ref, small_ref, pick_ref, *refs):
    nodes, width = h_ref.shape
    block = 256
    fetch = len(refs) > 5
    if last:
        before_ref, h_out, *pays = refs
    elif not fetch:
        h_out, x_out, sent_out = refs
    else:
        h_out, x_out, sent_out, w_out, c_out, sems = refs[-6:]
        parts = w_out.at[pl.ds(0, width), :], w_out.at[pl.ds(width, width), :]
        copies = fetch_layer(section + 1, 0, ids, cands_of(refs[:-6], 0, width), *parts, c_out, sems)

    def odd(i, carry):
        rows = pl.ds(aligned(i * block, block), block)
        agg = agg_ref[rows, :] + remote(c_ref, recv_ref, i, block)
        z = z_ref[rows, :] + dot(agg.astype(BF16), w2_ref[...])
        h = stepped(h_ref[rows, :], z)
        h_out[rows, :] = h
        if last:
            for r, pay_ref in enumerate(pays, 1):
                pay_ref[rows, :] = jnp.where(ids[0] == section ^ r, h, before_ref[rows, :])
        else:
            x_out[rows, :] = normed(h.astype(F32), small_ref[section + 1, 0:1, width : 2 * width])
        return carry

    lax.fori_loop(0, nodes // block, odd, 0)
    if not last:
        sent_out[...] = dot(pick_ref[section + 1, 0], x_out[...]).astype(BF16)
    if fetch:
        for copy in copies:
            copy.wait()


def collect_kernel(sections, ids, *refs):
    out_ref, sems = refs[-2:]
    for k in range(sections):

        @pl.when(ids[0] == k)
        def _():
            made = []
            for r in range(sections):
                made.append(pltpu.make_async_copy(refs[k * sections + r], out_ref.at[0, k ^ r], sems.at[r]))
            for copy in made:
                copy.start()
            for copy in made:
                copy.wait()


def shards(features, weights, bias, gain, tile_val, tile_col, tile_count, cross_val, send_rows):
    sections = lax.axis_size("segment")
    doms = lax.axis_size("dom")
    seg = lax.axis_index("segment")
    core = lax.axis_index("dom") & 1
    steps, _, width = weights.shape
    nodes = features.shape[1]
    bound = send_rows.shape[1]
    nbits = doms.bit_length() - 1
    ids = jnp.stack([seg, core]).astype(jnp.int32)

    def moved(value, target, sources=range(sections)):
        pairs = []
        for s in sources:
            for d in range(doms):
                t, e = target(s, d)
                pairs.append((s * doms + d, t * doms + e))
        return lax.ppermute(value, ("segment", "dom"), pairs)

    def sent_to(value, routes):
        return moved(value, lambda s, d: (routes[s], d), list(routes))

    def near(s, d):
        return s ^ (1 + (d & 1)), d

    def far(s, d):
        return s ^ (2 - (d & 1)), d

    def sibling(s, d):
        return s, d ^ 1

    def across(r):
        return lambda s, d: (s ^ r, d)

    def exchange(sent, step):
        bit = step * (nbits - 1) // max(steps - 1, 1)
        return lax.ppermute(sent, "dom", [(i, i ^ 1 << bit) for i in range(doms)])

    mat = jax.ShapeDtypeStruct((nodes, width), BF16)
    mat32 = jax.ShapeDtypeStruct((nodes, width), F32)
    edge = jax.ShapeDtypeStruct((bound, width), BF16)
    edge32 = jax.ShapeDtypeStruct((bound, width), F32)
    half = jax.ShapeDtypeStruct((width, width), BF16)
    both = jax.ShapeDtypeStruct((2 * width, width), BF16)
    load = jax.ShapeDtypeStruct((width + bound, width), BF16)
    picks = jax.ShapeDtypeStruct((sections, steps, bound, nodes), BF16)
    unit = 2 * nodes * width * width
    dmas = pltpu.SemaphoreType.DMA((2 + cross_val.shape[1],))

    own = call(
        payload_kernel,
        [load] * steps,
        [SM, HBM, HBM],
        scratch=[pltpu.SemaphoreType.DMA((steps, 1 + cross_val.shape[1]))],
        vmem=48 * 2**20,
    )(ids, weights, cross_val)
    small = jnp.concatenate([bias, gain, send_rows.astype(F32)], axis=1)
    smalls = [small] + [moved(small, across(r)) for r in range(1, sections)]
    h, adj, x, sent, small, pick = call(
        first_kernel,
        (mat, jax.ShapeDtypeStruct((nodes, nodes), BF16), mat, edge, jax.ShapeDtypeStruct((sections,) + small.shape, F32), picks),
        [SM, SM, SM, HBM, VM] + [VM] * sections,
        scratch=[pltpu.SemaphoreType.DMA],
    )(ids, tile_col, tile_count, features, tile_val, *smalls)
    recv = exchange(sent, 0)

    inner, outer = (1, 2), (0, 3)
    a0 = moved(own[0], near)
    a1 = moved(own[1], near)
    (pay,) = select(ids, [a0, own[0]], [(inner, outer)])
    b0 = moved(pay, far)
    sa0 = moved(a0, sibling)
    (pay,) = select(ids, [a1, own[1]], [(inner, outer)], [sa0, sent])
    b1 = moved(pay, far)
    (pay,) = select(ids, [own[0], a0], [(inner, outer)], [pay])
    c0 = moved(pay, far)
    sb0 = moved(b0, sibling)
    brought, swapped = [[a0, b0], []], [[sa0, sb0], []]

    def candidates(p):
        return [weights, cross_val, *brought[p], *swapped[p]]

    def loaded(section, dep):
        cands = candidates(0)
        specs = [SM, ANY, HBM, HBM] + [ANY] * (len(cands) - 2)
        kernel = functools.partial(load_kernel, section)
        return call(kernel, (both, edge), specs, scratch=[dmas])(ids, dep, *cands)

    w, c = loaded(0, pay)

    ends, got = [], [[] for _ in range(sections)]
    for k in range(sections):
        last = k == sections - 1
        if k > 0:
            recv = exchange(sent, 0)
        if k == 1:
            brought[0].append(tie(c0, x))
            swapped[0].append(moved(brought[0][2], sibling))
            brought[1].append(tie(c1, x))
            swapped[1].append(moved(brought[1][2], sibling))
            w, c = loaded(1, x)
        edges = call(
            functools.partial(edge_kernel, k),
            (edge32, edge32, jax.ShapeDtypeStruct((bound, bound), BF16), edge),
            [VM] * 7,
            flops=LOAD * unit / 4,
        )(x, h, adj, w, c, small, pick)
        sent = call(functools.partial(send_kernel, k), edge, [VM] * 7, flops=LOAD * unit / 4)(recv, *edges[:3], edges[3], w, small)
        recv2 = exchange(sent, 1)
        h, x = call(functools.partial(even_kernel, k), (mat, mat), [VM] * 7 + [ANY], flops=(20 if k == 0 else LOAD) * unit)(
            x, h, adj, recv, w, c, small, sent
        )
        if k == 0:
            stacked = jax.ShapeDtypeStruct((2 * width, width), BF16)
            stacked = call(stack_kernel, stacked, [VM, VM, ANY])(a1, b1, sent)
            brought[1] = [a1, b1]
            swapped[1] = [moved(stacked, sibling)]
            (third_pay,) = select(ids, [own[1], a1], [(inner, outer)], [sent])
            c1 = moved(third_pay, far)
        cands = candidates(1)
        agg, z, w2, c2 = call(
            functools.partial(odd_kernel, k),
            (mat32, mat32, half, edge),
            [SM] + [VM] * 3 + [HBM, HBM] + [ANY] * (len(cands) - 2),
            scratch=[pltpu.VMEM((width, width), BF16), dmas],
            flops=(20 if k == 2 else LOAD) * unit,
        )(ids, x, adj, small, *cands)
        if k == 2:
            rules = [((r,), (1 ^ r,)) for r in range(1, sections)]
            pays = select(ids, ends, rules, [x])
            for r, pay in enumerate(pays, 1):
                v = sent_to(pay, {r: 0, 1 ^ r: 1})
                got[0].append(v)
                got[1].append(v)
        cands = [] if last or k == 0 else candidates(0)
        if last:
            outs, more, specs = (mat,) * sections, [ends[-1]], [VM]
        elif cands:
            outs, more, specs = (mat, mat, edge, both, edge), cands, [HBM, HBM] + [ANY] * (len(cands) - 2)
        else:
            outs, more, specs = (mat, mat, edge), [], []
        out = call(
            functools.partial(finish_kernel, k, last),
            outs,
            [SM] + [VM] * 8 + specs,
            scratch=[dmas] if cands else [],
            flops=LOAD * unit,
        )(ids, recv2, agg, z, w2, c2, h, small, pick, *more)
        ends.append(out[0])
        if not last:
            h, x, sent = out[:3]
        if cands:
            w, c = out[3:]
    for r, pay in enumerate(out[1:], 1):
        v = sent_to(pay, {2 ^ r: 2, 3 ^ r: 3})
        got[2].append(v)
        got[3].append(v)
    pieces = []
    for k in range(sections):
        pieces += [ends[k], *got[k]]
    return call(
        functools.partial(collect_kernel, sections),
        jax.ShapeDtypeStruct((1, sections, nodes, width), BF16),
        [SM] + [ANY] * len(pieces),
        scratch=[pltpu.SemaphoreType.DMA((sections,))],
        out_specs=ANY,
    )(ids, *pieces)


def solution(mesh):
    in_specs = (
        P(None, "dom", None),
        P("segment", None, None),
        P("segment", None),
        P("segment", None),
        P("dom", None, None, None),
        P("dom", None),
        P("dom"),
        P("segment", "dom", None, None),
        P("segment", "dom"),
    )
    out_specs = P("segment", None, "dom", None)
    return jax.shard_map(shards, mesh=mesh, in_specs=in_specs, out_specs=out_specs, check_vma=False)
```

```python
import functools

import jax
import jax.numpy as jnp
from jax import lax
from jax.experimental import pallas as pl
from jax.experimental.pallas import tpu as pltpu
from jax.sharding import PartitionSpec as P

F32 = jnp.float32
BF16 = jnp.bfloat16
VMEM_BYTES = 12 * 2**20
LOAD = 0.5
VM = pl.BlockSpec(memory_space=pltpu.VMEM)
SM = pl.BlockSpec(memory_space=pltpu.SMEM)
ANY = pl.BlockSpec(memory_space=pl.ANY)
HBM = pl.BlockSpec(memory_space=pltpu.HBM)


def call(body, outs, in_specs, scratch=(), out_specs=None, flops=0, vmem=VMEM_BYTES):
    if out_specs is None:
        out_specs = jax.tree.map(lambda _: VM, outs)
    inner = body.func if isinstance(body, functools.partial) else body
    return pl.pallas_call(
        body,
        name=inner.__name__,
        out_shape=outs,
        in_specs=in_specs,
        out_specs=out_specs,
        scratch_shapes=scratch,
        compiler_params=pltpu.CompilerParams(vmem_limit_bytes=vmem),
        cost_estimate=pl.CostEstimate(flops=int(flops), bytes_accessed=0, transcendentals=0),
    )


def dot(a, b):
    return jnp.dot(a, b, preferred_element_type=F32)


def aligned(start, unit):
    return start if isinstance(start, int) else pl.multiple_of(start, unit)


def normed(hf, gain):
    meansq = jnp.mean(hf * hf, axis=-1, keepdims=True)
    return (hf * lax.rsqrt(meansq + 1e-05) * gain).astype(BF16)


def stepped(h, z):
    return (h.astype(F32) + z / (1.0 + jnp.exp(-z))).astype(BF16)


def start_one(choices, dst, sem):
    for condition, source in choices:

        @pl.when(condition)
        def _():
            pltpu.make_async_copy(source, dst, sem).start()

    return pltpu.make_async_copy(choices[0][1], dst, sem)


def source_of(seg, section, half):
    near, far = 1 + half, 2 - half
    via = seg ^ far
    passed = jnp.logical_or(via == 1, via == 2)
    second = jnp.where(passed, seg ^ 3, via)
    return jnp.where(seg == section, 0, jnp.where((seg ^ near) == section, 1, jnp.where(second == section, 2, 3)))


def fetch_half(seg, core, section, half, own, mine, theirs, dst, sem):
    width = dst.shape[1]
    source = source_of(seg, section, half)
    choices = [(source == 0, own.at[pl.ds(half * width, width), :])]
    for here, refs in ((core == half, mine), (core != half, theirs)):
        for i, (ref, row) in enumerate(refs):
            choices.append((jnp.logical_and(here, source == i + 1), ref.at[pl.ds(row, width), :]))
    return [start_one(choices, dst, sem)]


def fetch_cross(seg, core, section, own, mine, dst, sems):
    tile = dst.shape[0]
    width = dst.shape[1]
    blocks = own.shape[0]
    source = jnp.where(core == 0, source_of(seg, section, 0), source_of(seg, section, 1))
    for i, (ref, _) in enumerate(mine):

        @pl.when(source == i + 1)
        def _():
            for b in range(blocks):
                part = ref.at[pl.ds(width, tile), pl.ds(b * tile, tile)]
                pltpu.make_async_copy(part, dst.at[:, pl.ds(b * tile, tile)], sems.at[b]).start()

    @pl.when(source == 0)
    def _():
        for b in range(blocks):
            pltpu.make_async_copy(own.at[b], dst.at[:, pl.ds(b * tile, tile)], sems.at[b]).start()

    return [pltpu.make_async_copy(own.at[b], dst.at[:, pl.ds(b * tile, tile)], sems.at[b]) for b in range(blocks)]


def fetch_layer(section, step, ids, cands, top, bottom, cross, sems):
    own, own_cross, mine, theirs = cands
    seg, core = ids[0], ids[1]
    return (
        fetch_half(seg, core, section, 0, own.at[step], mine, theirs, top, sems.at[0])
        + fetch_half(seg, core, section, 1, own.at[step], mine, theirs, bottom, sems.at[1])
        + fetch_cross(seg, core, section, own_cross.at[step], mine, cross, sems.at[pl.ds(2, own_cross.shape[1])])
    )


def cands_of(refs, step, width):
    own, cross, rest = refs[0], refs[1], refs[2:]
    n = len(rest) // 2
    theirs = [(rest[n], step * width)] + [(ref, 0) for ref in rest[n + 1 :]]
    return own, cross, [(ref, 0) for ref in rest[:n]], theirs


def first_kernel(ids, cols, counts, feat_ref, tiles_ref, s0, s1, s2, s3, h_ref, adj_ref, x_ref, sent_ref, small_ref, pick_ref, sem):
    nblk, slots, tile, _ = tiles_ref.shape
    nodes, width = h_ref.shape
    seg = ids[0]
    copy = pltpu.make_async_copy(feat_ref.at[seg], h_ref, sem)
    copy.start()
    for r in range(nblk):
        for j in range(nblk):
            total = jnp.zeros((tile, tile), F32)
            for k in range(slots):
                used = jnp.logical_and(k < counts[r], cols[r, k] == j)
                total = total + jnp.where(used, tiles_ref[r, k].astype(F32), 0.0)
            adj_ref[r * tile : (r + 1) * tile, j * tile : (j + 1) * tile] = total.astype(BF16)
    for r, ref in enumerate((s0, s1, s2, s3)):
        small_ref[seg ^ r] = ref[...]
    sections, steps = small_ref.shape[:2]
    bound = small_ref.shape[2] - 2 * width
    for k in range(sections):
        for p in range(steps):
            rows = small_ref[k, p : p + 1, 2 * width :]
            index = lax.broadcasted_iota(jnp.int32, (nodes, bound), 0).astype(F32)
            pick_ref[k, p] = jnp.where(index == rows, 1.0, 0.0).T.astype(BF16)
    copy.wait()
    x = normed(h_ref[...].astype(F32), small_ref[0, 0:1, width : 2 * width])
    x_ref[...] = x
    sent_ref[...] = dot(pick_ref[0, 0], x).astype(BF16)


def payload_kernel(steps, ids, own, cross, *refs):
    outs, sems = refs[-steps - 1 : -1], refs[-1]
    copies = []
    for p, out_ref in enumerate(outs):
        width = out_ref.shape[1]
        tile = cross.shape[-1]
        half = own.at[p, pl.ds(pl.multiple_of(ids[1] * width, width), width), :]
        copies.append(pltpu.make_async_copy(half, out_ref.at[pl.ds(0, width), :], sems.at[p, 0]))
        for b in range(cross.shape[1]):
            dst = out_ref.at[pl.ds(width, tile), pl.ds(b * tile, tile)]
            copies.append(pltpu.make_async_copy(cross.at[p, b], dst, sems.at[p, b + 1]))
    for copy in copies:
        copy.start()
    for copy in copies:
        copy.wait()


def select_kernel(wanted, ids, *refs):
    count = len(wanted)
    outs, sources = refs[-count:], refs
    for out_ref, rule in zip(outs, wanted):
        for i, segments in enumerate(rule):
            here = functools.reduce(jnp.logical_or, [ids[0] == s for s in segments])

            @pl.when(here)
            def _():
                out_ref[...] = sources[i][...]


def stack_kernel(a_ref, b_ref, out_ref):
    rows = out_ref.shape[0] // 2
    out_ref[:rows, :] = a_ref[:rows, :]
    out_ref[rows:, :] = b_ref[:rows, :]


def select(ids, sources, wanted, deps=()):
    shape = jax.ShapeDtypeStruct(sources[0].shape, sources[0].dtype)
    specs = [SM] + [VM] * len(sources) + [ANY] * len(deps)
    return call(functools.partial(select_kernel, wanted), [shape] * len(wanted), specs, vmem=8 * 2**20)(ids, *sources, *deps)


def tie(value, *deps):
    return pl.pallas_call(
        lambda *refs: None,
        name="tie",
        out_shape=jax.ShapeDtypeStruct(value.shape, value.dtype),
        in_specs=[ANY] * (1 + len(deps)),
        out_specs=ANY,
        input_output_aliases={0: 0},
        compiler_params=pltpu.CompilerParams(vmem_limit_bytes=2**20),
    )(value, *deps)


def load_kernel(section, ids, dep, *refs):
    w_ref, c_ref, sems = refs[-3:]
    width = w_ref.shape[1]
    parts = w_ref.at[pl.ds(0, width), :], w_ref.at[pl.ds(width, width), :]
    for copy in fetch_layer(section, 0, ids, cands_of(refs[:-3], 0, width), *parts, c_ref, sems):
        copy.wait()


def edge_kernel(section, x_ref, h_ref, adj_ref, w_ref, c_ref, small_ref, pick_ref, agg_ref, z_ref, cross_ref, h_out):
    width = x_ref.shape[1]
    pick = pick_ref[section, 1]
    x = x_ref[...]
    adj = dot(pick, adj_ref[...]).astype(BF16)
    agg_ref[...] = dot(adj, x)
    xb = dot(pick, x).astype(BF16)
    z_ref[...] = dot(xb, w_ref[:width, :]) + small_ref[section, 0:1, :width]
    tile = c_ref.shape[0]
    cross = jnp.zeros((pick.shape[0], tile), F32)
    for b in range(c_ref.shape[1] // tile):
        lanes = slice(b * tile, (b + 1) * tile)
        cross = cross + dot(pick[:, lanes], c_ref[:, lanes])
    cross_ref[...] = cross.astype(BF16)
    h_out[...] = dot(pick, h_ref[...]).astype(BF16)


def send_kernel(section, recv_ref, agg_ref, z_ref, cross_ref, h_ref, w_ref, small_ref, sent_ref):
    width = h_ref.shape[1]
    agg = (agg_ref[...] + dot(cross_ref[...], recv_ref[...])).astype(BF16)
    z = z_ref[...] + dot(agg, w_ref[width:, :])
    h = stepped(h_ref[...], z)
    sent_ref[...] = normed(h.astype(F32), small_ref[section, 1:2, width : 2 * width])


def remote(c_ref, recv_ref, i, block):
    tile = c_ref.shape[0]
    parts = []
    for b in range(block // tile):
        lanes = pl.ds(aligned(i * block + b * tile, tile), tile)
        parts.append(dot(c_ref[:, lanes], recv_ref[...]))
    return jnp.concatenate(parts, axis=0)


def even_kernel(section, x_ref, h_ref, adj_ref, recv_ref, w_ref, c_ref, small_ref, dep, h_out, x_out):
    nodes, width = x_ref.shape
    block = 256

    def even(i, carry):
        rows = pl.ds(aligned(i * block, block), block)
        agg = dot(adj_ref[rows, :], x_ref[...]) + remote(c_ref, recv_ref, i, block)
        z = dot(x_ref[rows, :], w_ref[:width, :]) + small_ref[section, 0:1, :width]
        z = z + dot(agg.astype(BF16), w_ref[width:, :])
        h = stepped(h_ref[rows, :], z)
        h_out[rows, :] = h
        x_out[rows, :] = normed(h.astype(F32), small_ref[section, 1:2, width : 2 * width])
        return carry

    lax.fori_loop(0, nodes // block, even, 0)


def odd_kernel(section, ids, x_ref, adj_ref, small_ref, *refs):
    agg_out, z_out, w2_out, c_out, w1_ref, sems = refs[-6:]
    nodes, width = x_ref.shape
    block = 256
    copies = fetch_layer(section, 1, ids, cands_of(refs[:-6], 1, width), w1_ref, w2_out, c_out, sems)
    copies[0].wait()

    def odd(i, carry):
        rows = pl.ds(aligned(i * block, block), block)
        agg_out[rows, :] = dot(adj_ref[rows, :], x_ref[...])
        z_out[rows, :] = dot(x_ref[rows, :], w1_ref[...]) + small_ref[section, 1:2, :width]
        return carry

    lax.fori_loop(0, nodes // block, odd, 0)
    for copy in copies[1:]:
        copy.wait()


def finish_kernel(section, last, ids, recv_ref, agg_ref, z_ref, w2_ref, c_ref, h_ref, small_ref, pick_ref, *refs):
    nodes, width = h_ref.shape
    block = 256
    fetch = not last and len(refs) > 5
    if last:
        ends, (h_out, *pays) = refs[:section], refs[section:]
    elif not fetch:
        h_out, x_out, sent_out = refs
    else:
        h_out, x_out, sent_out, w_out, c_out, sems = refs[-6:]
        parts = w_out.at[pl.ds(0, width), :], w_out.at[pl.ds(width, width), :]
        copies = fetch_layer(section + 1, 0, ids, cands_of(refs[:-6], 0, width), *parts, c_out, sems)

    def odd(i, carry):
        rows = pl.ds(aligned(i * block, block), block)
        agg = agg_ref[rows, :] + remote(c_ref, recv_ref, i, block)
        z = z_ref[rows, :] + dot(agg.astype(BF16), w2_ref[...])
        h = stepped(h_ref[rows, :], z)
        h_out[rows, :] = h
        if last:
            for r, pay_ref in enumerate(pays, 1):

                @pl.when(ids[0] == section ^ r)
                def _():
                    pay_ref[rows, :] = h
        else:
            x_out[rows, :] = normed(h.astype(F32), small_ref[section + 1, 0:1, width : 2 * width])
        return carry

    if last:
        for k, end_ref in enumerate(ends):
            for r, pay_ref in enumerate(pays, 1):

                @pl.when(ids[0] == k ^ r)
                def _():
                    pay_ref[...] = end_ref[...]

    lax.fori_loop(0, nodes // block, odd, 0)
    if not last:
        sent_out[...] = dot(pick_ref[section + 1, 0], x_out[...]).astype(BF16)
    if fetch:
        for copy in copies:
            copy.wait()


def collect_kernel(ids, *refs):
    out_ref, sems = refs[-2:]
    sections = out_ref.shape[1]
    ends, got = refs[:sections], refs[sections:-2]
    copies = [start_one([(ids[0] == k, end) for k, end in enumerate(ends)], out_ref.at[0, ids[0]], sems.at[0])]
    for r, ref in enumerate(got, 1):
        copies.append(pltpu.make_async_copy(ref, out_ref.at[0, ids[0] ^ r], sems.at[r]))
        copies[-1].start()
    for copy in copies:
        copy.wait()


def shards(features, weights, bias, gain, tile_val, tile_col, tile_count, cross_val, send_rows):
    sections = lax.axis_size("segment")
    doms = lax.axis_size("dom")
    seg = lax.axis_index("segment")
    core = lax.axis_index("dom") & 1
    steps, _, width = weights.shape
    nodes = features.shape[1]
    bound = send_rows.shape[1]
    nbits = doms.bit_length() - 1
    ids = jnp.stack([seg, core]).astype(jnp.int32)

    def moved(value, target, sources=range(sections)):
        pairs = []
        for s in sources:
            for d in range(doms):
                t, e = target(s, d)
                pairs.append((s * doms + d, t * doms + e))
        return lax.ppermute(value, ("segment", "dom"), pairs)

    def near(s, d):
        return s ^ (1 + (d & 1)), d

    def far(s, d):
        return s ^ (2 - (d & 1)), d

    def sibling(s, d):
        return s, d ^ 1

    def across(r):
        return lambda s, d: (s ^ r, d)

    def exchange(sent, step):
        bit = step * (nbits - 1) // max(steps - 1, 1)
        return lax.ppermute(sent, "dom", [(i, i ^ 1 << bit) for i in range(doms)])

    mat = jax.ShapeDtypeStruct((nodes, width), BF16)
    mat32 = jax.ShapeDtypeStruct((nodes, width), F32)
    edge = jax.ShapeDtypeStruct((bound, width), BF16)
    edge32 = jax.ShapeDtypeStruct((bound, width), F32)
    half = jax.ShapeDtypeStruct((width, width), BF16)
    both = jax.ShapeDtypeStruct((2 * width, width), BF16)
    load = jax.ShapeDtypeStruct((width + bound, width), BF16)
    picks = jax.ShapeDtypeStruct((sections, steps, bound, nodes), BF16)
    unit = 2 * nodes * width * width
    dmas = pltpu.SemaphoreType.DMA((2 + cross_val.shape[1],))

    small = jnp.concatenate([bias, gain, send_rows.astype(F32)], axis=1)
    smalls = [small] + [moved(small, across(r)) for r in range(1, sections)]
    own = call(
        functools.partial(payload_kernel, steps),
        [load] * steps,
        [SM, HBM, HBM] + [ANY] * (sections - 1),
        scratch=[pltpu.SemaphoreType.DMA((steps, 1 + cross_val.shape[1]))],
        vmem=60 * 2**20,
    )(ids, weights, cross_val, *smalls[1:])
    h, adj, x, sent, small, pick = call(
        first_kernel,
        (mat, jax.ShapeDtypeStruct((nodes, nodes), BF16), mat, edge, jax.ShapeDtypeStruct((sections,) + small.shape, F32), picks),
        [SM, SM, SM, HBM, VM] + [VM] * sections,
        scratch=[pltpu.SemaphoreType.DMA],
    )(ids, tile_col, tile_count, features, tile_val, *smalls)
    recv = exchange(sent, 0)

    inner, outer = (1, 2), (0, 3)
    a0, a1 = [moved(v, near) for v in own]
    (pay,) = select(ids, [a0, own[0]], [(inner, outer)], [a1, sent])
    b0 = moved(pay, far)
    (pay,) = select(ids, [a1, own[1]], [(inner, outer)], [pay])
    b1 = moved(pay, far)
    (pay,) = select(ids, [own[0], a0], [(inner, outer)], [pay])
    c0 = moved(pay, far)
    (pay,) = select(ids, [own[1], a1], [(inner, outer)], [pay])
    c1 = moved(pay, far)
    stacked = call(stack_kernel, both, [VM, VM])(a0, a1)
    sa = moved(stacked, sibling)
    b0 = tie(b0, sa)
    sb0 = moved(b0, sibling)
    brought, swapped = [[a0, b0], [a1]], [[sa, sb0], [sa]]

    def candidates(p):
        return [weights, cross_val, *brought[p], *swapped[p]]

    def loaded(section, dep):
        cands = candidates(0)
        specs = [SM, ANY, HBM, HBM] + [ANY] * (len(cands) - 2)
        kernel = functools.partial(load_kernel, section)
        return call(kernel, (both, edge), specs, scratch=[dmas])(ids, dep, *cands)

    w, c = loaded(0, b1)

    ends = []
    for k in range(sections):
        last = k == sections - 1
        if k > 0:
            recv = exchange(sent, 0)
        if k == 1:
            w, c = loaded(1, x)
        edges = call(
            functools.partial(edge_kernel, k),
            (edge32, edge32, jax.ShapeDtypeStruct((bound, bound), BF16), edge),
            [VM] * 7,
            flops=LOAD * unit / 4,
        )(x, h, adj, w, c, small, pick)
        sent = call(functools.partial(send_kernel, k), edge, [VM] * 7, flops=LOAD * unit / 4)(recv, *edges[:3], edges[3], w, small)
        recv2 = exchange(sent, 1)
        if k == 1:
            brought[1].append(tie(c1, sent))
            swapped[1].append(moved(brought[1][2], sibling))
        h, x = call(functools.partial(even_kernel, k), (mat, mat), [VM] * 7 + [ANY], flops=LOAD * unit)(
            x, h, adj, recv, w, c, small, sent
        )
        if k == 0:
            brought[1].append(b1)
            swapped[1].append(moved(b1, sibling))
        cands = candidates(1)
        agg, z, w2, c2 = call(
            functools.partial(odd_kernel, k),
            (mat32, mat32, half, edge),
            [SM] + [VM] * 3 + [HBM, HBM] + [ANY] * (len(cands) - 2),
            scratch=[pltpu.VMEM((width, width), BF16), dmas],
            flops=LOAD * unit,
        )(ids, x, adj, small, *cands)
        if k == 0:
            brought[0].append(tie(c0, recv2, agg))
            swapped[0].append(moved(brought[0][2], sibling))
        cands = [] if last or k == 0 else candidates(0)
        if last:
            outs, more, specs = (mat,) * sections, ends, [VM] * len(ends)
        elif cands:
            outs, more, specs = (mat, mat, edge, both, edge), cands, [HBM, HBM] + [ANY] * (len(cands) - 2)
        else:
            outs, more, specs = (mat, mat, edge), [], []
        out = call(
            functools.partial(finish_kernel, k, last),
            outs,
            [SM] + [VM] * 8 + specs,
            scratch=[dmas] if cands else [],
            flops=LOAD * unit,
        )(ids, recv2, agg, z, w2, c2, h, small, pick, *more)
        ends.append(out[0])
        if not last:
            h, x, sent = out[:3]
        if cands:
            w, c = out[3:]
    got = [moved(pay, across(r)) for r, pay in enumerate(out[1:], 1)]
    return call(
        collect_kernel,
        jax.ShapeDtypeStruct((1, sections, nodes, width), BF16),
        [SM] + [ANY] * (2 * sections - 1),
        scratch=[pltpu.SemaphoreType.DMA((sections,))],
        out_specs=ANY,
    )(ids, *ends, *got)


def solution(mesh):
    in_specs = (
        P(None, "dom", None),
        P("segment", None, None),
        P("segment", None),
        P("segment", None),
        P("dom", None, None, None),
        P("dom", None),
        P("dom"),
        P("segment", "dom", None, None),
        P("segment", "dom"),
    )
    out_specs = P("segment", None, "dom", None)
    return jax.shard_map(shards, mesh=mesh, in_specs=in_specs, out_specs=out_specs, check_vma=False)
```

```python
import functools

import jax
import jax.numpy as jnp
from jax import lax
from jax.experimental import pallas as pl
from jax.experimental.pallas import tpu as pltpu
from jax.sharding import PartitionSpec as P

F32 = jnp.float32
BF16 = jnp.bfloat16
VMEM_BYTES = 12 * 2**20
LOAD = 0.5
VM = pl.BlockSpec(memory_space=pltpu.VMEM)
SM = pl.BlockSpec(memory_space=pltpu.SMEM)
ANY = pl.BlockSpec(memory_space=pl.ANY)
HBM = pl.BlockSpec(memory_space=pltpu.HBM)


def call(body, outs, in_specs, scratch=(), out_specs=None, flops=0, vmem=VMEM_BYTES):
    if out_specs is None:
        out_specs = jax.tree.map(lambda _: VM, outs)
    inner = body.func if isinstance(body, functools.partial) else body
    return pl.pallas_call(
        body,
        name=inner.__name__,
        out_shape=outs,
        in_specs=in_specs,
        out_specs=out_specs,
        scratch_shapes=scratch,
        compiler_params=pltpu.CompilerParams(vmem_limit_bytes=vmem),
        cost_estimate=pl.CostEstimate(flops=int(flops), bytes_accessed=0, transcendentals=0),
    )


def dot(a, b):
    return jnp.dot(a, b, preferred_element_type=F32)


def aligned(start, unit):
    return start if isinstance(start, int) else pl.multiple_of(start, unit)


def normed(hf, gain):
    meansq = jnp.mean(hf * hf, axis=-1, keepdims=True)
    return (hf * lax.rsqrt(meansq + 1e-05) * gain).astype(BF16)


def stepped(h, z):
    return (h.astype(F32) + z / (1.0 + jnp.exp(-z))).astype(BF16)


def start_one(choices, dst, sem):
    for condition, source in choices:

        @pl.when(condition)
        def _():
            pltpu.make_async_copy(source, dst, sem).start()

    return pltpu.make_async_copy(choices[0][1], dst, sem)


def source_of(seg, section, half):
    near, far = 1 + half, 2 - half
    via = seg ^ far
    passed = jnp.logical_or(via == 1, via == 2)
    second = jnp.where(passed, seg ^ 3, via)
    return jnp.where(seg == section, 0, jnp.where((seg ^ near) == section, 1, jnp.where(second == section, 2, 3)))


def fetch_half(seg, core, section, half, own, mine, theirs, dst, sem):
    width = dst.shape[1]
    source = source_of(seg, section, half)
    choices = [(source == 0, own.at[pl.ds(half * width, width), :])]
    for here, refs in ((core == half, mine), (core != half, theirs)):
        for i, ref in enumerate(refs):
            choices.append((jnp.logical_and(here, source == i + 1), ref.at[pl.ds(0, width), :]))
    return [start_one(choices, dst, sem)]


def fetch_cross(seg, core, section, own, mine, dst, sems):
    tile = dst.shape[0]
    width = dst.shape[1]
    blocks = own.shape[0]
    source = jnp.where(core == 0, source_of(seg, section, 0), source_of(seg, section, 1))
    for i, ref in enumerate(mine):

        @pl.when(source == i + 1)
        def _():
            for b in range(blocks):
                part = ref.at[pl.ds(width, tile), pl.ds(b * tile, tile)]
                pltpu.make_async_copy(part, dst.at[:, pl.ds(b * tile, tile)], sems.at[b]).start()

    @pl.when(source == 0)
    def _():
        for b in range(blocks):
            pltpu.make_async_copy(own.at[b], dst.at[:, pl.ds(b * tile, tile)], sems.at[b]).start()

    return [pltpu.make_async_copy(own.at[b], dst.at[:, pl.ds(b * tile, tile)], sems.at[b]) for b in range(blocks)]


def fetch_layer(section, step, ids, cands, top, bottom, cross, sems):
    own, own_cross, mine, theirs = cands
    seg, core = ids[0], ids[1]
    return (
        fetch_half(seg, core, section, 0, own.at[step], mine, theirs, top, sems.at[0])
        + fetch_half(seg, core, section, 1, own.at[step], mine, theirs, bottom, sems.at[1])
        + fetch_cross(seg, core, section, own_cross.at[step], mine, cross, sems.at[pl.ds(2, own_cross.shape[1])])
    )


def cands_of(refs):
    n = (len(refs) - 2) // 2
    return refs[0], refs[1], refs[2 : 2 + n], refs[2 + n :]


def first_kernel(ids, cols, counts, feat_ref, tiles_ref, s0, s1, s2, s3, h_ref, adj_ref, x_ref, sent_ref, small_ref, pick_ref, sem):
    nblk, slots, tile, _ = tiles_ref.shape
    nodes, width = h_ref.shape
    seg = ids[0]
    copy = pltpu.make_async_copy(feat_ref.at[seg], h_ref, sem)
    copy.start()
    for r in range(nblk):
        for j in range(nblk):
            total = jnp.zeros((tile, tile), F32)
            for k in range(slots):
                used = jnp.logical_and(k < counts[r], cols[r, k] == j)
                total = total + jnp.where(used, tiles_ref[r, k].astype(F32), 0.0)
            adj_ref[r * tile : (r + 1) * tile, j * tile : (j + 1) * tile] = total.astype(BF16)
    for r, ref in enumerate((s0, s1, s2, s3)):
        small_ref[seg ^ r] = ref[...]
    sections, steps = small_ref.shape[:2]
    bound = small_ref.shape[2] - 2 * width
    for k in range(sections):
        for p in range(steps):
            rows = small_ref[k, p : p + 1, 2 * width :]
            index = lax.broadcasted_iota(jnp.int32, (nodes, bound), 0).astype(F32)
            pick_ref[k, p] = jnp.where(index == rows, 1.0, 0.0).T.astype(BF16)
    copy.wait()
    x = normed(h_ref[...].astype(F32), small_ref[0, 0:1, width : 2 * width])
    x_ref[...] = x
    sent_ref[...] = dot(pick_ref[0, 0], x).astype(BF16)


def payload_kernel(ids, own, cross, *refs):
    outs, sems = refs[:-1], refs[-1]
    copies = []
    for p, out_ref in enumerate(outs):
        width = out_ref.shape[1]
        tile = cross.shape[-1]
        half = own.at[p, pl.ds(pl.multiple_of(ids[1] * width, width), width), :]
        copies.append(pltpu.make_async_copy(half, out_ref.at[pl.ds(0, width), :], sems.at[p, 0]))
        for b in range(cross.shape[1]):
            dst = out_ref.at[pl.ds(width, tile), pl.ds(b * tile, tile)]
            copies.append(pltpu.make_async_copy(cross.at[p, b], dst, sems.at[p, b + 1]))
    for copy in copies:
        copy.start()
    for copy in copies:
        copy.wait()


def select_kernel(wanted, ids, *refs):
    count = len(wanted)
    outs, sources = refs[-count:], refs
    for out_ref, rule in zip(outs, wanted):
        for i, segments in enumerate(rule):
            here = functools.reduce(jnp.logical_or, [ids[0] == s for s in segments])

            @pl.when(here)
            def _():
                out_ref[...] = sources[i][...]


def select(ids, sources, wanted, deps=()):
    shape = jax.ShapeDtypeStruct(sources[0].shape, sources[0].dtype)
    specs = [SM] + [VM] * len(sources) + [ANY] * len(deps)
    return call(functools.partial(select_kernel, wanted), [shape] * len(wanted), specs, vmem=8 * 2**20)(ids, *sources, *deps)


def tie(value, *deps):
    return pl.pallas_call(
        lambda *refs: None,
        name="tie",
        out_shape=jax.ShapeDtypeStruct(value.shape, value.dtype),
        in_specs=[ANY] * (1 + len(deps)),
        out_specs=ANY,
        input_output_aliases={0: 0},
        compiler_params=pltpu.CompilerParams(vmem_limit_bytes=2**20),
    )(value, *deps)


def load_kernel(section, ids, dep, *refs):
    w_ref, c_ref, sems = refs[-3:]
    width = w_ref.shape[1]
    parts = w_ref.at[pl.ds(0, width), :], w_ref.at[pl.ds(width, width), :]
    for copy in fetch_layer(section, 0, ids, cands_of(refs[:-3]), *parts, c_ref, sems):
        copy.wait()


def edge_kernel(section, x_ref, h_ref, adj_ref, w_ref, c_ref, small_ref, pick_ref, agg_ref, z_ref, cross_ref, h_out):
    width = x_ref.shape[1]
    pick = pick_ref[section, 1]
    x = x_ref[...]
    adj = dot(pick, adj_ref[...]).astype(BF16)
    agg_ref[...] = dot(adj, x)
    xb = dot(pick, x).astype(BF16)
    z_ref[...] = dot(xb, w_ref[:width, :]) + small_ref[section, 0:1, :width]
    tile = c_ref.shape[0]
    cross = jnp.zeros((pick.shape[0], tile), F32)
    for b in range(c_ref.shape[1] // tile):
        lanes = slice(b * tile, (b + 1) * tile)
        cross = cross + dot(pick[:, lanes], c_ref[:, lanes])
    cross_ref[...] = cross.astype(BF16)
    h_out[...] = dot(pick, h_ref[...]).astype(BF16)


def send_kernel(section, recv_ref, agg_ref, z_ref, cross_ref, h_ref, w_ref, small_ref, sent_ref):
    width = h_ref.shape[1]
    agg = (agg_ref[...] + dot(cross_ref[...], recv_ref[...])).astype(BF16)
    z = z_ref[...] + dot(agg, w_ref[width:, :])
    h = stepped(h_ref[...], z)
    sent_ref[...] = normed(h.astype(F32), small_ref[section, 1:2, width : 2 * width])


def remote(c_ref, recv_ref, i, block):
    tile = c_ref.shape[0]
    parts = []
    for b in range(block // tile):
        lanes = pl.ds(aligned(i * block + b * tile, tile), tile)
        parts.append(dot(c_ref[:, lanes], recv_ref[...]))
    return jnp.concatenate(parts, axis=0)


def even_kernel(section, x_ref, h_ref, adj_ref, recv_ref, w_ref, c_ref, small_ref, dep, h_out, x_out):
    nodes, width = x_ref.shape
    block = 256

    def even(i, carry):
        rows = pl.ds(aligned(i * block, block), block)
        agg = dot(adj_ref[rows, :], x_ref[...]) + remote(c_ref, recv_ref, i, block)
        z = dot(x_ref[rows, :], w_ref[:width, :]) + small_ref[section, 0:1, :width]
        z = z + dot(agg.astype(BF16), w_ref[width:, :])
        h = stepped(h_ref[rows, :], z)
        h_out[rows, :] = h
        x_out[rows, :] = normed(h.astype(F32), small_ref[section, 1:2, width : 2 * width])
        return carry

    lax.fori_loop(0, nodes // block, even, 0)


def odd_kernel(section, ids, dep, x_ref, adj_ref, small_ref, *refs):
    agg_out, z_out, w2_out, c_out, w1_ref, sems = refs[-6:]
    nodes, width = x_ref.shape
    block = 256
    copies = fetch_layer(section, 1, ids, cands_of(refs[:-6]), w1_ref, w2_out, c_out, sems)
    copies[0].wait()

    def odd(i, carry):
        rows = pl.ds(aligned(i * block, block), block)
        agg_out[rows, :] = dot(adj_ref[rows, :], x_ref[...])
        z_out[rows, :] = dot(x_ref[rows, :], w1_ref[...]) + small_ref[section, 1:2, :width]
        return carry

    lax.fori_loop(0, nodes // block, odd, 0)
    for copy in copies[1:]:
        copy.wait()


def finish_kernel(section, last, ids, recv_ref, agg_ref, z_ref, w2_ref, c_ref, h_ref, small_ref, pick_ref, *refs):
    nodes, width = h_ref.shape
    block = 256
    fetch = not last and len(refs) > 5
    if last:
        ends, (h_out, *pays) = refs[:section], refs[section:]
    elif not fetch:
        h_out, x_out, sent_out = refs
    else:
        h_out, x_out, sent_out, w_out, c_out, sems = refs[-6:]
        parts = w_out.at[pl.ds(0, width), :], w_out.at[pl.ds(width, width), :]
        copies = fetch_layer(section + 1, 0, ids, cands_of(refs[:-6]), *parts, c_out, sems)

    def odd(i, carry):
        rows = pl.ds(aligned(i * block, block), block)
        agg = agg_ref[rows, :] + remote(c_ref, recv_ref, i, block)
        z = z_ref[rows, :] + dot(agg.astype(BF16), w2_ref[...])
        h = stepped(h_ref[rows, :], z)
        h_out[rows, :] = h
        if last:
            for r, pay_ref in enumerate(pays, 1):

                @pl.when(ids[0] == section ^ r)
                def _():
                    pay_ref[rows, :] = h
        else:
            x_out[rows, :] = normed(h.astype(F32), small_ref[section + 1, 0:1, width : 2 * width])
        return carry

    if last:
        for k, end_ref in enumerate(ends):
            for r, pay_ref in enumerate(pays, 1):

                @pl.when(ids[0] == k ^ r)
                def _():
                    pay_ref[...] = end_ref[...]

    lax.fori_loop(0, nodes // block, odd, 0)
    if not last:
        sent_out[...] = dot(pick_ref[section + 1, 0], x_out[...]).astype(BF16)
    if fetch:
        for copy in copies:
            copy.wait()


def collect_kernel(ids, *refs):
    out_ref, sems = refs[-2:]
    sections = out_ref.shape[1]
    ends, got = refs[:sections], refs[sections:-2]
    copies = [start_one([(ids[0] == k, end) for k, end in enumerate(ends)], out_ref.at[0, ids[0]], sems.at[0])]
    for r, ref in enumerate(got, 1):
        copies.append(pltpu.make_async_copy(ref, out_ref.at[0, ids[0] ^ r], sems.at[r]))
        copies[-1].start()
    for copy in copies:
        copy.wait()


def shards(features, weights, bias, gain, tile_val, tile_col, tile_count, cross_val, send_rows):
    sections = lax.axis_size("segment")
    doms = lax.axis_size("dom")
    seg = lax.axis_index("segment")
    core = lax.axis_index("dom") & 1
    steps, _, width = weights.shape
    nodes = features.shape[1]
    bound = send_rows.shape[1]
    nbits = doms.bit_length() - 1
    ids = jnp.stack([seg, core]).astype(jnp.int32)

    def moved(value, target, sources=range(sections)):
        pairs = []
        for s in sources:
            for d in range(doms):
                t, e = target(s, d)
                pairs.append((s * doms + d, t * doms + e))
        return lax.ppermute(value, ("segment", "dom"), pairs)

    def near(s, d):
        return s ^ (1 + (d & 1)), d

    def far(s, d):
        return s ^ (2 - (d & 1)), d

    def sibling(s, d):
        return s, d ^ 1

    def across(r):
        return lambda s, d: (s ^ r, d)

    def exchange(sent, step):
        bit = step * (nbits - 1) // max(steps - 1, 1)
        return lax.ppermute(sent, "dom", [(i, i ^ 1 << bit) for i in range(doms)])

    mat = jax.ShapeDtypeStruct((nodes, width), BF16)
    mat32 = jax.ShapeDtypeStruct((nodes, width), F32)
    edge = jax.ShapeDtypeStruct((bound, width), BF16)
    edge32 = jax.ShapeDtypeStruct((bound, width), F32)
    half = jax.ShapeDtypeStruct((width, width), BF16)
    both = jax.ShapeDtypeStruct((2 * width, width), BF16)
    load = jax.ShapeDtypeStruct((width + bound, width), BF16)
    picks = jax.ShapeDtypeStruct((sections, steps, bound, nodes), BF16)
    unit = 2 * nodes * width * width
    dmas = pltpu.SemaphoreType.DMA((2 + cross_val.shape[1],))

    small = jnp.concatenate([bias, gain, send_rows.astype(F32)], axis=1)
    smalls = [small] + [moved(small, across(r)) for r in range(1, sections)]
    own = call(
        payload_kernel,
        [load] * steps,
        [SM, HBM, HBM],
        scratch=[pltpu.SemaphoreType.DMA((steps, 1 + cross_val.shape[1]))],
    )(ids, weights, cross_val)
    own = [tie(v, *smalls[1:]) for v in own]
    h, adj, x, sent, small, pick = call(
        first_kernel,
        (mat, jax.ShapeDtypeStruct((nodes, nodes), BF16), mat, edge, jax.ShapeDtypeStruct((sections,) + small.shape, F32), picks),
        [SM, SM, SM, HBM, VM] + [VM] * sections,
        scratch=[pltpu.SemaphoreType.DMA],
    )(ids, tile_col, tile_count, features, tile_val, *smalls)
    recv = exchange(sent, 0)

    inner, outer = (1, 2), (0, 3)
    a0, a1 = [moved(v, near) for v in own]
    (pay,) = select(ids, [a0, own[0]], [(inner, outer)])
    b0 = moved(pay, far)
    (pay,) = select(ids, [a1, own[1]], [(inner, outer)], [pay, sent])
    b1 = moved(pay, far)
    b0 = tie(b0, pay)
    (pay,) = select(ids, [own[0], a0], [(inner, outer)], [pay])
    c0 = moved(pay, far)
    (pay,) = select(ids, [own[1], a1], [(inner, outer)], [pay])
    c1 = moved(pay, far)
    sa0 = moved(a0, sibling)
    sb0 = moved(b0, sibling)
    brought, swapped = [[a0, b0], [a1]], [[sa0, sb0], []]

    def candidates(p):
        return [weights, cross_val, *brought[p], *swapped[p]]

    def loaded(section, dep):
        cands = candidates(0)
        specs = [SM, ANY, HBM, HBM] + [ANY] * (len(cands) - 2)
        kernel = functools.partial(load_kernel, section)
        return call(kernel, (both, edge), specs, scratch=[dmas])(ids, dep, *cands)

    w, c = loaded(0, b1)

    ends = []
    for k in range(sections):
        last = k == sections - 1
        if k > 0:
            recv = exchange(sent, 0)
        if k == 1:
            w, c = loaded(1, x)
        edges = call(
            functools.partial(edge_kernel, k),
            (edge32, edge32, jax.ShapeDtypeStruct((bound, bound), BF16), edge),
            [VM] * 7,
            flops=LOAD * unit / 4,
        )(x, h, adj, w, c, small, pick)
        sent = call(functools.partial(send_kernel, k), edge, [VM] * 7, flops=LOAD * unit / 4)(recv, *edges[:3], edges[3], w, small)
        recv2 = exchange(sent, 1)
        if k == 1:
            brought[1].append(tie(c1, sent))
            swapped[1].append(moved(brought[1][2], sibling))
        h, x = call(functools.partial(even_kernel, k), (mat, mat), [VM] * 7 + [ANY], flops=LOAD * unit)(
            x, h, adj, recv, w, c, small, sent
        )
        if k == 0:
            brought[1] = [tie(a1, sent), b1]
            swapped[1] = [moved(v, sibling) for v in brought[1]]
        cands = candidates(1)
        agg, z, w2, c2 = call(
            functools.partial(odd_kernel, k),
            (mat32, mat32, half, edge),
            [SM, ANY] + [VM] * 3 + [HBM, HBM] + [ANY] * (len(cands) - 2),
            scratch=[pltpu.VMEM((width, width), BF16), dmas],
            flops=LOAD * unit,
        )(ids, c0 if k == 0 else x, x, adj, small, *cands)
        if k == 0:
            brought[0].append(tie(c0, recv2, agg))
            swapped[0].append(moved(brought[0][2], sibling))
        cands = [] if last or k == 0 else candidates(0)
        if last:
            outs, more, specs = (mat,) * sections, ends, [VM] * len(ends)
        elif cands:
            outs, more, specs = (mat, mat, edge, both, edge), cands, [HBM, HBM] + [ANY] * (len(cands) - 2)
        else:
            outs, more, specs = (mat, mat, edge), [], []
        out = call(
            functools.partial(finish_kernel, k, last),
            outs,
            [SM] + [VM] * 8 + specs,
            scratch=[dmas] if cands else [],
            flops=LOAD * unit,
        )(ids, recv2, agg, z, w2, c2, h, small, pick, *more)
        ends.append(out[0])
        if not last:
            h, x, sent = out[:3]
        if cands:
            w, c = out[3:]
    got = [moved(pay, across(r)) for r, pay in enumerate(out[1:], 1)]
    return call(
        collect_kernel,
        jax.ShapeDtypeStruct((1, sections, nodes, width), BF16),
        [SM] + [ANY] * (2 * sections - 1),
        scratch=[pltpu.SemaphoreType.DMA((sections,))],
        out_specs=ANY,
    )(ids, *ends, *got)


def solution(mesh):
    in_specs = (
        P(None, "dom", None),
        P("segment", None, None),
        P("segment", None),
        P("segment", None),
        P("dom", None, None, None),
        P("dom", None),
        P("dom"),
        P("segment", "dom", None, None),
        P("segment", "dom"),
    )
    out_specs = P("segment", None, "dom", None)
    return jax.shard_map(shards, mesh=mesh, in_specs=in_specs, out_specs=out_specs, check_vma=False)
```

```python
import functools

import jax
import jax.numpy as jnp
from jax import lax
from jax.experimental import pallas as pl
from jax.experimental.pallas import tpu as pltpu
from jax.sharding import PartitionSpec as P

F32 = jnp.float32
BF16 = jnp.bfloat16
VMEM_BYTES = 12 * 2**20
LOAD = 0.5
VM = pl.BlockSpec(memory_space=pltpu.VMEM)
SM = pl.BlockSpec(memory_space=pltpu.SMEM)
ANY = pl.BlockSpec(memory_space=pl.ANY)
HBM = pl.BlockSpec(memory_space=pltpu.HBM)


def call(body, outs, in_specs, scratch=(), out_specs=None, flops=0, vmem=VMEM_BYTES):
    if out_specs is None:
        out_specs = jax.tree.map(lambda _: VM, outs)
    inner = body.func if isinstance(body, functools.partial) else body
    return pl.pallas_call(
        body,
        name=inner.__name__,
        out_shape=outs,
        in_specs=in_specs,
        out_specs=out_specs,
        scratch_shapes=scratch,
        compiler_params=pltpu.CompilerParams(vmem_limit_bytes=vmem),
        cost_estimate=pl.CostEstimate(flops=int(flops), bytes_accessed=0, transcendentals=0),
    )


def dot(a, b):
    return jnp.dot(a, b, preferred_element_type=F32)


def aligned(start, unit):
    return start if isinstance(start, int) else pl.multiple_of(start, unit)


def normed(hf, gain):
    meansq = jnp.mean(hf * hf, axis=-1, keepdims=True)
    return (hf * lax.rsqrt(meansq + 1e-05) * gain).astype(BF16)


def stepped(h, z):
    half = 0.5 * z
    return (h.astype(F32) + half + half * jnp.tanh(half)).astype(BF16)


def start_one(choices, dst, sem):
    for condition, source in choices:

        @pl.when(condition)
        def _():
            pltpu.make_async_copy(source, dst, sem).start()

    return pltpu.make_async_copy(choices[0][1], dst, sem)


def source_of(seg, section, half):
    near, far = 1 + half, 2 - half
    via = seg ^ far
    passed = jnp.logical_or(via == 1, via == 2)
    second = jnp.where(passed, seg ^ 3, via)
    return jnp.where(seg == section, 0, jnp.where((seg ^ near) == section, 1, jnp.where(second == section, 2, 3)))


def fetch_half(seg, core, section, half, own, mine, theirs, dst, sem):
    width = dst.shape[1]
    source = source_of(seg, section, half)
    choices = [(source == 0, own.at[pl.ds(half * width, width), :])]
    for here, refs in ((core == half, mine), (core != half, theirs)):
        for i, ref in enumerate(refs):
            choices.append((jnp.logical_and(here, source == i + 1), ref.at[pl.ds(0, width), :]))
    return [start_one(choices, dst, sem)]


def fetch_cross(seg, core, section, own, mine, dst, sems):
    tile = dst.shape[0]
    width = dst.shape[1]
    blocks = own.shape[0]
    source = jnp.where(core == 0, source_of(seg, section, 0), source_of(seg, section, 1))
    for i, ref in enumerate(mine):

        @pl.when(source == i + 1)
        def _():
            for b in range(blocks):
                part = ref.at[pl.ds(width, tile), pl.ds(b * tile, tile)]
                pltpu.make_async_copy(part, dst.at[:, pl.ds(b * tile, tile)], sems.at[b]).start()

    @pl.when(source == 0)
    def _():
        for b in range(blocks):
            pltpu.make_async_copy(own.at[b], dst.at[:, pl.ds(b * tile, tile)], sems.at[b]).start()

    return [pltpu.make_async_copy(own.at[b], dst.at[:, pl.ds(b * tile, tile)], sems.at[b]) for b in range(blocks)]


def fetch_layer(section, step, ids, cands, top, bottom, cross, sems):
    own, own_cross, mine, theirs = cands
    seg, core = ids[0], ids[1]
    return (
        fetch_half(seg, core, section, 0, own.at[step], mine, theirs, top, sems.at[0])
        + fetch_half(seg, core, section, 1, own.at[step], mine, theirs, bottom, sems.at[1])
        + fetch_cross(seg, core, section, own_cross.at[step], mine, cross, sems.at[pl.ds(2, own_cross.shape[1])])
    )


def cands_of(refs):
    n = (len(refs) - 2) // 2
    return refs[0], refs[1], refs[2 : 2 + n], refs[2 + n :]


def first_kernel(ids, cols, counts, feat_ref, tiles_ref, s0, s1, s2, s3, h_ref, adj_ref, x_ref, sent_ref, small_ref, pick_ref, sem):
    nblk, slots, tile, _ = tiles_ref.shape
    nodes, width = h_ref.shape
    seg = ids[0]
    copy = pltpu.make_async_copy(feat_ref.at[seg], h_ref, sem)
    copy.start()
    for r in range(nblk):
        for j in range(nblk):
            total = jnp.zeros((tile, tile), F32)
            for k in range(slots):
                used = jnp.logical_and(k < counts[r], cols[r, k] == j)
                total = total + jnp.where(used, tiles_ref[r, k].astype(F32), 0.0)
            adj_ref[r * tile : (r + 1) * tile, j * tile : (j + 1) * tile] = total.astype(BF16)
    for r, ref in enumerate((s0, s1, s2, s3)):
        small_ref[seg ^ r] = ref[...]
    sections, steps = small_ref.shape[:2]
    bound = small_ref.shape[2] - 2 * width
    for k in range(sections):
        for p in range(steps):
            rows = small_ref[k, p : p + 1, 2 * width :]
            index = lax.broadcasted_iota(jnp.int32, (nodes, bound), 0).astype(F32)
            pick_ref[k, p] = jnp.where(index == rows, 1.0, 0.0).T.astype(BF16)
    copy.wait()
    x = normed(h_ref[...].astype(F32), small_ref[0, 0:1, width : 2 * width])
    x_ref[...] = x
    sent_ref[...] = dot(pick_ref[0, 0], x).astype(BF16)


def payload_kernel(ids, own, cross, *refs):
    outs, sems = refs[:-1], refs[-1]
    copies = []
    for p, out_ref in enumerate(outs):
        width = out_ref.shape[1]
        tile = cross.shape[-1]
        half = own.at[p, pl.ds(pl.multiple_of(ids[1] * width, width), width), :]
        copies.append(pltpu.make_async_copy(half, out_ref.at[pl.ds(0, width), :], sems.at[p, 0]))
        for b in range(cross.shape[1]):
            dst = out_ref.at[pl.ds(width, tile), pl.ds(b * tile, tile)]
            copies.append(pltpu.make_async_copy(cross.at[p, b], dst, sems.at[p, b + 1]))
    for copy in copies:
        copy.start()
    for copy in copies:
        copy.wait()


def select_kernel(wanted, ids, *refs):
    count = len(wanted)
    outs, sources = refs[-count:], refs
    for out_ref, rule in zip(outs, wanted):
        for i, segments in enumerate(rule):
            here = functools.reduce(jnp.logical_or, [ids[0] == s for s in segments])

            @pl.when(here)
            def _():
                out_ref[...] = sources[i][...]


def select(ids, sources, wanted, deps=()):
    shape = jax.ShapeDtypeStruct(sources[0].shape, sources[0].dtype)
    specs = [SM] + [VM] * len(sources) + [ANY] * len(deps)
    return call(functools.partial(select_kernel, wanted), [shape] * len(wanted), specs, vmem=8 * 2**20)(ids, *sources, *deps)


def tie(value, *deps):
    return pl.pallas_call(
        lambda *refs: None,
        name="tie",
        out_shape=jax.ShapeDtypeStruct(value.shape, value.dtype),
        in_specs=[ANY] * (1 + len(deps)),
        out_specs=ANY,
        input_output_aliases={0: 0},
        compiler_params=pltpu.CompilerParams(vmem_limit_bytes=2**20),
    )(value, *deps)


def load_kernel(section, ids, dep, *refs):
    w_ref, c_ref, sems = refs[-3:]
    width = w_ref.shape[1]
    parts = w_ref.at[pl.ds(0, width), :], w_ref.at[pl.ds(width, width), :]
    for copy in fetch_layer(section, 0, ids, cands_of(refs[:-3]), *parts, c_ref, sems):
        copy.wait()


def edge_kernel(section, x_ref, h_ref, adj_ref, w_ref, c_ref, small_ref, pick_ref, agg_ref, z_ref, cross_ref, h_out):
    width = x_ref.shape[1]
    pick = pick_ref[section, 1]
    x = x_ref[...]
    adj = dot(pick, adj_ref[...]).astype(BF16)
    agg_ref[...] = dot(adj, x)
    xb = dot(pick, x).astype(BF16)
    z_ref[...] = dot(xb, w_ref[:width, :]) + small_ref[section, 0:1, :width]
    tile = c_ref.shape[0]
    cross = jnp.zeros((pick.shape[0], tile), F32)
    for b in range(c_ref.shape[1] // tile):
        lanes = slice(b * tile, (b + 1) * tile)
        cross = cross + dot(pick[:, lanes], c_ref[:, lanes])
    cross_ref[...] = cross.astype(BF16)
    h_out[...] = dot(pick, h_ref[...]).astype(BF16)


def send_kernel(section, recv_ref, agg_ref, z_ref, cross_ref, h_ref, w_ref, small_ref, sent_ref):
    width = h_ref.shape[1]
    agg = (agg_ref[...] + dot(cross_ref[...], recv_ref[...])).astype(BF16)
    z = z_ref[...] + dot(agg, w_ref[width:, :])
    h = stepped(h_ref[...], z)
    sent_ref[...] = normed(h.astype(F32), small_ref[section, 1:2, width : 2 * width])


def remote(c_ref, recv_ref, i, block):
    tile = c_ref.shape[0]
    parts = []
    for b in range(block // tile):
        lanes = pl.ds(aligned(i * block + b * tile, tile), tile)
        parts.append(dot(c_ref[:, lanes], recv_ref[...]))
    return jnp.concatenate(parts, axis=0)


def even_kernel(section, x_ref, h_ref, adj_ref, recv_ref, w_ref, c_ref, small_ref, dep, h_out, x_out):
    nodes, width = x_ref.shape
    block = 256

    def even(i, carry):
        rows = pl.ds(aligned(i * block, block), block)
        agg = dot(adj_ref[rows, :], x_ref[...]) + remote(c_ref, recv_ref, i, block)
        z = dot(x_ref[rows, :], w_ref[:width, :]) + small_ref[section, 0:1, :width]
        z = z + dot(agg.astype(BF16), w_ref[width:, :])
        h = stepped(h_ref[rows, :], z)
        h_out[rows, :] = h
        x_out[rows, :] = normed(h.astype(F32), small_ref[section, 1:2, width : 2 * width])
        return carry

    lax.fori_loop(0, nodes // block, even, 0)


def odd_kernel(section, ids, dep, x_ref, adj_ref, small_ref, *refs):
    agg_out, z_out, w2_out, c_out, w1_ref, sems = refs[-6:]
    nodes, width = x_ref.shape
    block = 256
    copies = fetch_layer(section, 1, ids, cands_of(refs[:-6]), w1_ref, w2_out, c_out, sems)
    copies[0].wait()

    def odd(i, carry):
        rows = pl.ds(aligned(i * block, block), block)
        agg_out[rows, :] = dot(adj_ref[rows, :], x_ref[...])
        z_out[rows, :] = dot(x_ref[rows, :], w1_ref[...]) + small_ref[section, 1:2, :width]
        return carry

    lax.fori_loop(0, nodes // block, odd, 0)
    for copy in copies[1:]:
        copy.wait()


def finish_kernel(section, last, ids, recv_ref, agg_ref, z_ref, w2_ref, c_ref, h_ref, small_ref, pick_ref, *refs):
    nodes, width = h_ref.shape
    block = 256
    fetch = not last and len(refs) > 5
    if last:
        ends, (h_out, *pays) = refs[:section], refs[section:]
    elif not fetch:
        h_out, x_out, sent_out = refs
    else:
        h_out, x_out, sent_out, w_out, c_out, sems = refs[-6:]
        parts = w_out.at[pl.ds(0, width), :], w_out.at[pl.ds(width, width), :]
        copies = fetch_layer(section + 1, 0, ids, cands_of(refs[:-6]), *parts, c_out, sems)

    def odd(i, carry):
        rows = pl.ds(aligned(i * block, block), block)
        agg = agg_ref[rows, :] + remote(c_ref, recv_ref, i, block)
        z = z_ref[rows, :] + dot(agg.astype(BF16), w2_ref[...])
        h = stepped(h_ref[rows, :], z)
        h_out[rows, :] = h
        if last:
            for r, pay_ref in enumerate(pays, 1):

                @pl.when(ids[0] == section ^ r)
                def _():
                    pay_ref[rows, :] = h
        else:
            x_out[rows, :] = normed(h.astype(F32), small_ref[section + 1, 0:1, width : 2 * width])
        return carry

    if last:
        for k, end_ref in enumerate(ends):
            for r, pay_ref in enumerate(pays, 1):

                @pl.when(ids[0] == k ^ r)
                def _():
                    pay_ref[...] = end_ref[...]

    for i in range(nodes // block):
        odd(i, 0)
    if not last:
        sent_out[...] = dot(pick_ref[section + 1, 0], x_out[...]).astype(BF16)
    if fetch:
        for copy in copies:
            copy.wait()


def collect_kernel(ids, *refs):
    out_ref, sems = refs[-2:]
    sections = out_ref.shape[1]
    ends, got = refs[:sections], refs[sections:-2]
    copies = [start_one([(ids[0] == k, end) for k, end in enumerate(ends)], out_ref.at[0, ids[0]], sems.at[0])]
    for r, ref in enumerate(got, 1):
        copies.append(pltpu.make_async_copy(ref, out_ref.at[0, ids[0] ^ r], sems.at[r]))
        copies[-1].start()
    for copy in copies:
        copy.wait()


def shards(features, weights, bias, gain, tile_val, tile_col, tile_count, cross_val, send_rows):
    sections = lax.axis_size("segment")
    doms = lax.axis_size("dom")
    seg = lax.axis_index("segment")
    core = lax.axis_index("dom") & 1
    steps, _, width = weights.shape
    nodes = features.shape[1]
    bound = send_rows.shape[1]
    nbits = doms.bit_length() - 1
    ids = jnp.stack([seg, core]).astype(jnp.int32)

    def moved(value, target, sources=range(sections)):
        pairs = []
        for s in sources:
            for d in range(doms):
                t, e = target(s, d)
                pairs.append((s * doms + d, t * doms + e))
        return lax.ppermute(value, ("segment", "dom"), pairs)

    def near(s, d):
        return s ^ (1 + (d & 1)), d

    def far(s, d):
        return s ^ (2 - (d & 1)), d

    def sibling(s, d):
        return s, d ^ 1

    def across(r):
        return lambda s, d: (s ^ r, d)

    def exchange(sent, step):
        bit = step * (nbits - 1) // max(steps - 1, 1)
        return lax.ppermute(sent, "dom", [(i, i ^ 1 << bit) for i in range(doms)])

    mat = jax.ShapeDtypeStruct((nodes, width), BF16)
    mat32 = jax.ShapeDtypeStruct((nodes, width), F32)
    edge = jax.ShapeDtypeStruct((bound, width), BF16)
    edge32 = jax.ShapeDtypeStruct((bound, width), F32)
    half = jax.ShapeDtypeStruct((width, width), BF16)
    both = jax.ShapeDtypeStruct((2 * width, width), BF16)
    load = jax.ShapeDtypeStruct((width + bound, width), BF16)
    picks = jax.ShapeDtypeStruct((sections, steps, bound, nodes), BF16)
    unit = 2 * nodes * width * width
    dmas = pltpu.SemaphoreType.DMA((2 + cross_val.shape[1],))

    own = call(
        payload_kernel,
        [load] * steps,
        [SM, HBM, HBM],
        scratch=[pltpu.SemaphoreType.DMA((steps, 1 + cross_val.shape[1]))],
    )(ids, weights, cross_val)
    small = tie(jnp.concatenate([bias, gain, send_rows.astype(F32)], axis=1), own[0])
    smalls = [small] + [moved(small, across(r)) for r in range(1, sections)]
    h, adj, x, sent, small, pick = call(
        first_kernel,
        (mat, jax.ShapeDtypeStruct((nodes, nodes), BF16), mat, edge, jax.ShapeDtypeStruct((sections,) + small.shape, F32), picks),
        [SM, SM, SM, HBM, VM] + [VM] * sections,
        scratch=[pltpu.SemaphoreType.DMA],
    )(ids, tile_col, tile_count, features, tile_val, *smalls)
    recv = exchange(sent, 0)

    inner, outer = (1, 2), (0, 3)
    a0, a1 = [moved(v, near) for v in own]
    (pay,) = select(ids, [a0, own[0]], [(inner, outer)])
    b0 = moved(pay, far)
    (pay,) = select(ids, [a1, own[1]], [(inner, outer)], [pay])
    b1 = moved(pay, far)
    b0 = tie(b0, pay, sent)
    (pay,) = select(ids, [own[0], a0], [(inner, outer)], [pay])
    c0 = moved(pay, far)
    (pay,) = select(ids, [own[1], a1], [(inner, outer)], [pay])
    c1 = moved(pay, far)
    sa0 = moved(a0, sibling)
    sb0 = moved(b0, sibling)
    brought, swapped = [[a0, b0], [a1]], [[sa0, sb0], []]

    def candidates(p):
        return [weights, cross_val, *brought[p], *swapped[p]]

    def loaded(section, dep):
        cands = candidates(0)
        specs = [SM, ANY, HBM, HBM] + [ANY] * (len(cands) - 2)
        kernel = functools.partial(load_kernel, section)
        return call(kernel, (both, edge), specs, scratch=[dmas])(ids, dep, *cands)

    w, c = loaded(0, pay)

    ends = []
    for k in range(sections):
        last = k == sections - 1
        if k > 0:
            recv = exchange(sent, 0)
        if k == 1:
            c1 = tie(c1, x)
            w, c = loaded(1, c1)
        edges = call(
            functools.partial(edge_kernel, k),
            (edge32, edge32, jax.ShapeDtypeStruct((bound, bound), BF16), edge),
            [VM] * 7,
            flops=LOAD * unit / 4,
        )(x, h, adj, w, c, small, pick)
        sent = call(functools.partial(send_kernel, k), edge, [VM] * 7, flops=LOAD * unit / 4)(recv, *edges[:3], edges[3], w, small)
        recv2 = exchange(sent, 1)
        if k == 1:
            brought[1].append(c1)
            swapped[1].append(moved(brought[1][2], sibling))
        h, x = call(functools.partial(even_kernel, k), (mat, mat), [VM] * 7 + [ANY], flops=LOAD * unit)(
            x, h, adj, recv, w, c, small, sent
        )
        if k == 0:
            brought[1] = [tie(a1, sent), tie(b1, sent)]
            swapped[1] = [moved(v, sibling) for v in brought[1]]
        cands = candidates(1)
        agg, z, w2, c2 = call(
            functools.partial(odd_kernel, k),
            (mat32, mat32, half, edge),
            [SM, ANY] + [VM] * 3 + [HBM, HBM] + [ANY] * (len(cands) - 2),
            scratch=[pltpu.VMEM((width, width), BF16), dmas],
            flops=LOAD * unit,
        )(ids, c0 if k == 0 else x, x, adj, small, *cands)
        if k == 0:
            brought[0].append(tie(c0, recv2, agg))
            swapped[0].append(moved(brought[0][2], sibling))
        cands = [] if last or k == 0 else candidates(0)
        if last:
            outs, more, specs = (mat,) * sections, ends, [VM] * len(ends)
        elif cands:
            outs, more, specs = (mat, mat, edge, both, edge), cands, [HBM, HBM] + [ANY] * (len(cands) - 2)
        else:
            outs, more, specs = (mat, mat, edge), [], []
        out = call(
            functools.partial(finish_kernel, k, last),
            outs,
            [SM] + [VM] * 8 + specs,
            scratch=[dmas] if cands else [],
            flops=LOAD * unit,
        )(ids, recv2, agg, z, w2, c2, h, small, pick, *more)
        ends.append(out[0])
        if not last:
            h, x, sent = out[:3]
        if cands:
            w, c = out[3:]
    got = [moved(pay, across(r)) for r, pay in enumerate(out[1:], 1)]
    return call(
        collect_kernel,
        jax.ShapeDtypeStruct((1, sections, nodes, width), BF16),
        [SM] + [ANY] * (2 * sections - 1),
        scratch=[pltpu.SemaphoreType.DMA((sections,))],
        out_specs=ANY,
    )(ids, *ends, *got)


def solution(mesh):
    in_specs = (
        P(None, "dom", None),
        P("segment", None, None),
        P("segment", None),
        P("segment", None),
        P("dom", None, None, None),
        P("dom", None),
        P("dom"),
        P("segment", "dom", None, None),
        P("segment", "dom"),
    )
    out_specs = P("segment", None, "dom", None)
    return jax.shard_map(shards, mesh=mesh, in_specs=in_specs, out_specs=out_specs, check_vma=False)
```

```python
import functools

import jax
import jax.numpy as jnp
from jax import lax
from jax.experimental import pallas as pl
from jax.experimental.pallas import tpu as pltpu
from jax.sharding import PartitionSpec as P

F32 = jnp.float32
BF16 = jnp.bfloat16
VMEM_BYTES = 12 * 2**20
LOAD = 0.5
VM = pl.BlockSpec(memory_space=pltpu.VMEM)
SM = pl.BlockSpec(memory_space=pltpu.SMEM)
ANY = pl.BlockSpec(memory_space=pl.ANY)
HBM = pl.BlockSpec(memory_space=pltpu.HBM)


def call(body, outs, in_specs, scratch=(), out_specs=None, flops=0, vmem=VMEM_BYTES):
    if out_specs is None:
        out_specs = jax.tree.map(lambda _: VM, outs)
    inner = body.func if isinstance(body, functools.partial) else body
    return pl.pallas_call(
        body,
        name=inner.__name__,
        out_shape=outs,
        in_specs=in_specs,
        out_specs=out_specs,
        scratch_shapes=scratch,
        compiler_params=pltpu.CompilerParams(vmem_limit_bytes=vmem),
        cost_estimate=pl.CostEstimate(flops=int(flops), bytes_accessed=0, transcendentals=0),
    )


def dot(a, b):
    return jnp.dot(a, b, preferred_element_type=F32)


def aligned(start, unit):
    return start if isinstance(start, int) else pl.multiple_of(start, unit)


def normed(hf, gain):
    meansq = jnp.mean(hf * hf, axis=-1, keepdims=True)
    return (hf * lax.rsqrt(meansq + 1e-05) * gain).astype(BF16)


def stepped(h, z):
    half = 0.5 * z
    return (h.astype(F32) + half + half * jnp.tanh(half)).astype(BF16)


def start_one(choices, dst, sem):
    for condition, source in choices:

        @pl.when(condition)
        def _():
            pltpu.make_async_copy(source, dst, sem).start()

    return pltpu.make_async_copy(choices[0][1], dst, sem)


def source_of(seg, section, half):
    near, far = 1 + half, 2 - half
    via = seg ^ far
    passed = jnp.logical_or(via == 1, via == 2)
    second = jnp.where(passed, seg ^ 3, via)
    return jnp.where(seg == section, 0, jnp.where((seg ^ near) == section, 1, jnp.where(second == section, 2, 3)))


def fetch_half(seg, core, section, half, own, mine, theirs, dst, sem):
    width = dst.shape[1]
    source = source_of(seg, section, half)
    choices = [(source == 0, own.at[pl.ds(half * width, width), :])]
    for here, refs in ((core == half, mine), (core != half, theirs)):
        for i, ref in enumerate(refs):
            choices.append((jnp.logical_and(here, source == i + 1), ref.at[pl.ds(0, width), :]))
    return [start_one(choices, dst, sem)]


def fetch_cross(seg, core, section, own, mine, dst, sems):
    tile = dst.shape[0]
    width = dst.shape[1]
    blocks = own.shape[0]
    source = jnp.where(core == 0, source_of(seg, section, 0), source_of(seg, section, 1))
    for i, ref in enumerate(mine):

        @pl.when(source == i + 1)
        def _():
            for b in range(blocks):
                part = ref.at[pl.ds(width, tile), pl.ds(b * tile, tile)]
                pltpu.make_async_copy(part, dst.at[:, pl.ds(b * tile, tile)], sems.at[b]).start()

    @pl.when(source == 0)
    def _():
        for b in range(blocks):
            pltpu.make_async_copy(own.at[b], dst.at[:, pl.ds(b * tile, tile)], sems.at[b]).start()

    return [pltpu.make_async_copy(own.at[b], dst.at[:, pl.ds(b * tile, tile)], sems.at[b]) for b in range(blocks)]


def fetch_layer(section, step, ids, cands, top, bottom, cross, sems):
    own, own_cross, mine, theirs = cands
    seg, core = ids[0], ids[1]
    return (
        fetch_half(seg, core, section, 0, own.at[step], mine, theirs, top, sems.at[0])
        + fetch_half(seg, core, section, 1, own.at[step], mine, theirs, bottom, sems.at[1])
        + fetch_cross(seg, core, section, own_cross.at[step], mine, cross, sems.at[pl.ds(2, own_cross.shape[1])])
    )


def cands_of(refs):
    n = (len(refs) - 2) // 2
    return refs[0], refs[1], refs[2 : 2 + n], refs[2 + n :]


def first_kernel(dep, ids, cols, counts, feat_ref, tiles_ref, s0, s1, s2, s3, h_ref, adj_ref, x_ref, sent_ref, small_ref, pick_ref, sem):
    nblk, slots, tile, _ = tiles_ref.shape
    nodes, width = h_ref.shape
    seg = ids[0]
    copy = pltpu.make_async_copy(feat_ref.at[seg], h_ref, sem)
    copy.start()
    for r in range(nblk):
        for j in range(nblk):
            total = jnp.zeros((tile, tile), F32)
            for k in range(slots):
                used = jnp.logical_and(k < counts[r], cols[r, k] == j)
                total = total + jnp.where(used, tiles_ref[r, k].astype(F32), 0.0)
            adj_ref[r * tile : (r + 1) * tile, j * tile : (j + 1) * tile] = total.astype(BF16)
    for r, ref in enumerate((s0, s1, s2, s3)):
        small_ref[seg ^ r] = ref[...]
    sections, steps = small_ref.shape[:2]
    bound = small_ref.shape[2] - 2 * width
    for k in range(sections):
        for p in range(steps):
            rows = small_ref[k, p : p + 1, 2 * width :]
            index = lax.broadcasted_iota(jnp.int32, (nodes, bound), 0).astype(F32)
            pick_ref[k, p] = jnp.where(index == rows, 1.0, 0.0).T.astype(BF16)
    copy.wait()
    x = normed(h_ref[...].astype(F32), small_ref[0, 0:1, width : 2 * width])
    x_ref[...] = x
    sent_ref[...] = dot(pick_ref[0, 0], x).astype(BF16)


def payload_kernel(ids, own, cross, *refs):
    outs, sems = refs[:-1], refs[-1]
    copies = []
    for p, out_ref in enumerate(outs):
        width = out_ref.shape[1]
        tile = cross.shape[-1]
        half = own.at[p, pl.ds(pl.multiple_of(ids[1] * width, width), width), :]
        copies.append(pltpu.make_async_copy(half, out_ref.at[pl.ds(0, width), :], sems.at[p, 0]))
        for b in range(cross.shape[1]):
            dst = out_ref.at[pl.ds(width, tile), pl.ds(b * tile, tile)]
            copies.append(pltpu.make_async_copy(cross.at[p, b], dst, sems.at[p, b + 1]))
    for copy in copies:
        copy.start()
    for copy in copies:
        copy.wait()


def select_kernel(wanted, ids, *refs):
    count = len(wanted)
    outs, sources = refs[-count:], refs
    for out_ref, rule in zip(outs, wanted):
        for i, segments in enumerate(rule):
            here = functools.reduce(jnp.logical_or, [ids[0] == s for s in segments])

            @pl.when(here)
            def _():
                out_ref[...] = sources[i][...]


def select(ids, sources, wanted, deps=()):
    shape = jax.ShapeDtypeStruct(sources[0].shape, sources[0].dtype)
    specs = [SM] + [VM] * len(sources) + [ANY] * len(deps)
    return call(functools.partial(select_kernel, wanted), [shape] * len(wanted), specs, vmem=8 * 2**20)(ids, *sources, *deps)


def tie(value, *deps):
    return pl.pallas_call(
        lambda *refs: None,
        name="tie",
        out_shape=jax.ShapeDtypeStruct(value.shape, value.dtype),
        in_specs=[ANY] * (1 + len(deps)),
        out_specs=ANY,
        input_output_aliases={0: 0},
        compiler_params=pltpu.CompilerParams(vmem_limit_bytes=2**20),
    )(value, *deps)


def top_kernel(dep, in_ref, out_ref):
    out_ref[...] = in_ref[: out_ref.shape[0], :]


def load_kernel(section, ids, dep, *refs):
    w_ref, c_ref, sems = refs[-3:]
    width = w_ref.shape[1]
    parts = w_ref.at[pl.ds(0, width), :], w_ref.at[pl.ds(width, width), :]
    for copy in fetch_layer(section, 0, ids, cands_of(refs[:-3]), *parts, c_ref, sems):
        copy.wait()


def edge_kernel(section, x_ref, h_ref, adj_ref, w_ref, c_ref, small_ref, pick_ref, agg_ref, z_ref, cross_ref, h_out):
    width = x_ref.shape[1]
    pick = pick_ref[section, 1]
    x = x_ref[...]
    adj = dot(pick, adj_ref[...]).astype(BF16)
    agg_ref[...] = dot(adj, x)
    xb = dot(pick, x).astype(BF16)
    z_ref[...] = dot(xb, w_ref[:width, :]) + small_ref[section, 0:1, :width]
    tile = c_ref.shape[0]
    cross = jnp.zeros((pick.shape[0], tile), F32)
    for b in range(c_ref.shape[1] // tile):
        lanes = slice(b * tile, (b + 1) * tile)
        cross = cross + dot(pick[:, lanes], c_ref[:, lanes])
    cross_ref[...] = cross.astype(BF16)
    h_out[...] = dot(pick, h_ref[...]).astype(BF16)


def send_kernel(section, recv_ref, agg_ref, z_ref, cross_ref, h_ref, w_ref, small_ref, sent_ref):
    width = h_ref.shape[1]
    agg = (agg_ref[...] + dot(cross_ref[...], recv_ref[...])).astype(BF16)
    z = z_ref[...] + dot(agg, w_ref[width:, :])
    h = stepped(h_ref[...], z)
    sent_ref[...] = normed(h.astype(F32), small_ref[section, 1:2, width : 2 * width])


def remote(c_ref, recv, i, block):
    tile = c_ref.shape[0]
    parts = []
    for b in range(block // tile):
        lanes = pl.ds(aligned(i * block + b * tile, tile), tile)
        parts.append(dot(c_ref[:, lanes], recv))
    return jnp.concatenate(parts, axis=0)


def even_kernel(section, x_ref, h_ref, adj_ref, recv_ref, w_ref, c_ref, small_ref, dep, h_out, x_out):
    nodes, width = x_ref.shape
    block = 256

    def even(i, carry):
        rows = pl.ds(aligned(i * block, block), block)
        agg = dot(adj_ref[rows, :], x_ref[...]) + remote(c_ref, recv_ref[...], i, block)
        z = dot(x_ref[rows, :], w_ref[:width, :]) + small_ref[section, 0:1, :width]
        z = z + dot(agg.astype(BF16), w_ref[width:, :])
        h = stepped(h_ref[rows, :], z)
        h_out[rows, :] = h
        x_out[rows, :] = normed(h.astype(F32), small_ref[section, 1:2, width : 2 * width])
        return carry

    lax.fori_loop(0, nodes // block, even, 0)


def odd_kernel(section, fetch, ids, dep, x_ref, adj_ref, small_ref, *refs):
    if fetch:
        z_out, w2_out, c_out, w_out, next_c_out, w1_ref, sems, next_sems = refs[-8:]
        cands, ahead = refs[: fetch], refs[fetch:-8]
    else:
        z_out, w2_out, c_out, w1_ref, sems = refs[-5:]
        cands = refs[:-5]
    nodes, width = x_ref.shape
    block = 256
    copies = fetch_layer(section, 1, ids, cands_of(cands), w1_ref, w2_out, c_out, sems)
    if fetch:
        parts = w_out.at[pl.ds(0, width), :], w_out.at[pl.ds(width, width), :]
        copies += fetch_layer(section + 1, 0, ids, cands_of(ahead), *parts, next_c_out, next_sems)
    copies[0].wait()
    copies[1].wait()

    def odd(i, carry):
        rows = pl.ds(aligned(i * block, block), block)
        agg = dot(adj_ref[rows, :], x_ref[...]).astype(BF16)
        z = dot(x_ref[rows, :], w1_ref[...]) + small_ref[section, 1:2, :width]
        z_out[rows, :] = z + dot(agg, w2_out[...])
        return carry

    lax.fori_loop(0, nodes // block, odd, 0)
    for copy in copies[2:]:
        copy.wait()


def finish_kernel(section, last, ids, recv_ref, z_ref, w2_ref, c_ref, h_ref, small_ref, pick_ref, *refs):
    nodes, width = h_ref.shape
    block = 256
    if last:
        ends, (h_out, *pays) = refs[:section], refs[section:]
        for k, end_ref in enumerate(ends):
            for r, pay_ref in enumerate(pays, 1):

                @pl.when(ids[0] == k ^ r)
                def _():
                    pay_ref[...] = end_ref[...]
    else:
        h_out, x_out, sent_out = refs
    seen = dot(recv_ref[...], w2_ref[...]).astype(BF16)
    for i in range(nodes // block):
        rows = pl.ds(i * block, block)
        z = z_ref[rows, :] + remote(c_ref, seen, i, block)
        h = stepped(h_ref[rows, :], z)
        h_out[rows, :] = h
        if last:
            for r, pay_ref in enumerate(pays, 1):

                @pl.when(ids[0] == section ^ r)
                def _():
                    pay_ref[rows, :] = h
        else:
            x_out[rows, :] = normed(h.astype(F32), small_ref[section + 1, 0:1, width : 2 * width])
    if not last:
        sent_out[...] = dot(pick_ref[section + 1, 0], x_out[...]).astype(BF16)


def collect_kernel(rounds, ids, *refs):
    out_ref, sems = refs[-2:]
    sections = out_ref.shape[1]
    copies = []
    for i, r in enumerate(rounds):
        dst = out_ref.at[0, ids[0] ^ r]
        if r == 0:
            copies.append(start_one([(ids[0] == k, end) for k, end in enumerate(refs[:sections])], dst, sems.at[i]))
        else:
            copies.append(pltpu.make_async_copy(refs[i if rounds[0] else sections + i - 1], dst, sems.at[i]))
            copies[-1].start()
    for copy in copies:
        copy.wait()


def shards(features, weights, bias, gain, tile_val, tile_col, tile_count, cross_val, send_rows):
    sections = lax.axis_size("segment")
    doms = lax.axis_size("dom")
    seg = lax.axis_index("segment")
    core = lax.axis_index("dom") & 1
    steps, _, width = weights.shape
    nodes = features.shape[1]
    bound = send_rows.shape[1]
    nbits = doms.bit_length() - 1
    ids = jnp.stack([seg, core]).astype(jnp.int32)

    def moved(value, target, sources=range(sections)):
        pairs = []
        for s in sources:
            for d in range(doms):
                t, e = target(s, d)
                pairs.append((s * doms + d, t * doms + e))
        return lax.ppermute(value, ("segment", "dom"), pairs)

    def near(s, d):
        return s ^ (1 + (d & 1)), d

    def far(s, d):
        return s ^ (2 - (d & 1)), d

    def sibling(s, d):
        return s, d ^ 1

    def across(r):
        return lambda s, d: (s ^ r, d)

    def exchange(sent, step):
        bit = step * (nbits - 1) // max(steps - 1, 1)
        return lax.ppermute(sent, "dom", [(i, i ^ 1 << bit) for i in range(doms)])

    mat = jax.ShapeDtypeStruct((nodes, width), BF16)
    mat32 = jax.ShapeDtypeStruct((nodes, width), F32)
    edge = jax.ShapeDtypeStruct((bound, width), BF16)
    edge32 = jax.ShapeDtypeStruct((bound, width), F32)
    half = jax.ShapeDtypeStruct((width, width), BF16)
    both = jax.ShapeDtypeStruct((2 * width, width), BF16)
    load = jax.ShapeDtypeStruct((width + bound, width), BF16)
    picks = jax.ShapeDtypeStruct((sections, steps, bound, nodes), BF16)
    unit = 2 * nodes * width * width
    dmas = pltpu.SemaphoreType.DMA((2 + cross_val.shape[1],))

    own = call(
        payload_kernel,
        [load] * steps,
        [SM, HBM, HBM],
        scratch=[pltpu.SemaphoreType.DMA((steps, 1 + cross_val.shape[1]))],
    )(ids, weights, cross_val)
    small = tie(jnp.concatenate([bias, gain, send_rows.astype(F32)], axis=1), own[0])
    smalls = [small] + [moved(small, across(r)) for r in range(1, sections)]
    inner, outer = (1, 2), (0, 3)
    a0, a1 = [moved(v, near) for v in own]
    (pay,) = select(ids, [a0, own[0]], [(inner, outer)])
    b0 = moved(pay, far)
    h, adj, x, sent, small, pick = call(
        first_kernel,
        (mat, jax.ShapeDtypeStruct((nodes, nodes), BF16), mat, edge, jax.ShapeDtypeStruct((sections,) + small.shape, F32), picks),
        [ANY, SM, SM, SM, HBM, VM] + [VM] * sections,
        scratch=[pltpu.SemaphoreType.DMA],
    )(own[0], ids, tile_col, tile_count, features, tile_val, *smalls)
    recv = exchange(sent, 0)

    (pay,) = select(ids, [a1, own[1]], [(inner, outer)], [pay, sent])
    b1 = moved(pay, far)
    issued = pay
    (pay,) = select(ids, [own[0], a0], [(inner, outer)], [pay])
    c0 = moved(pay, far)
    (pay,) = select(ids, [own[1], a1], [(inner, outer)], [pay])
    c1 = moved(pay, far)
    sa0 = moved(call(top_kernel, half, [ANY, VM])(issued, a0), sibling)
    sb0 = moved(call(top_kernel, half, [ANY, VM])(sent, b0), sibling)
    brought, swapped = [[a0, b0], [a1]], [[sa0, sb0], []]

    def candidates(p):
        return [weights, cross_val, *brought[p], *swapped[p]]

    def loaded(section, dep):
        cands = candidates(0)
        specs = [SM, ANY, HBM, HBM] + [ANY] * (len(cands) - 2)
        kernel = functools.partial(load_kernel, section)
        return call(kernel, (both, edge), specs, scratch=[dmas])(ids, dep, *cands)

    w, c = loaded(0, pay)

    ends = []
    for k in range(sections):
        last = k == sections - 1
        if k > 0:
            recv = exchange(sent, 0)
        if k == 1:
            c1 = tie(c1, x)
            w, c = loaded(1, c1)
        edges = call(
            functools.partial(edge_kernel, k),
            (edge32, edge32, jax.ShapeDtypeStruct((bound, bound), BF16), edge),
            [VM] * 7,
            flops=LOAD * unit / 4,
        )(x, h, adj, w, c, small, pick)
        sent = call(functools.partial(send_kernel, k), edge, [VM] * 7, flops=LOAD * unit / 4)(recv, *edges[:3], edges[3], w, small)
        recv2 = exchange(sent, 1)
        if k == 1:
            brought[1].append(c1)
            swapped[1].append(moved(brought[1][2], sibling))
        h, x = call(functools.partial(even_kernel, k), (mat, mat), [VM] * 7 + [ANY], flops=LOAD * unit)(
            x, h, adj, recv, w, c, small, sent
        )
        if k == 0:
            brought[1] = [tie(a1, sent), tie(b1, sent)]
            swapped[1] = [moved(v, sibling) for v in brought[1]]
        cands = candidates(1)
        ahead = candidates(0) if k in range(1, sections - 1) else []
        fetch = len(cands) if ahead else 0
        specs = [([HBM, HBM] + [ANY] * (len(v) - 2) if v else []) for v in (cands, ahead)]
        z, w2, c2, *loads = call(
            functools.partial(odd_kernel, k, fetch),
            (mat32, half, edge) + ((both, edge) if ahead else ()),
            [SM, ANY] + [VM] * 3 + specs[0] + specs[1],
            scratch=[pltpu.VMEM((width, width), BF16), dmas] + ([dmas] if ahead else []),
            flops=LOAD * unit,
        )(ids, c0 if k == 0 else x, x, adj, small, *cands, *ahead)
        if k == 0:
            brought[0].append(tie(c0, recv2, z))
            swapped[0].append(moved(brought[0][2], sibling))
        out = call(
            functools.partial(finish_kernel, k, last),
            (mat,) * sections if last else (mat, mat, edge),
            [SM] + [VM] * 7 + ([VM] * len(ends) if last else []),
            flops=LOAD * unit,
        )(ids, recv2, z, w2, c2, h, small, pick, *(ends if last else []))
        ends.append(out[0])
        if not last:
            h, x, sent = out
        if ahead:
            w, c = loads
    got = [moved(pay, across(r)) for r, pay in enumerate(out[1:], 1)]
    whole = jax.ShapeDtypeStruct((1, sections, nodes, width), BF16)
    sems = [pltpu.SemaphoreType.DMA((sections,))]
    specs = [SM] + [ANY] * (sections + 1)
    early = call(functools.partial(collect_kernel, (0, 1)), whole, specs, scratch=sems, out_specs=ANY)(ids, *ends, got[0])
    return pl.pallas_call(
        lambda ids, *refs: collect_kernel((2, 3), ids, *refs[:2], *refs[3:]),
        name="collect_kernel",
        out_shape=whole,
        in_specs=[SM] + [ANY] * 3,
        out_specs=ANY,
        scratch_shapes=sems,
        input_output_aliases={3: 0},
        compiler_params=pltpu.CompilerParams(vmem_limit_bytes=2**20),
    )(ids, *got[1:], early)


def solution(mesh):
    in_specs = (
        P(None, "dom", None),
        P("segment", None, None),
        P("segment", None),
        P("segment", None),
        P("dom", None, None, None),
        P("dom", None),
        P("dom"),
        P("segment", "dom", None, None),
        P("segment", "dom"),
    )
    out_specs = P("segment", None, "dom", None)
    return jax.shard_map(shards, mesh=mesh, in_specs=in_specs, out_specs=out_specs, check_vma=False)
```

```python
import functools

import jax
import jax.numpy as jnp
from jax import lax
from jax.experimental import pallas as pl
from jax.experimental.pallas import tpu as pltpu
from jax.sharding import PartitionSpec as P

F32 = jnp.float32
BF16 = jnp.bfloat16
VMEM_BYTES = 12 * 2**20
LOAD = 0.5
VM = pl.BlockSpec(memory_space=pltpu.VMEM)
SM = pl.BlockSpec(memory_space=pltpu.SMEM)
ANY = pl.BlockSpec(memory_space=pl.ANY)
HBM = pl.BlockSpec(memory_space=pltpu.HBM)


def call(body, outs, in_specs, scratch=(), out_specs=None, flops=0, vmem=VMEM_BYTES):
    if out_specs is None:
        out_specs = jax.tree.map(lambda _: VM, outs)
    inner = body.func if isinstance(body, functools.partial) else body
    return pl.pallas_call(
        body,
        name=inner.__name__,
        out_shape=outs,
        in_specs=in_specs,
        out_specs=out_specs,
        scratch_shapes=scratch,
        compiler_params=pltpu.CompilerParams(vmem_limit_bytes=vmem),
        cost_estimate=pl.CostEstimate(flops=int(flops), bytes_accessed=0, transcendentals=0),
    )


def dot(a, b):
    return jnp.dot(a, b, preferred_element_type=F32)


def aligned(start, unit):
    return start if isinstance(start, int) else pl.multiple_of(start, unit)


def normed(hf, gain):
    meansq = jnp.mean(hf * hf, axis=-1, keepdims=True)
    return (hf * lax.rsqrt(meansq + 1e-05) * gain).astype(BF16)


def stepped(h, z):
    half = 0.5 * z
    return (h.astype(F32) + half + half * jnp.tanh(half)).astype(BF16)


def start_one(choices, dst, sem):
    for condition, source in choices:

        @pl.when(condition)
        def _():
            pltpu.make_async_copy(source, dst, sem).start()

    return pltpu.make_async_copy(choices[0][1], dst, sem)


def source_of(seg, section, half):
    near, far = 1 + half, 2 - half
    via = seg ^ far
    passed = jnp.logical_or(via == 1, via == 2)
    second = jnp.where(passed, seg ^ 3, via)
    return jnp.where(seg == section, 0, jnp.where((seg ^ near) == section, 1, jnp.where(second == section, 2, 3)))


def fetch_half(seg, core, section, half, own, mine, theirs, dst, sem):
    width = dst.shape[1]
    source = source_of(seg, section, half)
    choices = [(source == 0, own.at[pl.ds(half * width, width), :])]
    for here, refs in ((core == half, mine), (core != half, theirs)):
        for i, ref in enumerate(refs):
            choices.append((jnp.logical_and(here, source == i + 1), ref.at[pl.ds(0, width), :]))
    return [start_one(choices, dst, sem)]


def fetch_cross(seg, core, section, own, mine, dst, sems):
    tile = dst.shape[0]
    width = dst.shape[1]
    blocks = own.shape[0]
    source = jnp.where(core == 0, source_of(seg, section, 0), source_of(seg, section, 1))
    for i, ref in enumerate(mine):

        @pl.when(source == i + 1)
        def _():
            for b in range(blocks):
                part = ref.at[pl.ds(width, tile), pl.ds(b * tile, tile)]
                pltpu.make_async_copy(part, dst.at[:, pl.ds(b * tile, tile)], sems.at[b]).start()

    @pl.when(source == 0)
    def _():
        for b in range(blocks):
            pltpu.make_async_copy(own.at[b], dst.at[:, pl.ds(b * tile, tile)], sems.at[b]).start()

    return [pltpu.make_async_copy(own.at[b], dst.at[:, pl.ds(b * tile, tile)], sems.at[b]) for b in range(blocks)]


def fetch_layer(section, step, ids, cands, top, bottom, cross, sems):
    own, own_cross, mine, theirs = cands
    seg, core = ids[0], ids[1]
    return (
        fetch_half(seg, core, section, 0, own.at[step], mine, theirs, top, sems.at[0])
        + fetch_half(seg, core, section, 1, own.at[step], mine, theirs, bottom, sems.at[1])
        + fetch_cross(seg, core, section, own_cross.at[step], mine, cross, sems.at[pl.ds(2, own_cross.shape[1])])
    )


def cands_of(refs):
    n = (len(refs) - 2) // 2
    return refs[0], refs[1], refs[2 : 2 + n], refs[2 + n :]


def first_kernel(dep, ids, cols, counts, feat_ref, tiles_ref, s0, s1, s2, s3, h_ref, adj_ref, x_ref, sent_ref, small_ref, pick_ref, sem):
    nblk, slots, tile, _ = tiles_ref.shape
    nodes, width = h_ref.shape
    seg = ids[0]
    copy = pltpu.make_async_copy(feat_ref.at[seg], h_ref, sem)
    copy.start()
    for r in range(nblk):
        for j in range(nblk):
            total = jnp.zeros((tile, tile), F32)
            for k in range(slots):
                used = jnp.logical_and(k < counts[r], cols[r, k] == j)
                total = total + jnp.where(used, tiles_ref[r, k].astype(F32), 0.0)
            adj_ref[r * tile : (r + 1) * tile, j * tile : (j + 1) * tile] = total.astype(BF16)
    for r, ref in enumerate((s0, s1, s2, s3)):
        small_ref[seg ^ r] = ref[...]
    sections, steps = small_ref.shape[:2]
    bound = small_ref.shape[2] - 2 * width
    for k in range(sections):
        for p in range(steps):
            rows = small_ref[k, p : p + 1, 2 * width :]
            index = lax.broadcasted_iota(jnp.int32, (nodes, bound), 0).astype(F32)
            pick_ref[k, p] = jnp.where(index == rows, 1.0, 0.0).T.astype(BF16)
    copy.wait()
    x = normed(h_ref[...].astype(F32), small_ref[0, 0:1, width : 2 * width])
    x_ref[...] = x
    sent_ref[...] = dot(pick_ref[0, 0], x).astype(BF16)


def payload_kernel(own, cross, *refs):
    outs, sems = refs[:-1], refs[-1]
    copies = []
    for p, out_ref in enumerate(outs):
        width = out_ref.shape[1]
        tile = cross.shape[-1]
        copies.append(pltpu.make_async_copy(own.at[p], out_ref.at[pl.ds(0, width), :], sems.at[p, 0]))
        for b in range(cross.shape[1]):
            dst = out_ref.at[pl.ds(width, tile), pl.ds(b * tile, tile)]
            copies.append(pltpu.make_async_copy(cross.at[p, b], dst, sems.at[p, b + 1]))
    for copy in copies:
        copy.start()
    for copy in copies:
        copy.wait()


def select_kernel(wanted, ids, *refs):
    count = len(wanted)
    outs, sources = refs[-count:], refs
    rows = sources[0].shape[0]
    for out_ref, rule in zip(outs, wanted):
        if out_ref.shape[0] > rows:
            out_ref[rows:, :] = jnp.zeros((out_ref.shape[0] - rows, out_ref.shape[1]), out_ref.dtype)
        for i, segments in enumerate(rule):
            here = functools.reduce(jnp.logical_or, [ids[0] == s for s in segments])

            @pl.when(here)
            def _():
                out_ref[:rows, :] = sources[i][...]


def select(ids, sources, wanted, deps=(), extra=0):
    rows, columns = sources[0].shape
    shape = jax.ShapeDtypeStruct((rows + extra, columns), sources[0].dtype)
    specs = [SM] + [VM] * len(sources) + [ANY] * len(deps)
    return call(functools.partial(select_kernel, wanted), [shape] * len(wanted), specs, vmem=8 * 2**20)(ids, *sources, *deps)


def tie(value, *deps):
    return pl.pallas_call(
        lambda *refs: None,
        name="tie",
        out_shape=jax.ShapeDtypeStruct(value.shape, value.dtype),
        in_specs=[ANY] * (1 + len(deps)),
        out_specs=ANY,
        input_output_aliases={0: 0},
        compiler_params=pltpu.CompilerParams(vmem_limit_bytes=2**20),
    )(value, *deps)


def top_kernel(dep, in_ref, out_ref):
    out_ref[...] = in_ref[: out_ref.shape[0], :]


def load_kernel(section, ids, dep, *refs):
    w_ref, c_ref, sems = refs[-3:]
    width = w_ref.shape[1]
    parts = w_ref.at[pl.ds(0, width), :], w_ref.at[pl.ds(width, width), :]
    for copy in fetch_layer(section, 0, ids, cands_of(refs[:-3]), *parts, c_ref, sems):
        copy.wait()


def edge_kernel(section, x_ref, h_ref, adj_ref, w_ref, c_ref, small_ref, pick_ref, agg_ref, z_ref, cross_ref, h_out):
    width = x_ref.shape[1]
    pick = pick_ref[section, 1]
    x = x_ref[...]
    adj = dot(pick, adj_ref[...]).astype(BF16)
    agg_ref[...] = dot(adj, x)
    xb = dot(pick, x).astype(BF16)
    z_ref[...] = dot(xb, w_ref[:width, :]) + small_ref[section, 0:1, :width]
    tile = c_ref.shape[0]
    cross = jnp.zeros((pick.shape[0], tile), F32)
    for b in range(c_ref.shape[1] // tile):
        lanes = slice(b * tile, (b + 1) * tile)
        cross = cross + dot(pick[:, lanes], c_ref[:, lanes])
    cross_ref[...] = cross.astype(BF16)
    h_out[...] = dot(pick, h_ref[...]).astype(BF16)


def send_kernel(section, recv_ref, agg_ref, z_ref, cross_ref, h_ref, w_ref, small_ref, sent_ref):
    width = h_ref.shape[1]
    agg = (agg_ref[...] + dot(cross_ref[...], recv_ref[...])).astype(BF16)
    z = z_ref[...] + dot(agg, w_ref[width:, :])
    h = stepped(h_ref[...], z)
    sent_ref[...] = normed(h.astype(F32), small_ref[section, 1:2, width : 2 * width])


def remote(c_ref, recv, i, block):
    tile = c_ref.shape[0]
    parts = []
    for b in range(block // tile):
        lanes = pl.ds(aligned(i * block + b * tile, tile), tile)
        parts.append(dot(c_ref[:, lanes], recv))
    return jnp.concatenate(parts, axis=0)


def even_kernel(section, x_ref, h_ref, adj_ref, recv_ref, w_ref, c_ref, small_ref, dep, h_out, x_out):
    nodes, width = x_ref.shape
    block = 256

    def even(i, carry):
        rows = pl.ds(aligned(i * block, block), block)
        agg = dot(adj_ref[rows, :], x_ref[...]) + remote(c_ref, recv_ref[...], i, block)
        z = dot(x_ref[rows, :], w_ref[:width, :]) + small_ref[section, 0:1, :width]
        z = z + dot(agg.astype(BF16), w_ref[width:, :])
        h = stepped(h_ref[rows, :], z)
        h_out[rows, :] = h
        x_out[rows, :] = normed(h.astype(F32), small_ref[section, 1:2, width : 2 * width])
        return carry

    lax.fori_loop(0, nodes // block, even, 0)


def odd_kernel(section, fetch, ids, dep, x_ref, adj_ref, small_ref, *refs):
    if fetch:
        z_out, w2_out, c_out, w_out, next_c_out, w1_ref, sems, next_sems = refs[-8:]
        cands, ahead = refs[: fetch], refs[fetch:-8]
    else:
        z_out, w2_out, c_out, w1_ref, sems = refs[-5:]
        cands = refs[:-5]
    nodes, width = x_ref.shape
    block = 256
    copies = fetch_layer(section, 1, ids, cands_of(cands), w1_ref, w2_out, c_out, sems)
    if fetch:
        parts = w_out.at[pl.ds(0, width), :], w_out.at[pl.ds(width, width), :]
        copies += fetch_layer(section + 1, 0, ids, cands_of(ahead), *parts, next_c_out, next_sems)
    copies[0].wait()
    copies[1].wait()

    def odd(i, carry):
        rows = pl.ds(aligned(i * block, block), block)
        agg = dot(adj_ref[rows, :], x_ref[...]).astype(BF16)
        z = dot(x_ref[rows, :], w1_ref[...]) + small_ref[section, 1:2, :width]
        z_out[rows, :] = z + dot(agg, w2_out[...])
        return carry

    lax.fori_loop(0, nodes // block, odd, 0)
    for copy in copies[2:]:
        copy.wait()


def finish_kernel(section, last, ids, recv_ref, z_ref, w2_ref, c_ref, h_ref, small_ref, pick_ref, *refs):
    nodes, width = h_ref.shape
    block = 256
    if last:
        ends, (h_out, *pays) = refs[:section], refs[section:]
        for k, end_ref in enumerate(ends):
            for r, pay_ref in enumerate(pays, 1):

                @pl.when(ids[0] == k ^ r)
                def _():
                    pay_ref[...] = end_ref[...]
    else:
        h_out, x_out, sent_out = refs
    seen = dot(recv_ref[...], w2_ref[...]).astype(BF16)
    for i in range(nodes // block):
        rows = pl.ds(i * block, block)
        z = z_ref[rows, :] + remote(c_ref, seen, i, block)
        h = stepped(h_ref[rows, :], z)
        h_out[rows, :] = h
        if last:
            for r, pay_ref in enumerate(pays, 1):

                @pl.when(ids[0] == section ^ r)
                def _():
                    pay_ref[rows, :] = h
        else:
            x_out[rows, :] = normed(h.astype(F32), small_ref[section + 1, 0:1, width : 2 * width])
    if not last:
        sent_out[...] = dot(pick_ref[section + 1, 0], x_out[...]).astype(BF16)


def collect_early_kernel(ids, *refs):
    across_ref, out_ref, sems = refs[-3:]
    sections = out_ref.shape[1]
    own = start_one([(ids[0] == k, end) for k, end in enumerate(refs[:sections])], out_ref.at[0, ids[0]], sems.at[0])

    @pl.when(ids[0] != sections - 1)
    def _():
        copy = pltpu.make_async_copy(across_ref.at[pl.ds(0, out_ref.shape[2]), :], out_ref.at[0, ids[0] ^ 3], sems.at[1])
        copy.start()
        copy.wait()

    own.wait()


def collect_last_kernel(ids, one_ref, two_ref, three_ref, _, out_ref, sems):
    last = out_ref.shape[1] - 1
    copies = [pltpu.make_async_copy(ref, out_ref.at[0, ids[0] ^ r], sems.at[r]) for r, ref in ((1, one_ref), (2, two_ref))]
    for copy in copies:
        copy.start()

    @pl.when(ids[0] == last)
    def _():
        copy = pltpu.make_async_copy(three_ref, out_ref.at[0, last ^ 3], sems.at[3])
        copy.start()
        copy.wait()

    for copy in copies:
        copy.wait()


def shards(features, weights, bias, gain, tile_val, tile_col, tile_count, cross_val, send_rows):
    sections = lax.axis_size("segment")
    doms = lax.axis_size("dom")
    seg = lax.axis_index("segment")
    core = lax.axis_index("dom") & 1
    steps, _, width = weights.shape
    nodes = features.shape[1]
    bound = send_rows.shape[1]
    nbits = doms.bit_length() - 1
    ids = jnp.stack([seg, core]).astype(jnp.int32)

    def moved(value, target, sources=range(sections)):
        pairs = []
        for s in sources:
            for d in range(doms):
                t, e = target(s, d)
                pairs.append((s * doms + d, t * doms + e))
        return lax.ppermute(value, ("segment", "dom"), pairs)

    def near(s, d):
        return s ^ (1 + (d & 1)), d

    def far(s, d):
        return s ^ (2 - (d & 1)), d

    def sibling(s, d):
        return s, d ^ 1

    def across(r):
        return lambda s, d: (s ^ r, d)

    def exchange(sent, step):
        bit = step * (nbits - 1) // max(steps - 1, 1)
        return lax.ppermute(sent, "dom", [(i, i ^ 1 << bit) for i in range(doms)])

    mat = jax.ShapeDtypeStruct((nodes, width), BF16)
    mat32 = jax.ShapeDtypeStruct((nodes, width), F32)
    edge = jax.ShapeDtypeStruct((bound, width), BF16)
    edge32 = jax.ShapeDtypeStruct((bound, width), F32)
    half = jax.ShapeDtypeStruct((width, width), BF16)
    both = jax.ShapeDtypeStruct((2 * width, width), BF16)
    load = jax.ShapeDtypeStruct((width + bound, width), BF16)
    picks = jax.ShapeDtypeStruct((sections, steps, bound, nodes), BF16)
    unit = 2 * nodes * width * width
    dmas = pltpu.SemaphoreType.DMA((2 + cross_val.shape[1],))

    own = call(
        payload_kernel,
        [load] * steps,
        [ANY, ANY],
        scratch=[pltpu.SemaphoreType.DMA((steps, 1 + cross_val.shape[1]))],
    )(lax.dynamic_slice_in_dim(weights, core * width, width, axis=1), cross_val)
    small = tie(jnp.concatenate([bias, gain, send_rows.astype(F32)], axis=1), own[0])
    smalls = [small] + [moved(small, across(r)) for r in range(1, sections)]
    inner, outer = (1, 2), (0, 3)
    a0, a1 = [moved(v, near) for v in own]
    (pay,) = select(ids, [a0, own[0]], [(inner, outer)])
    b0 = moved(pay, far)
    h, adj, x, sent, small, pick = call(
        first_kernel,
        (mat, jax.ShapeDtypeStruct((nodes, nodes), BF16), mat, edge, jax.ShapeDtypeStruct((sections,) + small.shape, F32), picks),
        [ANY, SM, SM, SM, HBM, VM] + [VM] * sections,
        scratch=[pltpu.SemaphoreType.DMA],
    )(own[0], ids, tile_col, tile_count, features, tile_val, *smalls)
    recv = exchange(sent, 0)

    (pay,) = select(ids, [a1, own[1]], [(inner, outer)], [pay, sent])
    b1 = moved(pay, far)
    issued = pay
    (pay,) = select(ids, [own[0], a0], [(inner, outer)], [pay])
    c0 = moved(pay, far)
    (pay,) = select(ids, [own[1], a1], [(inner, outer)], [pay])
    c1 = moved(pay, far)
    sa0 = moved(call(top_kernel, half, [ANY, VM])(issued, a0), sibling)
    sb0 = moved(call(top_kernel, half, [ANY, VM])(sent, b0), sibling)
    brought, swapped = [[a0, b0], [a1]], [[sa0, sb0], []]

    def candidates(p):
        return [weights, cross_val, *brought[p], *swapped[p]]

    def loaded(section, dep):
        cands = candidates(0)
        specs = [SM, ANY, HBM, HBM] + [ANY] * (len(cands) - 2)
        kernel = functools.partial(load_kernel, section)
        return call(kernel, (both, edge), specs, scratch=[dmas])(ids, dep, *cands)

    w, c = loaded(0, pay)

    ends = []
    last_segment = sections - 1
    for k in range(sections):
        last = k == sections - 1
        if k > 0:
            recv = exchange(sent, 0)
        if k == 1:
            c1 = tie(c1, x)
            w, c = loaded(1, c1)
        edges = call(
            functools.partial(edge_kernel, k),
            (edge32, edge32, jax.ShapeDtypeStruct((bound, bound), BF16), edge),
            [VM] * 7,
            flops=LOAD * unit / 4,
        )(x, h, adj, w, c, small, pick)
        sent = call(functools.partial(send_kernel, k), edge, [VM] * 7, flops=LOAD * unit / 4)(recv, *edges[:3], edges[3], w, small)
        recv2 = exchange(sent, 1)
        if k == 1:
            brought[1].append(c1)
            swapped[1].append(moved(brought[1][2], sibling))
        h, x = call(functools.partial(even_kernel, k), (mat, mat), [VM] * 7 + [ANY], flops=LOAD * unit)(
            x, h, adj, recv, w, c, small, sent
        )
        if k == 0:
            brought[1] = [tie(a1, sent), tie(b1, sent)]
            swapped[1] = [moved(v, sibling) for v in brought[1]]
        cands = candidates(1)
        ahead = candidates(0) if k in range(1, sections - 1) else []
        fetch = len(cands) if ahead else 0
        specs = [([HBM, HBM] + [ANY] * (len(v) - 2) if v else []) for v in (cands, ahead)]
        z, w2, c2, *loads = call(
            functools.partial(odd_kernel, k, fetch),
            (mat32, half, edge) + ((both, edge) if ahead else ()),
            [SM, ANY] + [VM] * 3 + specs[0] + specs[1],
            scratch=[pltpu.VMEM((width, width), BF16), dmas] + ([dmas] if ahead else []),
            flops=(20 if last else LOAD) * unit,
        )(ids, c0 if k == 0 else x, x, adj, small, *cands, *ahead)
        if k == 0:
            brought[0].append(tie(c0, recv2, z))
            swapped[0].append(moved(brought[0][2], sibling))
        if last:
            (pay,) = select(ids, ends, [[(j ^ 3,) for j in range(last_segment)]], [x], extra=16)
            early = moved(pay, across(3), [s for s in range(sections) if s ^ 3 != last_segment])
        out = call(
            functools.partial(finish_kernel, k, last),
            (mat,) * (sections - 1) if last else (mat, mat, edge),
            [SM] + [VM] * 7 + ([VM] * len(ends) if last else []),
            flops=LOAD * unit,
        )(ids, recv2, z, w2, c2, h, small, pick, *(ends if last else []))
        ends.append(out[0])
        if not last:
            h, x, sent = out
        if ahead:
            w, c = loads
    hop = moved(ends[-1], near, [last_segment ^ 3])
    two = moved(out[2], across(2))
    one = moved(out[1], across(1))
    pairs = []
    for d in range(doms):
        s, _ = near(last_segment ^ 3, d)
        pairs.append((s * doms + d, last_segment * doms + d))
    three = lax.ppermute(tie(hop, early), ("segment", "dom"), pairs)
    whole = jax.ShapeDtypeStruct((1, sections, nodes, width), BF16)
    sems = [pltpu.SemaphoreType.DMA((sections,))]
    specs = [SM] + [ANY] * (sections + 1)
    partly = call(collect_early_kernel, whole, specs, scratch=sems, out_specs=ANY)(ids, *ends, early)
    return pl.pallas_call(
        collect_last_kernel,
        name="collect_last_kernel",
        out_shape=whole,
        in_specs=[SM] + [ANY] * 4,
        out_specs=ANY,
        scratch_shapes=sems,
        input_output_aliases={4: 0},
        compiler_params=pltpu.CompilerParams(vmem_limit_bytes=2**20),
    )(ids, one, two, three, partly)


def solution(mesh):
    in_specs = (
        P(None, "dom", None),
        P("segment", None, None),
        P("segment", None),
        P("segment", None),
        P("dom", None, None, None),
        P("dom", None),
        P("dom"),
        P("segment", "dom", None, None),
        P("segment", "dom"),
    )
    out_specs = P("segment", None, "dom", None)
    return jax.shard_map(shards, mesh=mesh, in_specs=in_specs, out_specs=out_specs, check_vma=False)
```

```python
import functools

import jax
import jax.numpy as jnp
from jax import lax
from jax.experimental import pallas as pl
from jax.experimental.pallas import tpu as pltpu
from jax.sharding import PartitionSpec as P

F32 = jnp.float32
BF16 = jnp.bfloat16
VMEM_BYTES = 12 * 2**20
LOAD = 0.5
VM = pl.BlockSpec(memory_space=pltpu.VMEM)
SM = pl.BlockSpec(memory_space=pltpu.SMEM)
ANY = pl.BlockSpec(memory_space=pl.ANY)
HBM = pl.BlockSpec(memory_space=pltpu.HBM)


def call(body, outs, in_specs, scratch=(), out_specs=None, flops=0, vmem=VMEM_BYTES):
    if out_specs is None:
        out_specs = jax.tree.map(lambda _: VM, outs)
    inner = body.func if isinstance(body, functools.partial) else body
    return pl.pallas_call(
        body,
        name=inner.__name__,
        out_shape=outs,
        in_specs=in_specs,
        out_specs=out_specs,
        scratch_shapes=scratch,
        compiler_params=pltpu.CompilerParams(vmem_limit_bytes=vmem),
        cost_estimate=pl.CostEstimate(flops=int(flops), bytes_accessed=0, transcendentals=0),
    )


def dot(a, b):
    return jnp.dot(a, b, preferred_element_type=F32)


def aligned(start, unit):
    return start if isinstance(start, int) else pl.multiple_of(start, unit)


def normed(hf, gain):
    meansq = jnp.mean(hf * hf, axis=-1, keepdims=True)
    return (hf * lax.rsqrt(meansq + 1e-05) * gain).astype(BF16)


def stepped(h, z):
    half = 0.5 * z
    return (h.astype(F32) + half + half * jnp.tanh(half)).astype(BF16)


def start_one(choices, dst, sem):
    for condition, source in choices:

        @pl.when(condition)
        def _():
            pltpu.make_async_copy(source, dst, sem).start()

    return pltpu.make_async_copy(choices[0][1], dst, sem)


def source_of(seg, section, half):
    near, far = 1 + half, 2 - half
    via = seg ^ far
    passed = jnp.logical_or(via == 1, via == 2)
    second = jnp.where(passed, seg ^ 3, via)
    return jnp.where(seg == section, 0, jnp.where((seg ^ near) == section, 1, jnp.where(second == section, 2, 3)))


def fetch_half(seg, core, section, half, own, mine, theirs, dst, sem):
    width = dst.shape[1]
    source = source_of(seg, section, half)
    choices = [(source == 0, own.at[pl.ds(half * width, width), :])]
    for here, refs in ((core == half, mine), (core != half, theirs)):
        for i, ref in enumerate(refs):
            choices.append((jnp.logical_and(here, source == i + 1), ref.at[pl.ds(0, width), :]))
    return [start_one(choices, dst, sem)]


def fetch_cross(seg, core, section, own, mine, dst, sems):
    tile = dst.shape[0]
    width = dst.shape[1]
    blocks = own.shape[0]
    source = jnp.where(core == 0, source_of(seg, section, 0), source_of(seg, section, 1))
    for i, ref in enumerate(mine):

        @pl.when(source == i + 1)
        def _():
            for b in range(blocks):
                part = ref.at[pl.ds(width, tile), pl.ds(b * tile, tile)]
                pltpu.make_async_copy(part, dst.at[:, pl.ds(b * tile, tile)], sems.at[b]).start()

    @pl.when(source == 0)
    def _():
        for b in range(blocks):
            pltpu.make_async_copy(own.at[b], dst.at[:, pl.ds(b * tile, tile)], sems.at[b]).start()

    return [pltpu.make_async_copy(own.at[b], dst.at[:, pl.ds(b * tile, tile)], sems.at[b]) for b in range(blocks)]


def fetch_layer(section, step, ids, cands, top, bottom, cross, sems):
    own, own_cross, mine, theirs = cands
    seg, core = ids[0], ids[1]
    return (
        fetch_half(seg, core, section, 0, own.at[step], mine, theirs, top, sems.at[0])
        + fetch_half(seg, core, section, 1, own.at[step], mine, theirs, bottom, sems.at[1])
        + fetch_cross(seg, core, section, own_cross.at[step], mine, cross, sems.at[pl.ds(2, own_cross.shape[1])])
    )


def cands_of(refs):
    n = (len(refs) - 2) // 2
    return refs[0], refs[1], refs[2 : 2 + n], refs[2 + n :]


def first_kernel(dep, ids, cols, counts, feat_ref, tiles_ref, s0, s1, s2, s3, h_ref, adj_ref, x_ref, sent_ref, small_ref, pick_ref, sem):
    nblk, slots, tile, _ = tiles_ref.shape
    nodes, width = h_ref.shape
    seg = ids[0]
    copy = pltpu.make_async_copy(feat_ref.at[seg], h_ref, sem)
    copy.start()
    for r in range(nblk):
        for j in range(nblk):
            total = jnp.zeros((tile, tile), F32)
            for k in range(slots):
                used = jnp.logical_and(k < counts[r], cols[r, k] == j)
                total = total + jnp.where(used, tiles_ref[r, k].astype(F32), 0.0)
            adj_ref[r * tile : (r + 1) * tile, j * tile : (j + 1) * tile] = total.astype(BF16)
    for r, ref in enumerate((s0, s1, s2, s3)):
        small_ref[seg ^ r] = ref[...]
    sections, steps = small_ref.shape[:2]
    bound = small_ref.shape[2] - 2 * width
    for k in range(sections):
        for p in range(steps):
            rows = small_ref[k, p : p + 1, 2 * width :]
            index = lax.broadcasted_iota(jnp.int32, (nodes, bound), 0).astype(F32)
            pick_ref[k, p] = jnp.where(index == rows, 1.0, 0.0).T.astype(BF16)
    copy.wait()
    x = normed(h_ref[...].astype(F32), small_ref[0, 0:1, width : 2 * width])
    x_ref[...] = x
    sent_ref[...] = dot(pick_ref[0, 0], x).astype(BF16)


def payload_kernel(own, cross, *refs):
    outs, sems = refs[:-1], refs[-1]
    copies = []
    for p, out_ref in enumerate(outs):
        width = out_ref.shape[1]
        tile = cross.shape[-1]
        copies.append(pltpu.make_async_copy(own.at[p], out_ref.at[pl.ds(0, width), :], sems.at[p, 0]))
        for b in range(cross.shape[1]):
            dst = out_ref.at[pl.ds(width, tile), pl.ds(b * tile, tile)]
            copies.append(pltpu.make_async_copy(cross.at[p, b], dst, sems.at[p, b + 1]))
    for copy in copies:
        copy.start()
    for copy in copies:
        copy.wait()


def select_kernel(wanted, ids, *refs):
    count = len(wanted)
    outs, sources = refs[-count:], refs
    rows = sources[0].shape[0]
    for out_ref, rule in zip(outs, wanted):
        if out_ref.shape[0] > rows:
            out_ref[rows:, :] = jnp.zeros((out_ref.shape[0] - rows, out_ref.shape[1]), out_ref.dtype)
        for i, segments in enumerate(rule):
            here = functools.reduce(jnp.logical_or, [ids[0] == s for s in segments])

            @pl.when(here)
            def _():
                out_ref[:rows, :] = sources[i][...]


def select(ids, sources, wanted, deps=(), extra=0):
    rows, columns = sources[0].shape
    shape = jax.ShapeDtypeStruct((rows + extra, columns), sources[0].dtype)
    specs = [SM] + [VM] * len(sources) + [ANY] * len(deps)
    return call(functools.partial(select_kernel, wanted), [shape] * len(wanted), specs, vmem=8 * 2**20)(ids, *sources, *deps)


def tie(value, *deps):
    return pl.pallas_call(
        lambda *refs: None,
        name="tie",
        out_shape=jax.ShapeDtypeStruct(value.shape, value.dtype),
        in_specs=[ANY] * (1 + len(deps)),
        out_specs=ANY,
        input_output_aliases={0: 0},
        compiler_params=pltpu.CompilerParams(vmem_limit_bytes=2**20),
    )(value, *deps)


def top_kernel(dep, in_ref, out_ref):
    out_ref[...] = in_ref[: out_ref.shape[0], :]


def load_kernel(section, ids, dep, *refs):
    w_ref, c_ref, sems = refs[-3:]
    width = w_ref.shape[1]
    parts = w_ref.at[pl.ds(0, width), :], w_ref.at[pl.ds(width, width), :]
    for copy in fetch_layer(section, 0, ids, cands_of(refs[:-3]), *parts, c_ref, sems):
        copy.wait()


def edge_kernel(section, x_ref, h_ref, adj_ref, w_ref, c_ref, small_ref, pick_ref, agg_ref, z_ref, cross_ref, h_out):
    width = x_ref.shape[1]
    pick = pick_ref[section, 1]
    x = x_ref[...]
    adj = dot(pick, adj_ref[...]).astype(BF16)
    agg_ref[...] = dot(adj, x)
    xb = dot(pick, x).astype(BF16)
    z_ref[...] = dot(xb, w_ref[:width, :]) + small_ref[section, 0:1, :width]
    tile = c_ref.shape[0]
    cross = jnp.zeros((pick.shape[0], tile), F32)
    for b in range(c_ref.shape[1] // tile):
        lanes = slice(b * tile, (b + 1) * tile)
        cross = cross + dot(pick[:, lanes], c_ref[:, lanes])
    cross_ref[...] = cross.astype(BF16)
    h_out[...] = dot(pick, h_ref[...]).astype(BF16)


def send_kernel(section, recv_ref, agg_ref, z_ref, cross_ref, h_ref, w_ref, small_ref, sent_ref):
    width = h_ref.shape[1]
    agg = (agg_ref[...] + dot(cross_ref[...], recv_ref[...])).astype(BF16)
    z = z_ref[...] + dot(agg, w_ref[width:, :])
    h = stepped(h_ref[...], z)
    sent_ref[...] = normed(h.astype(F32), small_ref[section, 1:2, width : 2 * width])


def remote(c_ref, recv, i, block):
    tile = c_ref.shape[0]
    parts = []
    for b in range(block // tile):
        lanes = pl.ds(aligned(i * block + b * tile, tile), tile)
        parts.append(dot(c_ref[:, lanes], recv))
    return jnp.concatenate(parts, axis=0)


def even_kernel(section, x_ref, h_ref, adj_ref, recv_ref, w_ref, c_ref, small_ref, dep, h_out, x_out):
    nodes, width = x_ref.shape
    block = 256

    def even(i, carry):
        rows = pl.ds(aligned(i * block, block), block)
        agg = dot(adj_ref[rows, :], x_ref[...]) + remote(c_ref, recv_ref[...], i, block)
        z = dot(x_ref[rows, :], w_ref[:width, :]) + small_ref[section, 0:1, :width]
        z = z + dot(agg.astype(BF16), w_ref[width:, :])
        h = stepped(h_ref[rows, :], z)
        h_out[rows, :] = h
        x_out[rows, :] = normed(h.astype(F32), small_ref[section, 1:2, width : 2 * width])
        return carry

    lax.fori_loop(0, nodes // block, even, 0)


def odd_kernel(section, fetch, ids, dep, x_ref, adj_ref, small_ref, *refs):
    if fetch:
        z_out, w2_out, c_out, w_out, next_c_out, w1_ref, sems, next_sems = refs[-8:]
        cands, ahead = refs[: fetch], refs[fetch:-8]
    else:
        z_out, w2_out, c_out, w1_ref, sems = refs[-5:]
        cands = refs[:-5]
    nodes, width = x_ref.shape
    block = 256
    copies = fetch_layer(section, 1, ids, cands_of(cands), w1_ref, w2_out, c_out, sems)
    if fetch:
        parts = w_out.at[pl.ds(0, width), :], w_out.at[pl.ds(width, width), :]
        copies += fetch_layer(section + 1, 0, ids, cands_of(ahead), *parts, next_c_out, next_sems)
    copies[0].wait()
    copies[1].wait()

    def odd(i, carry):
        rows = pl.ds(aligned(i * block, block), block)
        agg = dot(adj_ref[rows, :], x_ref[...]).astype(BF16)
        z = dot(x_ref[rows, :], w1_ref[...]) + small_ref[section, 1:2, :width]
        z_out[rows, :] = z + dot(agg, w2_out[...])
        return carry

    lax.fori_loop(0, nodes // block, odd, 0)
    for copy in copies[2:]:
        copy.wait()


def finish_kernel(section, last, ids, recv_ref, z_ref, w2_ref, c_ref, h_ref, small_ref, pick_ref, *refs):
    nodes, width = h_ref.shape
    block = 256
    if last:
        ends, (h_out, *pays) = refs[:section], refs[section:]
        for k, end_ref in enumerate(ends):
            for r, pay_ref in enumerate(pays, 1):

                @pl.when(ids[0] == k ^ r)
                def _():
                    pay_ref[...] = end_ref[...]
    else:
        h_out, x_out, sent_out = refs
    seen = dot(recv_ref[...], w2_ref[...]).astype(BF16)
    for i in range(nodes // block):
        rows = pl.ds(i * block, block)
        z = z_ref[rows, :] + remote(c_ref, seen, i, block)
        h = stepped(h_ref[rows, :], z)
        h_out[rows, :] = h
        if last:
            for r, pay_ref in enumerate(pays, 1):

                @pl.when(ids[0] == section ^ r)
                def _():
                    pay_ref[rows, :] = h
        else:
            x_out[rows, :] = normed(h.astype(F32), small_ref[section + 1, 0:1, width : 2 * width])
    if not last:
        sent_out[...] = dot(pick_ref[section + 1, 0], x_out[...]).astype(BF16)


def collect_early_kernel(ids, *refs):
    early_ref, later_ref, out_ref, sems = refs[-4:]
    sections = out_ref.shape[1]
    own = start_one([(ids[0] == k, end) for k, end in enumerate(refs[:sections])], out_ref.at[0, ids[0]], sems.at[0])

    @pl.when(ids[0] != sections - 1)
    def _():
        rows = pl.ds(0, out_ref.shape[2])
        choices = [(ids[1] == 0, early_ref.at[rows, :]), (ids[1] != 0, later_ref.at[rows, :])]
        start_one(choices, out_ref.at[0, ids[0] ^ 3], sems.at[1]).wait()

    own.wait()


def collect_last_kernel(ids, one_ref, two_ref, three_ref, _, out_ref, sems):
    last = out_ref.shape[1] - 1
    copies = [pltpu.make_async_copy(ref, out_ref.at[0, ids[0] ^ r], sems.at[r]) for r, ref in ((1, one_ref), (2, two_ref))]
    for copy in copies:
        copy.start()

    @pl.when(ids[0] == last)
    def _():
        copy = pltpu.make_async_copy(three_ref, out_ref.at[0, last ^ 3], sems.at[3])
        copy.start()
        copy.wait()

    for copy in copies:
        copy.wait()


def shards(features, weights, bias, gain, tile_val, tile_col, tile_count, cross_val, send_rows):
    sections = lax.axis_size("segment")
    doms = lax.axis_size("dom")
    seg = lax.axis_index("segment")
    core = lax.axis_index("dom") & 1
    steps, _, width = weights.shape
    nodes = features.shape[1]
    bound = send_rows.shape[1]
    nbits = doms.bit_length() - 1
    ids = jnp.stack([seg, core]).astype(jnp.int32)

    def moved(value, target, sources=range(sections)):
        pairs = []
        for s in sources:
            for d in range(doms):
                t, e = target(s, d)
                pairs.append((s * doms + d, t * doms + e))
        return lax.ppermute(value, ("segment", "dom"), pairs)

    def near(s, d):
        return s ^ (1 + (d & 1)), d

    def far(s, d):
        return s ^ (2 - (d & 1)), d

    def sibling(s, d):
        return s, d ^ 1

    def across(r):
        return lambda s, d: (s ^ r, d)

    def exchange(sent, step):
        bit = step * (nbits - 1) // max(steps - 1, 1)
        return lax.ppermute(sent, "dom", [(i, i ^ 1 << bit) for i in range(doms)])

    mat = jax.ShapeDtypeStruct((nodes, width), BF16)
    mat32 = jax.ShapeDtypeStruct((nodes, width), F32)
    edge = jax.ShapeDtypeStruct((bound, width), BF16)
    edge32 = jax.ShapeDtypeStruct((bound, width), F32)
    half = jax.ShapeDtypeStruct((width, width), BF16)
    both = jax.ShapeDtypeStruct((2 * width, width), BF16)
    load = jax.ShapeDtypeStruct((width + bound, width), BF16)
    picks = jax.ShapeDtypeStruct((sections, steps, bound, nodes), BF16)
    unit = 2 * nodes * width * width
    dmas = pltpu.SemaphoreType.DMA((2 + cross_val.shape[1],))

    own = call(
        payload_kernel,
        [load] * steps,
        [ANY, ANY],
        scratch=[pltpu.SemaphoreType.DMA((steps, 1 + cross_val.shape[1]))],
    )(lax.dynamic_slice_in_dim(weights, core * width, width, axis=1), cross_val)
    small = tie(jnp.concatenate([bias, gain, send_rows.astype(F32)], axis=1), own[0])
    smalls = [small] + [moved(small, across(r)) for r in range(1, sections)]
    inner, outer = (1, 2), (0, 3)
    a0, a1 = [moved(v, near) for v in own]
    (pay,) = select(ids, [a0, own[0]], [(inner, outer)])
    b0 = moved(pay, far)
    h, adj, x, sent, small, pick = call(
        first_kernel,
        (mat, jax.ShapeDtypeStruct((nodes, nodes), BF16), mat, edge, jax.ShapeDtypeStruct((sections,) + small.shape, F32), picks),
        [ANY, SM, SM, SM, HBM, VM] + [VM] * sections,
        scratch=[pltpu.SemaphoreType.DMA],
    )(own[0], ids, tile_col, tile_count, features, tile_val, *smalls)
    recv = exchange(sent, 0)

    (pay,) = select(ids, [a1, own[1]], [(inner, outer)], [pay, sent])
    b1 = moved(pay, far)
    issued = pay
    (pay,) = select(ids, [own[0], a0], [(inner, outer)], [pay])
    c0 = moved(pay, far)
    (pay,) = select(ids, [own[1], a1], [(inner, outer)], [pay])
    c1 = moved(pay, far)
    sa0 = moved(call(top_kernel, half, [ANY, VM])(issued, a0), sibling)
    sb0 = moved(call(top_kernel, half, [ANY, VM])(sent, b0), sibling)
    brought, swapped = [[a0, b0], [a1]], [[sa0, sb0], []]

    def candidates(p):
        return [weights, cross_val, *brought[p], *swapped[p]]

    def loaded(section, dep):
        cands = candidates(0)
        specs = [SM, ANY, HBM, HBM] + [ANY] * (len(cands) - 2)
        kernel = functools.partial(load_kernel, section)
        return call(kernel, (both, edge), specs, scratch=[dmas])(ids, dep, *cands)

    w, c = loaded(0, pay)

    ends = []
    last_segment = sections - 1
    for k in range(sections):
        last = k == sections - 1
        if k > 0:
            recv = exchange(sent, 0)
        if k == 1:
            c1 = tie(c1, x)
            w, c = loaded(1, c1)
        edges = call(
            functools.partial(edge_kernel, k),
            (edge32, edge32, jax.ShapeDtypeStruct((bound, bound), BF16), edge),
            [VM] * 7,
            flops=LOAD * unit / 4,
        )(x, h, adj, w, c, small, pick)
        sent = call(functools.partial(send_kernel, k), edge, [VM] * 7, flops=LOAD * unit / 4)(recv, *edges[:3], edges[3], w, small)
        recv2 = exchange(sent, 1)
        if k == 1:
            brought[1].append(c1)
            swapped[1].append(moved(brought[1][2], sibling))
        h, x = call(functools.partial(even_kernel, k), (mat, mat), [VM] * 7 + [ANY], flops=LOAD * unit)(
            x, h, adj, recv, w, c, small, sent
        )
        if k == 0:
            brought[1] = [tie(a1, sent), tie(b1, sent)]
            swapped[1] = [moved(v, sibling) for v in brought[1]]
        cands = candidates(1)
        ahead = candidates(0) if k in range(1, sections - 1) else []
        fetch = len(cands) if ahead else 0
        specs = [([HBM, HBM] + [ANY] * (len(v) - 2) if v else []) for v in (cands, ahead)]
        z, w2, c2, *loads = call(
            functools.partial(odd_kernel, k, fetch),
            (mat32, half, edge) + ((both, edge) if ahead else ()),
            [SM, ANY] + [VM] * 3 + specs[0] + specs[1],
            scratch=[pltpu.VMEM((width, width), BF16), dmas] + ([dmas] if ahead else []),
            flops=(20 if last else LOAD) * unit,
        )(ids, c0 if k == 0 else x, x, adj, small, *cands, *ahead)
        if k == 0:
            brought[0].append(tie(c0, recv2, z))
            swapped[0].append(moved(brought[0][2], sibling))
        if last:
            (pay,) = select(ids, ends, [[(j ^ 3,) for j in range(last_segment)]], [x], extra=16)
            others = [s for s in range(sections) if s ^ 3 != last_segment]
            early = moved(pay, lambda s, d: (s ^ (2 if d & 1 else 3), d), others)
        out = call(
            functools.partial(finish_kernel, k, last),
            (mat,) * (sections - 1) if last else (mat, mat, edge),
            [SM] + [VM] * 7 + ([VM] * len(ends) if last else []),
            flops=LOAD * unit,
        )(ids, recv2, z, w2, c2, h, small, pick, *(ends if last else []))
        ends.append(out[0])
        if not last:
            h, x, sent = out
        if ahead:
            w, c = loads
    hop = moved(ends[-1], near, [last_segment ^ 3])
    two = moved(out[2], across(2))
    one = moved(out[1], across(1))
    def onward(value, between, sources, parity=None):
        pairs = []
        for s in sources:
            for d in range(doms):
                if parity is None or d & 1 == parity:
                    pairs.append((between(s, d) * doms + d, (s ^ 3) * doms + d))
        return lax.ppermute(value, ("segment", "dom"), pairs)

    three = onward(tie(hop, early), lambda s, d: near(s, d)[0], [last_segment ^ 3])
    later = onward(early, lambda s, d: s ^ 2, others, 1)
    whole = jax.ShapeDtypeStruct((1, sections, nodes, width), BF16)
    sems = [pltpu.SemaphoreType.DMA((sections,))]
    specs = [SM] + [ANY] * (sections + 2)
    partly = call(collect_early_kernel, whole, specs, scratch=sems, out_specs=ANY)(ids, *ends, early, later)
    return pl.pallas_call(
        collect_last_kernel,
        name="collect_last_kernel",
        out_shape=whole,
        in_specs=[SM] + [ANY] * 4,
        out_specs=ANY,
        scratch_shapes=sems,
        input_output_aliases={4: 0},
        compiler_params=pltpu.CompilerParams(vmem_limit_bytes=2**20),
    )(ids, one, two, three, partly)


def solution(mesh):
    in_specs = (
        P(None, "dom", None),
        P("segment", None, None),
        P("segment", None),
        P("segment", None),
        P("dom", None, None, None),
        P("dom", None),
        P("dom"),
        P("segment", "dom", None, None),
        P("segment", "dom"),
    )
    out_specs = P("segment", None, "dom", None)
    return jax.shard_map(shards, mesh=mesh, in_specs=in_specs, out_specs=out_specs, check_vma=False)
```

```python
import functools

import jax
import jax.numpy as jnp
from jax import lax
from jax.experimental import pallas as pl
from jax.experimental.pallas import tpu as pltpu
from jax.sharding import PartitionSpec as P

F32 = jnp.float32
BF16 = jnp.bfloat16
VMEM_BYTES = 12 * 2**20
LOAD = 0.5
VM = pl.BlockSpec(memory_space=pltpu.VMEM)
SM = pl.BlockSpec(memory_space=pltpu.SMEM)
ANY = pl.BlockSpec(memory_space=pl.ANY)
HBM = pl.BlockSpec(memory_space=pltpu.HBM)


def call(body, outs, in_specs, scratch=(), out_specs=None, flops=0, vmem=VMEM_BYTES):
    if out_specs is None:
        out_specs = jax.tree.map(lambda _: VM, outs)
    inner = body.func if isinstance(body, functools.partial) else body
    return pl.pallas_call(
        body,
        name=inner.__name__,
        out_shape=outs,
        in_specs=in_specs,
        out_specs=out_specs,
        scratch_shapes=scratch,
        compiler_params=pltpu.CompilerParams(vmem_limit_bytes=vmem),
        cost_estimate=pl.CostEstimate(flops=int(flops), bytes_accessed=0, transcendentals=0),
    )


def dot(a, b):
    return jnp.dot(a, b, preferred_element_type=F32)


def aligned(start, unit):
    return start if isinstance(start, int) else pl.multiple_of(start, unit)


def normed(hf, gain):
    meansq = jnp.mean(hf * hf, axis=-1, keepdims=True)
    return (hf * lax.rsqrt(meansq + 1e-05) * gain).astype(BF16)


def stepped(h, z):
    half = 0.5 * z
    return (h.astype(F32) + half + half * jnp.tanh(half)).astype(BF16)


def start_one(choices, dst, sem):
    for condition, source in choices:

        @pl.when(condition)
        def _():
            pltpu.make_async_copy(source, dst, sem).start()

    return pltpu.make_async_copy(choices[0][1], dst, sem)


def source_of(seg, section, half):
    near, far = 1 + half, 2 - half
    via = seg ^ far
    passed = jnp.logical_or(via == 1, via == 2)
    second = jnp.where(passed, seg ^ 3, via)
    return jnp.where(seg == section, 0, jnp.where((seg ^ near) == section, 1, jnp.where(second == section, 2, 3)))


def fetch_half(seg, core, section, half, own, mine, theirs, dst, sem):
    width = dst.shape[1]
    source = source_of(seg, section, half)
    choices = [(source == 0, own.at[pl.ds(half * width, width), :])]
    for here, refs in ((core == half, mine), (core != half, theirs)):
        for i, ref in enumerate(refs):
            choices.append((jnp.logical_and(here, source == i + 1), ref.at[pl.ds(0, width), :]))
    return [start_one(choices, dst, sem)]


def fetch_cross(seg, core, section, own, mine, dst, sems):
    tile = dst.shape[0]
    width = dst.shape[1]
    blocks = own.shape[0]
    source = jnp.where(core == 0, source_of(seg, section, 0), source_of(seg, section, 1))
    for i, ref in enumerate(mine):

        @pl.when(source == i + 1)
        def _():
            for b in range(blocks):
                part = ref.at[pl.ds(width, tile), pl.ds(b * tile, tile)]
                pltpu.make_async_copy(part, dst.at[:, pl.ds(b * tile, tile)], sems.at[b]).start()

    @pl.when(source == 0)
    def _():
        for b in range(blocks):
            pltpu.make_async_copy(own.at[b], dst.at[:, pl.ds(b * tile, tile)], sems.at[b]).start()

    return [pltpu.make_async_copy(own.at[b], dst.at[:, pl.ds(b * tile, tile)], sems.at[b]) for b in range(blocks)]


def fetch_layer(section, step, ids, cands, top, bottom, cross, sems):
    own, own_cross, mine, theirs = cands
    seg, core = ids[0], ids[1]
    return (
        fetch_half(seg, core, section, 0, own.at[step], mine, theirs, top, sems.at[0])
        + fetch_half(seg, core, section, 1, own.at[step], mine, theirs, bottom, sems.at[1])
        + fetch_cross(seg, core, section, own_cross.at[step], mine, cross, sems.at[pl.ds(2, own_cross.shape[1])])
    )


def cands_of(refs):
    n = (len(refs) - 2) // 2
    return refs[0], refs[1], refs[2 : 2 + n], refs[2 + n :]


def first_kernel(dep, ids, cols, counts, feat_ref, tiles_ref, s0, s1, s2, s3, h_ref, adj_ref, x_ref, sent_ref, small_ref, pick_ref, sem):
    nblk, slots, tile, _ = tiles_ref.shape
    nodes, width = h_ref.shape
    seg = ids[0]
    copy = pltpu.make_async_copy(feat_ref.at[seg], h_ref, sem)
    copy.start()
    for r in range(nblk):
        for j in range(nblk):
            total = jnp.zeros((tile, tile), F32)
            for k in range(slots):
                used = jnp.logical_and(k < counts[r], cols[r, k] == j)
                total = total + jnp.where(used, tiles_ref[r, k].astype(F32), 0.0)
            adj_ref[r * tile : (r + 1) * tile, j * tile : (j + 1) * tile] = total.astype(BF16)
    for r, ref in enumerate((s0, s1, s2, s3)):
        small_ref[seg ^ r] = ref[...]
    sections, steps = small_ref.shape[:2]
    bound = small_ref.shape[2] - 2 * width
    for k in range(sections):
        for p in range(steps):
            rows = small_ref[k, p : p + 1, 2 * width :]
            index = lax.broadcasted_iota(jnp.int32, (nodes, bound), 0).astype(F32)
            pick_ref[k, p] = jnp.where(index == rows, 1.0, 0.0).T.astype(BF16)
    copy.wait()
    x = normed(h_ref[...].astype(F32), small_ref[0, 0:1, width : 2 * width])
    x_ref[...] = x
    sent_ref[...] = dot(pick_ref[0, 0], x).astype(BF16)


def payload_kernel(own, cross, *refs):
    outs, sems = refs[:-1], refs[-1]
    copies = []
    for p, out_ref in enumerate(outs):
        width = out_ref.shape[1]
        tile = cross.shape[-1]
        copies.append(pltpu.make_async_copy(own.at[p], out_ref.at[pl.ds(0, width), :], sems.at[p, 0]))
        for b in range(cross.shape[1]):
            dst = out_ref.at[pl.ds(width, tile), pl.ds(b * tile, tile)]
            copies.append(pltpu.make_async_copy(cross.at[p, b], dst, sems.at[p, b + 1]))
    for copy in copies:
        copy.start()
    for copy in copies:
        copy.wait()


def select_kernel(wanted, ids, *refs):
    count = len(wanted)
    outs, sources = refs[-count:], refs
    rows = sources[0].shape[0]
    for out_ref, rule in zip(outs, wanted):
        if out_ref.shape[0] > rows:
            out_ref[rows:, :] = jnp.zeros((out_ref.shape[0] - rows, out_ref.shape[1]), out_ref.dtype)
        for i, segments in enumerate(rule):
            here = functools.reduce(jnp.logical_or, [ids[0] == s for s in segments])

            @pl.when(here)
            def _():
                out_ref[:rows, :] = sources[i][...]


def select(ids, sources, wanted, deps=(), extra=0):
    rows, columns = sources[0].shape
    shape = jax.ShapeDtypeStruct((rows + extra, columns), sources[0].dtype)
    specs = [SM] + [VM] * len(sources) + [ANY] * len(deps)
    return call(functools.partial(select_kernel, wanted), [shape] * len(wanted), specs, vmem=8 * 2**20)(ids, *sources, *deps)


def tie(value, *deps):
    return pl.pallas_call(
        lambda *refs: None,
        name="tie",
        out_shape=jax.ShapeDtypeStruct(value.shape, value.dtype),
        in_specs=[ANY] * (1 + len(deps)),
        out_specs=ANY,
        input_output_aliases={0: 0},
        compiler_params=pltpu.CompilerParams(vmem_limit_bytes=2**20),
    )(value, *deps)


def top_kernel(dep, in_ref, out_ref):
    out_ref[...] = in_ref[: out_ref.shape[0], :]


def load_kernel(section, ids, dep, *refs):
    w_ref, c_ref, sems = refs[-3:]
    width = w_ref.shape[1]
    parts = w_ref.at[pl.ds(0, width), :], w_ref.at[pl.ds(width, width), :]
    for copy in fetch_layer(section, 0, ids, cands_of(refs[:-3]), *parts, c_ref, sems):
        copy.wait()


def edge_kernel(section, x_ref, h_ref, adj_ref, w_ref, c_ref, small_ref, pick_ref, agg_ref, z_ref, cross_ref, h_out):
    width = x_ref.shape[1]
    pick = pick_ref[section, 1]
    x = x_ref[...]
    adj = dot(pick, adj_ref[...]).astype(BF16)
    agg_ref[...] = dot(adj, x)
    xb = dot(pick, x).astype(BF16)
    z_ref[...] = dot(xb, w_ref[:width, :]) + small_ref[section, 0:1, :width]
    tile = c_ref.shape[0]
    cross = jnp.zeros((pick.shape[0], tile), F32)
    for b in range(c_ref.shape[1] // tile):
        lanes = slice(b * tile, (b + 1) * tile)
        cross = cross + dot(pick[:, lanes], c_ref[:, lanes])
    cross_ref[...] = cross.astype(BF16)
    h_out[...] = dot(pick, h_ref[...]).astype(BF16)


def send_kernel(section, recv_ref, agg_ref, z_ref, cross_ref, h_ref, w_ref, small_ref, sent_ref):
    width = h_ref.shape[1]
    agg = (agg_ref[...] + dot(cross_ref[...], recv_ref[...])).astype(BF16)
    z = z_ref[...] + dot(agg, w_ref[width:, :])
    h = stepped(h_ref[...], z)
    sent_ref[...] = normed(h.astype(F32), small_ref[section, 1:2, width : 2 * width])


def remote(c_ref, recv, i, block):
    tile = c_ref.shape[0]
    parts = []
    for b in range(block // tile):
        lanes = pl.ds(aligned(i * block + b * tile, tile), tile)
        parts.append(dot(c_ref[:, lanes], recv))
    return jnp.concatenate(parts, axis=0)


def even_kernel(section, x_ref, h_ref, adj_ref, recv_ref, w_ref, c_ref, small_ref, dep, h_out, x_out):
    nodes, width = x_ref.shape
    block = 256

    def even(i, carry):
        rows = pl.ds(aligned(i * block, block), block)
        agg = dot(adj_ref[rows, :], x_ref[...]) + remote(c_ref, recv_ref[...], i, block)
        z = dot(x_ref[rows, :], w_ref[:width, :]) + small_ref[section, 0:1, :width]
        z = z + dot(agg.astype(BF16), w_ref[width:, :])
        h = stepped(h_ref[rows, :], z)
        h_out[rows, :] = h
        x_out[rows, :] = normed(h.astype(F32), small_ref[section, 1:2, width : 2 * width])
        return carry

    lax.fori_loop(0, nodes // block, even, 0)


def odd_kernel(section, fetch, ids, dep, x_ref, adj_ref, small_ref, *refs):
    if fetch:
        z_out, w2_out, c_out, w_out, next_c_out, w1_ref, sems, next_sems = refs[-8:]
        cands, ahead = refs[: fetch], refs[fetch:-8]
    else:
        z_out, w2_out, c_out, w1_ref, sems = refs[-5:]
        cands = refs[:-5]
    nodes, width = x_ref.shape
    block = 256
    copies = fetch_layer(section, 1, ids, cands_of(cands), w1_ref, w2_out, c_out, sems)
    if fetch:
        parts = w_out.at[pl.ds(0, width), :], w_out.at[pl.ds(width, width), :]
        copies += fetch_layer(section + 1, 0, ids, cands_of(ahead), *parts, next_c_out, next_sems)
    copies[0].wait()
    copies[1].wait()

    def odd(i, carry):
        rows = pl.ds(aligned(i * block, block), block)
        agg = dot(adj_ref[rows, :], x_ref[...]).astype(BF16)
        z = dot(x_ref[rows, :], w1_ref[...]) + small_ref[section, 1:2, :width]
        z_out[rows, :] = z + dot(agg, w2_out[...])
        return carry

    lax.fori_loop(0, nodes // block, odd, 0)
    for copy in copies[2:]:
        copy.wait()


def finish_kernel(section, last, ids, recv_ref, z_ref, w2_ref, c_ref, h_ref, small_ref, pick_ref, *refs):
    nodes, width = h_ref.shape
    block = 256
    if last:
        ends, (h_out, *pays) = refs[:section], refs[section:]
        for k, end_ref in enumerate(ends):
            for r, pay_ref in enumerate(pays, 1):

                @pl.when(ids[0] == k ^ r)
                def _():
                    pay_ref[:nodes, :] = end_ref[...]

        for pay_ref in pays:
            pay_ref[nodes:, :] = jnp.zeros((pay_ref.shape[0] - nodes, width), BF16)
    else:
        h_out, x_out, sent_out = refs
    seen = dot(recv_ref[...], w2_ref[...]).astype(BF16)
    for i in range(nodes // block):
        rows = pl.ds(i * block, block)
        z = z_ref[rows, :] + remote(c_ref, seen, i, block)
        h = stepped(h_ref[rows, :], z)
        h_out[rows, :] = h
        if last:
            for r, pay_ref in enumerate(pays, 1):

                @pl.when(ids[0] == section ^ r)
                def _():
                    pay_ref[rows, :] = h
        else:
            x_out[rows, :] = normed(h.astype(F32), small_ref[section + 1, 0:1, width : 2 * width])
    if not last:
        sent_out[...] = dot(pick_ref[section + 1, 0], x_out[...]).astype(BF16)


def collect_early_kernel(ids, *refs):
    out_ref, sem = refs[-2:]
    start_one([(ids[0] == k, end) for k, end in enumerate(refs[:-2])], out_ref.at[0, ids[0]], sem).wait()


def collect_last_kernel(ids, one_ref, two_ref, three_ref, early_ref, later_ref, _, out_ref, sems):
    last = out_ref.shape[1] - 1
    rows = pl.ds(0, out_ref.shape[2])
    copies = [
        pltpu.make_async_copy(ref.at[rows, :], out_ref.at[0, ids[0] ^ r], sems.at[r]) for r, ref in ((1, one_ref), (2, two_ref))
    ]
    for copy in copies:
        copy.start()
    choices = [
        (ids[0] == last, three_ref),
        (jnp.logical_and(ids[0] != last, ids[1] == 0), early_ref.at[rows, :]),
        (jnp.logical_and(ids[0] != last, ids[1] != 0), later_ref.at[rows, :]),
    ]
    copies.append(start_one(choices, out_ref.at[0, ids[0] ^ 3], sems.at[3]))
    for copy in copies:
        copy.wait()


def shards(features, weights, bias, gain, tile_val, tile_col, tile_count, cross_val, send_rows):
    sections = lax.axis_size("segment")
    doms = lax.axis_size("dom")
    seg = lax.axis_index("segment")
    core = lax.axis_index("dom") & 1
    steps, _, width = weights.shape
    nodes = features.shape[1]
    bound = send_rows.shape[1]
    nbits = doms.bit_length() - 1
    ids = jnp.stack([seg, core]).astype(jnp.int32)

    def moved(value, target, sources=range(sections)):
        pairs = []
        for s in sources:
            for d in range(doms):
                t, e = target(s, d)
                pairs.append((s * doms + d, t * doms + e))
        return lax.ppermute(value, ("segment", "dom"), pairs)

    def near(s, d):
        return s ^ (1 + (d & 1)), d

    def far(s, d):
        return s ^ (2 - (d & 1)), d

    def sibling(s, d):
        return s, d ^ 1

    def across(r):
        return lambda s, d: (s ^ r, d)

    def exchange(sent, step):
        bit = step * (nbits - 1) // max(steps - 1, 1)
        return lax.ppermute(sent, "dom", [(i, i ^ 1 << bit) for i in range(doms)])

    mat = jax.ShapeDtypeStruct((nodes, width), BF16)
    mat32 = jax.ShapeDtypeStruct((nodes, width), F32)
    tall = jax.ShapeDtypeStruct((nodes + 32, width), BF16)
    edge = jax.ShapeDtypeStruct((bound, width), BF16)
    edge32 = jax.ShapeDtypeStruct((bound, width), F32)
    half = jax.ShapeDtypeStruct((width, width), BF16)
    both = jax.ShapeDtypeStruct((2 * width, width), BF16)
    load = jax.ShapeDtypeStruct((width + bound, width), BF16)
    picks = jax.ShapeDtypeStruct((sections, steps, bound, nodes), BF16)
    unit = 2 * nodes * width * width
    dmas = pltpu.SemaphoreType.DMA((2 + cross_val.shape[1],))

    own = call(
        payload_kernel,
        [load] * steps,
        [ANY, ANY],
        scratch=[pltpu.SemaphoreType.DMA((steps, 1 + cross_val.shape[1]))],
    )(lax.dynamic_slice_in_dim(weights, core * width, width, axis=1), cross_val)
    small = tie(jnp.concatenate([bias, gain, send_rows.astype(F32)], axis=1), own[0])
    smalls = [small] + [moved(small, across(r)) for r in range(1, sections)]
    inner, outer = (1, 2), (0, 3)
    a0, a1 = [moved(v, near) for v in own]
    (pay,) = select(ids, [a0, own[0]], [(inner, outer)])
    b0 = moved(pay, far)
    h, adj, x, sent, small, pick = call(
        first_kernel,
        (mat, jax.ShapeDtypeStruct((nodes, nodes), BF16), mat, edge, jax.ShapeDtypeStruct((sections,) + small.shape, F32), picks),
        [ANY, SM, SM, SM, HBM, VM] + [VM] * sections,
        scratch=[pltpu.SemaphoreType.DMA],
    )(own[0], ids, tile_col, tile_count, features, tile_val, *smalls)
    recv = exchange(sent, 0)

    (pay,) = select(ids, [a1, own[1]], [(inner, outer)], [pay, sent])
    b1 = moved(pay, far)
    issued = pay
    (pay,) = select(ids, [own[0], a0], [(inner, outer)], [pay])
    c0 = moved(pay, far)
    (pay,) = select(ids, [own[1], a1], [(inner, outer)], [pay])
    c1 = moved(pay, far)
    sa0 = moved(call(top_kernel, half, [ANY, VM])(issued, a0), sibling)
    sb0 = moved(call(top_kernel, half, [ANY, VM])(sent, b0), sibling)
    brought, swapped = [[a0, b0], [a1]], [[sa0, sb0], []]

    def candidates(p):
        return [weights, cross_val, *brought[p], *swapped[p]]

    def loaded(section, dep):
        cands = candidates(0)
        specs = [SM, ANY, HBM, HBM] + [ANY] * (len(cands) - 2)
        kernel = functools.partial(load_kernel, section)
        return call(kernel, (both, edge), specs, scratch=[dmas])(ids, dep, *cands)

    w, c = loaded(0, pay)

    ends = []
    last_segment = sections - 1
    for k in range(sections):
        last = k == sections - 1
        if k > 0:
            recv = exchange(sent, 0)
        if k == 1:
            c1 = tie(c1, x)
            w, c = loaded(1, c1)
        edges = call(
            functools.partial(edge_kernel, k),
            (edge32, edge32, jax.ShapeDtypeStruct((bound, bound), BF16), edge),
            [VM] * 7,
            flops=LOAD * unit / 4,
        )(x, h, adj, w, c, small, pick)
        sent = call(functools.partial(send_kernel, k), edge, [VM] * 7, flops=LOAD * unit / 4)(recv, *edges[:3], edges[3], w, small)
        recv2 = exchange(sent, 1)
        if k == 1:
            brought[1].append(c1)
            swapped[1].append(moved(brought[1][2], sibling))
        h, x = call(functools.partial(even_kernel, k), (mat, mat), [VM] * 7 + [ANY], flops=LOAD * unit)(
            x, h, adj, recv, w, c, small, sent
        )
        if k == 0:
            brought[1] = [tie(a1, sent), tie(b1, sent)]
            swapped[1] = [moved(v, sibling) for v in brought[1]]
        cands = candidates(1)
        ahead = candidates(0) if k in range(1, sections - 1) else []
        fetch = len(cands) if ahead else 0
        specs = [([HBM, HBM] + [ANY] * (len(v) - 2) if v else []) for v in (cands, ahead)]
        z, w2, c2, *loads = call(
            functools.partial(odd_kernel, k, fetch),
            (mat32, half, edge) + ((both, edge) if ahead else ()),
            [SM, ANY] + [VM] * 3 + specs[0] + specs[1],
            scratch=[pltpu.VMEM((width, width), BF16), dmas] + ([dmas] if ahead else []),
            flops=(20 if last else LOAD) * unit,
        )(ids, c0 if k == 0 else x, x, adj, small, *cands, *ahead)
        if k == 0:
            brought[0].append(tie(c0, recv2, z))
            swapped[0].append(moved(brought[0][2], sibling))
        if last:
            (pay,) = select(ids, ends, [[(j ^ 3,) for j in range(last_segment)]], [x], extra=16)
            others = [s for s in range(sections) if s ^ 3 != last_segment]
            early = moved(pay, lambda s, d: (s ^ (2 if d & 1 else 3), d), others)
        out = call(
            functools.partial(finish_kernel, k, last),
            (mat, tall, tall) if last else (mat, mat, edge),
            [SM] + [VM] * 7 + ([VM] * len(ends) if last else []),
            flops=LOAD * unit,
        )(ids, recv2, z, w2, c2, h, small, pick, *(ends if last else []))
        ends.append(out[0])
        if not last:
            h, x, sent = out
        if ahead:
            w, c = loads
    hop = moved(ends[-1], near, [last_segment ^ 3])
    two = moved(out[2], across(2))
    one = moved(out[1], across(1))
    def onward(value, between, sources, parity=None):
        pairs = []
        for s in sources:
            for d in range(doms):
                if parity is None or d & 1 == parity:
                    pairs.append((between(s, d) * doms + d, (s ^ 3) * doms + d))
        return lax.ppermute(value, ("segment", "dom"), pairs)

    three = onward(tie(hop, early), lambda s, d: near(s, d)[0], [last_segment ^ 3])
    later = onward(early, lambda s, d: s ^ 2, others, 1)
    whole = jax.ShapeDtypeStruct((1, sections, nodes, width), BF16)
    sems = [pltpu.SemaphoreType.DMA((sections,))]
    partly = call(
        collect_early_kernel, whole, [SM] + [ANY] * sections, scratch=[pltpu.SemaphoreType.DMA], out_specs=ANY
    )(ids, *ends)
    return pl.pallas_call(
        collect_last_kernel,
        name="collect_last_kernel",
        out_shape=whole,
        in_specs=[SM] + [ANY] * 6,
        out_specs=ANY,
        scratch_shapes=sems,
        input_output_aliases={6: 0},
        compiler_params=pltpu.CompilerParams(vmem_limit_bytes=2**20),
    )(ids, one, two, three, early, later, partly)


def solution(mesh):
    in_specs = (
        P(None, "dom", None),
        P("segment", None, None),
        P("segment", None),
        P("segment", None),
        P("dom", None, None, None),
        P("dom", None),
        P("dom"),
        P("segment", "dom", None, None),
        P("segment", "dom"),
    )
    out_specs = P("segment", None, "dom", None)
    return jax.shard_map(shards, mesh=mesh, in_specs=in_specs, out_specs=out_specs, check_vma=False)
```

```python
import functools

import jax
import jax.numpy as jnp
from jax import lax
from jax.experimental import pallas as pl
from jax.experimental.pallas import tpu as pltpu
from jax.sharding import PartitionSpec as P

F32 = jnp.float32
BF16 = jnp.bfloat16
VMEM_BYTES = 12 * 2**20
LOAD = 0.5
VM = pl.BlockSpec(memory_space=pltpu.VMEM)
SM = pl.BlockSpec(memory_space=pltpu.SMEM)
ANY = pl.BlockSpec(memory_space=pl.ANY)
HBM = pl.BlockSpec(memory_space=pltpu.HBM)


def call(body, outs, in_specs, scratch=(), out_specs=None, flops=0, vmem=VMEM_BYTES):
    if out_specs is None:
        out_specs = jax.tree.map(lambda _: VM, outs)
    inner = body.func if isinstance(body, functools.partial) else body
    return pl.pallas_call(
        body,
        name=inner.__name__,
        out_shape=outs,
        in_specs=in_specs,
        out_specs=out_specs,
        scratch_shapes=scratch,
        compiler_params=pltpu.CompilerParams(vmem_limit_bytes=vmem),
        cost_estimate=pl.CostEstimate(flops=int(flops), bytes_accessed=0, transcendentals=0),
    )


def dot(a, b):
    return jnp.dot(a, b, preferred_element_type=F32)


def aligned(start, unit):
    return start if isinstance(start, int) else pl.multiple_of(start, unit)


def normed(hf, gain):
    meansq = jnp.mean(hf * hf, axis=-1, keepdims=True)
    return (hf * lax.rsqrt(meansq + 1e-05) * gain).astype(BF16)


def stepped(h, z):
    half = 0.5 * z
    return (h.astype(F32) + half + half * jnp.tanh(half)).astype(BF16)


def start_one(choices, dst, sem):
    for condition, source in choices:

        @pl.when(condition)
        def _():
            pltpu.make_async_copy(source, dst, sem).start()

    return pltpu.make_async_copy(choices[0][1], dst, sem)


def source_of(seg, section, half):
    near, far = 1 + half, 2 - half
    via = seg ^ far
    passed = jnp.logical_or(via == 1, via == 2)
    second = jnp.where(passed, seg ^ 3, via)
    return jnp.where(seg == section, 0, jnp.where((seg ^ near) == section, 1, jnp.where(second == section, 2, 3)))


def fetch_half(seg, core, section, half, own, mine, theirs, dst, sem):
    width = dst.shape[1]
    source = source_of(seg, section, half)
    choices = [(source == 0, own.at[pl.ds(half * width, width), :])]
    for here, refs in ((core == half, mine), (core != half, theirs)):
        for i, ref in enumerate(refs):
            choices.append((jnp.logical_and(here, source == i + 1), ref.at[pl.ds(0, width), :]))
    return [start_one(choices, dst, sem)]


def fetch_cross(seg, core, section, own, mine, dst, sems):
    tile = dst.shape[0]
    width = dst.shape[1]
    blocks = own.shape[0]
    source = jnp.where(core == 0, source_of(seg, section, 0), source_of(seg, section, 1))
    for i, ref in enumerate(mine):

        @pl.when(source == i + 1)
        def _():
            for b in range(blocks):
                part = ref.at[pl.ds(width, tile), pl.ds(b * tile, tile)]
                pltpu.make_async_copy(part, dst.at[:, pl.ds(b * tile, tile)], sems.at[b]).start()

    @pl.when(source == 0)
    def _():
        for b in range(blocks):
            pltpu.make_async_copy(own.at[b], dst.at[:, pl.ds(b * tile, tile)], sems.at[b]).start()

    return [pltpu.make_async_copy(own.at[b], dst.at[:, pl.ds(b * tile, tile)], sems.at[b]) for b in range(blocks)]


def fetch_layer(section, step, ids, cands, top, bottom, cross, sems):
    own, own_cross, mine, theirs = cands
    seg, core = ids[0], ids[1]
    return (
        fetch_half(seg, core, section, 0, own.at[step], mine, theirs, top, sems.at[0])
        + fetch_half(seg, core, section, 1, own.at[step], mine, theirs, bottom, sems.at[1])
        + fetch_cross(seg, core, section, own_cross.at[step], mine, cross, sems.at[pl.ds(2, own_cross.shape[1])])
    )


def cands_of(refs):
    n = (len(refs) - 2) // 2
    return refs[0], refs[1], refs[2 : 2 + n], refs[2 + n :]


def first_kernel(dep, ids, cols, counts, feat_ref, tiles_ref, s0, s1, s2, s3, h_ref, adj_ref, x_ref, sent_ref, small_ref, pick_ref, sem):
    nblk, slots, tile, _ = tiles_ref.shape
    nodes, width = h_ref.shape
    seg = ids[0]
    copy = pltpu.make_async_copy(feat_ref.at[seg], h_ref, sem)
    copy.start()
    for r in range(nblk):
        for j in range(nblk):
            total = jnp.zeros((tile, tile), F32)
            for k in range(slots):
                used = jnp.logical_and(k < counts[r], cols[r, k] == j)
                total = total + jnp.where(used, tiles_ref[r, k].astype(F32), 0.0)
            adj_ref[r * tile : (r + 1) * tile, j * tile : (j + 1) * tile] = total.astype(BF16)
    for r, ref in enumerate((s0, s1, s2, s3)):
        small_ref[seg ^ r] = ref[...]
    sections, steps = small_ref.shape[:2]
    bound = small_ref.shape[2] - 2 * width
    for k in range(sections):
        for p in range(steps):
            rows = small_ref[k, p : p + 1, 2 * width :]
            index = lax.broadcasted_iota(jnp.int32, (nodes, bound), 0).astype(F32)
            pick_ref[k, p] = jnp.where(index == rows, 1.0, 0.0).T.astype(BF16)
    copy.wait()
    x = normed(h_ref[...].astype(F32), small_ref[0, 0:1, width : 2 * width])
    x_ref[...] = x
    sent_ref[...] = dot(pick_ref[0, 0], x).astype(BF16)


def payload_kernel(own, cross, *refs):
    outs, sems = refs[:-1], refs[-1]
    copies = []
    for p, out_ref in enumerate(outs):
        width = out_ref.shape[1]
        tile = cross.shape[-1]
        copies.append(pltpu.make_async_copy(own.at[p], out_ref.at[pl.ds(0, width), :], sems.at[p, 0]))
        for b in range(cross.shape[1]):
            dst = out_ref.at[pl.ds(width, tile), pl.ds(b * tile, tile)]
            copies.append(pltpu.make_async_copy(cross.at[p, b], dst, sems.at[p, b + 1]))
    for copy in copies:
        copy.start()
    for copy in copies:
        copy.wait()


def select_kernel(wanted, ids, *refs):
    count = len(wanted)
    outs, sources = refs[-count:], refs
    rows = sources[0].shape[0]
    for out_ref, rule in zip(outs, wanted):
        if out_ref.shape[0] > rows:
            out_ref[rows:, :] = jnp.zeros((out_ref.shape[0] - rows, out_ref.shape[1]), out_ref.dtype)
        for i, segments in enumerate(rule):
            here = functools.reduce(jnp.logical_or, [ids[0] == s for s in segments])

            @pl.when(here)
            def _():
                out_ref[:rows, :] = sources[i][...]


def select(ids, sources, wanted, deps=(), extra=0):
    rows, columns = sources[0].shape
    shape = jax.ShapeDtypeStruct((rows + extra, columns), sources[0].dtype)
    specs = [SM] + [VM] * len(sources) + [ANY] * len(deps)
    return call(functools.partial(select_kernel, wanted), [shape] * len(wanted), specs, vmem=8 * 2**20)(ids, *sources, *deps)


def tie(value, *deps):
    return pl.pallas_call(
        lambda *refs: None,
        name="tie",
        out_shape=jax.ShapeDtypeStruct(value.shape, value.dtype),
        in_specs=[ANY] * (1 + len(deps)),
        out_specs=ANY,
        input_output_aliases={0: 0},
        compiler_params=pltpu.CompilerParams(vmem_limit_bytes=2**20),
    )(value, *deps)


def top_kernel(dep, in_ref, out_ref):
    out_ref[...] = in_ref[: out_ref.shape[0], :]


def load_kernel(section, ids, dep, *refs):
    w_ref, c_ref, sems = refs[-3:]
    width = w_ref.shape[1]
    parts = w_ref.at[pl.ds(0, width), :], w_ref.at[pl.ds(width, width), :]
    for copy in fetch_layer(section, 0, ids, cands_of(refs[:-3]), *parts, c_ref, sems):
        copy.wait()


def edge_kernel(section, x_ref, h_ref, adj_ref, w_ref, c_ref, small_ref, pick_ref, agg_ref, z_ref, cross_ref, h_out):
    width = x_ref.shape[1]
    pick = pick_ref[section, 1]
    x = x_ref[...]
    adj = dot(pick, adj_ref[...]).astype(BF16)
    agg_ref[...] = dot(adj, x)
    xb = dot(pick, x).astype(BF16)
    z_ref[...] = dot(xb, w_ref[:width, :]) + small_ref[section, 0:1, :width]
    tile = c_ref.shape[0]
    cross = jnp.zeros((pick.shape[0], tile), F32)
    for b in range(c_ref.shape[1] // tile):
        lanes = slice(b * tile, (b + 1) * tile)
        cross = cross + dot(pick[:, lanes], c_ref[:, lanes])
    cross_ref[...] = cross.astype(BF16)
    h_out[...] = dot(pick, h_ref[...]).astype(BF16)


def send_kernel(section, recv_ref, agg_ref, z_ref, cross_ref, h_ref, w_ref, small_ref, sent_ref):
    width = h_ref.shape[1]
    agg = (agg_ref[...] + dot(cross_ref[...], recv_ref[...])).astype(BF16)
    z = z_ref[...] + dot(agg, w_ref[width:, :])
    h = stepped(h_ref[...], z)
    sent_ref[...] = normed(h.astype(F32), small_ref[section, 1:2, width : 2 * width])


def remote(c_ref, recv, i, block):
    tile = c_ref.shape[0]
    parts = []
    for b in range(block // tile):
        lanes = pl.ds(aligned(i * block + b * tile, tile), tile)
        parts.append(dot(c_ref[:, lanes], recv))
    return jnp.concatenate(parts, axis=0)


def even_kernel(section, x_ref, h_ref, adj_ref, recv_ref, w_ref, c_ref, small_ref, dep, h_out, x_out):
    nodes, width = x_ref.shape
    block = 256

    def even(i, carry):
        rows = pl.ds(aligned(i * block, block), block)
        agg = dot(adj_ref[rows, :], x_ref[...]) + remote(c_ref, recv_ref[...], i, block)
        z = dot(x_ref[rows, :], w_ref[:width, :]) + small_ref[section, 0:1, :width]
        z = z + dot(agg.astype(BF16), w_ref[width:, :])
        h = stepped(h_ref[rows, :], z)
        h_out[rows, :] = h
        x_out[rows, :] = normed(h.astype(F32), small_ref[section, 1:2, width : 2 * width])
        return carry

    lax.fori_loop(0, nodes // block, even, 0)


def odd_kernel(section, fetch, ids, dep, x_ref, adj_ref, small_ref, *refs):
    if fetch:
        z_out, w2_out, c_out, w_out, next_c_out, w1_ref, sems, next_sems = refs[-8:]
        cands, ahead = refs[: fetch], refs[fetch:-8]
    else:
        z_out, w2_out, c_out, w1_ref, sems = refs[-5:]
        cands = refs[:-5]
    nodes, width = x_ref.shape
    block = 256
    copies = fetch_layer(section, 1, ids, cands_of(cands), w1_ref, w2_out, c_out, sems)
    if fetch:
        parts = w_out.at[pl.ds(0, width), :], w_out.at[pl.ds(width, width), :]
        copies += fetch_layer(section + 1, 0, ids, cands_of(ahead), *parts, next_c_out, next_sems)
    copies[0].wait()
    copies[1].wait()

    def odd(i, carry):
        rows = pl.ds(aligned(i * block, block), block)
        agg = dot(adj_ref[rows, :], x_ref[...]).astype(BF16)
        z = dot(x_ref[rows, :], w1_ref[...]) + small_ref[section, 1:2, :width]
        z_out[rows, :] = z + dot(agg, w2_out[...])
        return carry

    lax.fori_loop(0, nodes // block, odd, 0)
    for copy in copies[2:]:
        copy.wait()


def finish_kernel(section, last, ids, recv_ref, z_ref, w2_ref, c_ref, h_ref, small_ref, pick_ref, *refs):
    nodes, width = h_ref.shape
    block = 256
    if last:
        ends, (h_out, *pays) = refs[:section], refs[section:]
        for k, end_ref in enumerate(ends):
            for r, pay_ref in enumerate(pays, 1):

                @pl.when(ids[0] == k ^ r)
                def _():
                    pay_ref[:nodes, :] = end_ref[...]

        for pay_ref in pays:
            pay_ref[nodes:, :] = jnp.zeros((pay_ref.shape[0] - nodes, width), BF16)
    else:
        h_out, x_out, sent_out = refs
    seen = dot(recv_ref[...], w2_ref[...]).astype(BF16)
    for i in range(nodes // block):
        rows = pl.ds(i * block, block)
        z = z_ref[rows, :] + remote(c_ref, seen, i, block)
        h = stepped(h_ref[rows, :], z)
        h_out[rows, :] = h
        if last:
            for r, pay_ref in enumerate(pays, 1):

                @pl.when(ids[0] == section ^ r)
                def _():
                    pay_ref[rows, :] = h
        else:
            x_out[rows, :] = normed(h.astype(F32), small_ref[section + 1, 0:1, width : 2 * width])
    if not last:
        sent_out[...] = dot(pick_ref[section + 1, 0], x_out[...]).astype(BF16)


def collect_early_kernel(ids, *refs):
    out_ref, sem = refs[-2:]
    start_one([(ids[0] == k, end) for k, end in enumerate(refs[:-2])], out_ref.at[0, ids[0]], sem).wait()


def collect_last_kernel(ids, one_ref, two_ref, three_ref, first_ref, early_ref, later_ref, _, out_ref, sems):
    last = out_ref.shape[1] - 1
    rows = pl.ds(0, out_ref.shape[2])
    copies = [
        pltpu.make_async_copy(ref.at[rows, :], out_ref.at[0, ids[0] ^ r], sems.at[r]) for r, ref in ((1, one_ref), (2, two_ref))
    ]
    for copy in copies:
        copy.start()
    choices = [
        (ids[0] == last, three_ref),
        (ids[0] < 2, first_ref.at[rows, :]),
        (jnp.logical_and(ids[0] == 2, ids[1] == 0), early_ref.at[rows, :]),
        (jnp.logical_and(ids[0] == 2, ids[1] != 0), later_ref.at[rows, :]),
    ]
    copies.append(start_one(choices, out_ref.at[0, ids[0] ^ 3], sems.at[3]))
    for copy in copies:
        copy.wait()


def shards(features, weights, bias, gain, tile_val, tile_col, tile_count, cross_val, send_rows):
    sections = lax.axis_size("segment")
    doms = lax.axis_size("dom")
    seg = lax.axis_index("segment")
    core = lax.axis_index("dom") & 1
    steps, _, width = weights.shape
    nodes = features.shape[1]
    bound = send_rows.shape[1]
    nbits = doms.bit_length() - 1
    ids = jnp.stack([seg, core]).astype(jnp.int32)

    def moved(value, target, sources=range(sections)):
        pairs = []
        for s in sources:
            for d in range(doms):
                t, e = target(s, d)
                pairs.append((s * doms + d, t * doms + e))
        return lax.ppermute(value, ("segment", "dom"), pairs)

    def near(s, d):
        return s ^ (1 + (d & 1)), d

    def far(s, d):
        return s ^ (2 - (d & 1)), d

    def sibling(s, d):
        return s, d ^ 1

    def across(r):
        return lambda s, d: (s ^ r, d)

    def exchange(sent, step):
        bit = step * (nbits - 1) // max(steps - 1, 1)
        return lax.ppermute(sent, "dom", [(i, i ^ 1 << bit) for i in range(doms)])

    mat = jax.ShapeDtypeStruct((nodes, width), BF16)
    mat32 = jax.ShapeDtypeStruct((nodes, width), F32)
    tall = jax.ShapeDtypeStruct((nodes + 32, width), BF16)
    edge = jax.ShapeDtypeStruct((bound, width), BF16)
    edge32 = jax.ShapeDtypeStruct((bound, width), F32)
    half = jax.ShapeDtypeStruct((width, width), BF16)
    both = jax.ShapeDtypeStruct((2 * width, width), BF16)
    load = jax.ShapeDtypeStruct((width + bound, width), BF16)
    picks = jax.ShapeDtypeStruct((sections, steps, bound, nodes), BF16)
    unit = 2 * nodes * width * width
    dmas = pltpu.SemaphoreType.DMA((2 + cross_val.shape[1],))

    own = call(
        payload_kernel,
        [load] * steps,
        [ANY, ANY],
        scratch=[pltpu.SemaphoreType.DMA((steps, 1 + cross_val.shape[1]))],
    )(lax.dynamic_slice_in_dim(weights, core * width, width, axis=1), cross_val)
    small = tie(jnp.concatenate([bias, gain, send_rows.astype(F32)], axis=1), own[0])
    smalls = [small] + [moved(small, across(r)) for r in range(1, sections)]
    inner, outer = (1, 2), (0, 3)
    a0, a1 = [moved(v, near) for v in own]
    (pay,) = select(ids, [a0, own[0]], [(inner, outer)])
    b0 = moved(pay, far)
    h, adj, x, sent, small, pick = call(
        first_kernel,
        (mat, jax.ShapeDtypeStruct((nodes, nodes), BF16), mat, edge, jax.ShapeDtypeStruct((sections,) + small.shape, F32), picks),
        [ANY, SM, SM, SM, HBM, VM] + [VM] * sections,
        scratch=[pltpu.SemaphoreType.DMA],
    )(own[0], ids, tile_col, tile_count, features, tile_val, *smalls)
    recv = exchange(sent, 0)

    (pay,) = select(ids, [a1, own[1]], [(inner, outer)], [pay, sent])
    b1 = moved(pay, far)
    issued = pay
    (pay,) = select(ids, [own[0], a0], [(inner, outer)], [pay])
    c0 = moved(pay, far)
    (pay,) = select(ids, [own[1], a1], [(inner, outer)], [pay])
    c1 = moved(pay, far)
    sa0 = moved(call(top_kernel, half, [ANY, VM])(issued, a0), sibling)
    sb0 = moved(call(top_kernel, half, [ANY, VM])(sent, b0), sibling)
    brought, swapped = [[a0, b0], [a1]], [[sa0, sb0], []]

    def candidates(p):
        return [weights, cross_val, *brought[p], *swapped[p]]

    def loaded(section, dep):
        cands = candidates(0)
        specs = [SM, ANY, HBM, HBM] + [ANY] * (len(cands) - 2)
        kernel = functools.partial(load_kernel, section)
        return call(kernel, (both, edge), specs, scratch=[dmas])(ids, dep, *cands)

    w, c = loaded(0, pay)

    ends = []
    last_segment = sections - 1
    for k in range(sections):
        last = k == sections - 1
        if k > 0:
            recv = exchange(sent, 0)
        if k == 1:
            c1 = tie(c1, x)
            w, c = loaded(1, c1)
        edges = call(
            functools.partial(edge_kernel, k),
            (edge32, edge32, jax.ShapeDtypeStruct((bound, bound), BF16), edge),
            [VM] * 7,
            flops=LOAD * unit / 4,
        )(x, h, adj, w, c, small, pick)
        sent = call(functools.partial(send_kernel, k), edge, [VM] * 7, flops=LOAD * unit / 4)(recv, *edges[:3], edges[3], w, small)
        recv2 = exchange(sent, 1)
        if k == 1:
            brought[1].append(c1)
            swapped[1].append(moved(brought[1][2], sibling))
        h, x = call(functools.partial(even_kernel, k), (mat, mat), [VM] * 7 + [ANY], flops=LOAD * unit)(
            x, h, adj, recv, w, c, small, sent
        )
        if k == 0:
            brought[1] = [tie(a1, sent), tie(b1, sent)]
            swapped[1] = [moved(v, sibling) for v in brought[1]]
        cands = candidates(1)
        ahead = candidates(0) if k in range(1, sections - 1) else []
        fetch = len(cands) if ahead else 0
        specs = [([HBM, HBM] + [ANY] * (len(v) - 2) if v else []) for v in (cands, ahead)]
        z, w2, c2, *loads = call(
            functools.partial(odd_kernel, k, fetch),
            (mat32, half, edge) + ((both, edge) if ahead else ()),
            [SM, ANY] + [VM] * 3 + specs[0] + specs[1],
            scratch=[pltpu.VMEM((width, width), BF16), dmas] + ([dmas] if ahead else []),
            flops=(20 if k > 1 else LOAD) * unit,
        )(ids, c0 if k == 0 else first_two if last else x, x, adj, small, *cands, *ahead)
        if k == 0:
            brought[0].append(tie(c0, recv2, z))
            swapped[0].append(moved(brought[0][2], sibling))
        if k == 2:
            (pay,) = select(ids, ends, [[(j ^ 3,) for j in range(2)]], [x], extra=16)
            first_two = moved(pay, across(3), [j ^ 3 for j in range(2)])
        if last:
            (pay,) = select(ids, ends[2:], [[(2 ^ 3,)]], [x], extra=16)
            others = [2 ^ 3]
            early = moved(pay, lambda s, d: (s ^ (2 if d & 1 else 3), d), others)
        out = call(
            functools.partial(finish_kernel, k, last),
            (mat, tall, tall) if last else (mat, mat, edge),
            [SM] + [VM] * 7 + ([VM] * len(ends) if last else []),
            flops=LOAD * unit,
        )(ids, recv2, z, w2, c2, h, small, pick, *(ends if last else []))
        ends.append(out[0])
        if not last:
            h, x, sent = out
        if ahead:
            w, c = loads
    hop = moved(ends[-1], near, [last_segment ^ 3])
    two = moved(out[2], across(2))
    one = moved(out[1], across(1))
    def onward(value, between, sources, parity=None):
        pairs = []
        for s in sources:
            for d in range(doms):
                if parity is None or d & 1 == parity:
                    pairs.append((between(s, d) * doms + d, (s ^ 3) * doms + d))
        return lax.ppermute(value, ("segment", "dom"), pairs)

    three = onward(tie(hop, early), lambda s, d: near(s, d)[0], [last_segment ^ 3])
    later = onward(early, lambda s, d: s ^ 2, others, 1)
    whole = jax.ShapeDtypeStruct((1, sections, nodes, width), BF16)
    sems = [pltpu.SemaphoreType.DMA((sections,))]
    partly = call(
        collect_early_kernel, whole, [SM] + [ANY] * sections, scratch=[pltpu.SemaphoreType.DMA], out_specs=ANY
    )(ids, *ends)
    return pl.pallas_call(
        collect_last_kernel,
        name="collect_last_kernel",
        out_shape=whole,
        in_specs=[SM] + [ANY] * 7,
        out_specs=ANY,
        scratch_shapes=sems,
        input_output_aliases={7: 0},
        compiler_params=pltpu.CompilerParams(vmem_limit_bytes=2**20),
    )(ids, one, two, three, first_two, early, later, partly)


def solution(mesh):
    in_specs = (
        P(None, "dom", None),
        P("segment", None, None),
        P("segment", None),
        P("segment", None),
        P("dom", None, None, None),
        P("dom", None),
        P("dom"),
        P("segment", "dom", None, None),
        P("segment", "dom"),
    )
    out_specs = P("segment", None, "dom", None)
    return jax.shard_map(shards, mesh=mesh, in_specs=in_specs, out_specs=out_specs, check_vma=False)
```

```python
import functools

import jax
import jax.numpy as jnp
from jax import lax
from jax.experimental import pallas as pl
from jax.experimental.pallas import tpu as pltpu
from jax.sharding import PartitionSpec as P

F32 = jnp.float32
BF16 = jnp.bfloat16
VMEM_BYTES = 12 * 2**20
LOAD = 0.5
VM = pl.BlockSpec(memory_space=pltpu.VMEM)
SM = pl.BlockSpec(memory_space=pltpu.SMEM)
ANY = pl.BlockSpec(memory_space=pl.ANY)
HBM = pl.BlockSpec(memory_space=pltpu.HBM)


def call(body, outs, in_specs, scratch=(), out_specs=None, flops=0, vmem=VMEM_BYTES):
    if out_specs is None:
        out_specs = jax.tree.map(lambda _: VM, outs)
    inner = body.func if isinstance(body, functools.partial) else body
    return pl.pallas_call(
        body,
        name=inner.__name__,
        out_shape=outs,
        in_specs=in_specs,
        out_specs=out_specs,
        scratch_shapes=scratch,
        compiler_params=pltpu.CompilerParams(vmem_limit_bytes=vmem),
        cost_estimate=pl.CostEstimate(flops=int(flops), bytes_accessed=0, transcendentals=0),
    )


def dot(a, b):
    return jnp.dot(a, b, preferred_element_type=F32)


def aligned(start, unit):
    return start if isinstance(start, int) else pl.multiple_of(start, unit)


def normed(hf, gain):
    meansq = jnp.mean(hf * hf, axis=-1, keepdims=True)
    return (hf * lax.rsqrt(meansq + 1e-05) * gain).astype(BF16)


def stepped(h, z):
    half = 0.5 * z
    return (h.astype(F32) + half + half * jnp.tanh(half)).astype(BF16)


def start_one(choices, dst, sem):
    for condition, source in choices:

        @pl.when(condition)
        def _():
            pltpu.make_async_copy(source, dst, sem).start()

    return pltpu.make_async_copy(choices[0][1], dst, sem)


def source_of(seg, section, half):
    near, far = 1 + half, 2 - half
    via = seg ^ far
    passed = jnp.logical_or(via == 1, via == 2)
    second = jnp.where(passed, seg ^ 3, via)
    return jnp.where(seg == section, 0, jnp.where((seg ^ near) == section, 1, jnp.where(second == section, 2, 3)))


def fetch_half(seg, core, section, half, own, mine, theirs, dst, sem):
    width = dst.shape[1]
    source = source_of(seg, section, half)
    choices = [(source == 0, own.at[pl.ds(half * width, width), :])]
    for here, refs in ((core == half, mine), (core != half, theirs)):
        for i, ref in enumerate(refs):
            choices.append((jnp.logical_and(here, source == i + 1), ref.at[pl.ds(0, width), :]))
    return [start_one(choices, dst, sem)]


def fetch_cross(seg, core, section, own, mine, dst, sems):
    tile = dst.shape[0]
    width = dst.shape[1]
    blocks = own.shape[0]
    source = jnp.where(core == 0, source_of(seg, section, 0), source_of(seg, section, 1))
    for i, ref in enumerate(mine):

        @pl.when(source == i + 1)
        def _():
            for b in range(blocks):
                part = ref.at[pl.ds(width, tile), pl.ds(b * tile, tile)]
                pltpu.make_async_copy(part, dst.at[:, pl.ds(b * tile, tile)], sems.at[b]).start()

    @pl.when(source == 0)
    def _():
        for b in range(blocks):
            pltpu.make_async_copy(own.at[b], dst.at[:, pl.ds(b * tile, tile)], sems.at[b]).start()

    return [pltpu.make_async_copy(own.at[b], dst.at[:, pl.ds(b * tile, tile)], sems.at[b]) for b in range(blocks)]


def fetch_layer(section, step, ids, cands, top, bottom, cross, sems):
    own, own_cross, mine, theirs = cands
    seg, core = ids[0], ids[1]
    return (
        fetch_half(seg, core, section, 0, own.at[step], mine, theirs, top, sems.at[0])
        + fetch_half(seg, core, section, 1, own.at[step], mine, theirs, bottom, sems.at[1])
        + fetch_cross(seg, core, section, own_cross.at[step], mine, cross, sems.at[pl.ds(2, own_cross.shape[1])])
    )


def cands_of(refs):
    n = (len(refs) - 2) // 2
    return refs[0], refs[1], refs[2 : 2 + n], refs[2 + n :]


def first_kernel(dep, ids, cols, counts, feat_ref, tiles_ref, s0, s1, s2, s3, h_ref, adj_ref, x_ref, sent_ref, small_ref, pick_ref, sem):
    nblk, slots, tile, _ = tiles_ref.shape
    nodes, width = h_ref.shape
    seg = ids[0]
    copy = pltpu.make_async_copy(feat_ref.at[seg], h_ref, sem)
    copy.start()
    for r in range(nblk):
        for j in range(nblk):
            total = jnp.zeros((tile, tile), F32)
            for k in range(slots):
                used = jnp.logical_and(k < counts[r], cols[r, k] == j)
                total = total + jnp.where(used, tiles_ref[r, k].astype(F32), 0.0)
            adj_ref[r * tile : (r + 1) * tile, j * tile : (j + 1) * tile] = total.astype(BF16)
    for r, ref in enumerate((s0, s1, s2, s3)):
        small_ref[seg ^ r] = ref[...]
    sections, steps = small_ref.shape[:2]
    bound = small_ref.shape[2] - 2 * width
    for k in range(sections):
        for p in range(steps):
            rows = small_ref[k, p : p + 1, 2 * width :]
            index = lax.broadcasted_iota(jnp.int32, (nodes, bound), 0).astype(F32)
            pick_ref[k, p] = jnp.where(index == rows, 1.0, 0.0).T.astype(BF16)
    copy.wait()
    x = normed(h_ref[...].astype(F32), small_ref[0, 0:1, width : 2 * width])
    x_ref[...] = x
    sent_ref[...] = dot(pick_ref[0, 0], x).astype(BF16)


def payload_kernel(own, cross, *refs):
    outs, sems = refs[:-1], refs[-1]
    copies = []
    for p, out_ref in enumerate(outs):
        width = out_ref.shape[1]
        tile = cross.shape[-1]
        copies.append(pltpu.make_async_copy(own.at[p], out_ref.at[pl.ds(0, width), :], sems.at[p, 0]))
        for b in range(cross.shape[1]):
            dst = out_ref.at[pl.ds(width, tile), pl.ds(b * tile, tile)]
            copies.append(pltpu.make_async_copy(cross.at[p, b], dst, sems.at[p, b + 1]))
    for copy in copies:
        copy.start()
    for copy in copies:
        copy.wait()


def select_kernel(wanted, ids, *refs):
    count = len(wanted)
    outs, sources = refs[-count:], refs
    rows = sources[0].shape[0]
    for out_ref, rule in zip(outs, wanted):
        if out_ref.shape[0] > rows:
            out_ref[rows:, :] = jnp.zeros((out_ref.shape[0] - rows, out_ref.shape[1]), out_ref.dtype)
        for i, segments in enumerate(rule):
            here = functools.reduce(jnp.logical_or, [ids[0] == s for s in segments])

            @pl.when(here)
            def _():
                out_ref[:rows, :] = sources[i][...]


def select(ids, sources, wanted, deps=(), extra=0):
    rows, columns = sources[0].shape
    shape = jax.ShapeDtypeStruct((rows + extra, columns), sources[0].dtype)
    specs = [SM] + [VM] * len(sources) + [ANY] * len(deps)
    return call(functools.partial(select_kernel, wanted), [shape] * len(wanted), specs, vmem=8 * 2**20)(ids, *sources, *deps)


def tie(value, *deps):
    return pl.pallas_call(
        lambda *refs: None,
        name="tie",
        out_shape=jax.ShapeDtypeStruct(value.shape, value.dtype),
        in_specs=[ANY] * (1 + len(deps)),
        out_specs=ANY,
        input_output_aliases={0: 0},
        compiler_params=pltpu.CompilerParams(vmem_limit_bytes=2**20),
    )(value, *deps)


def top_kernel(dep, in_ref, out_ref):
    out_ref[...] = in_ref[: out_ref.shape[0], :]


def load_kernel(section, ids, dep, *refs):
    w_ref, c_ref, sems = refs[-3:]
    width = w_ref.shape[1]
    parts = w_ref.at[pl.ds(0, width), :], w_ref.at[pl.ds(width, width), :]
    for copy in fetch_layer(section, 0, ids, cands_of(refs[:-3]), *parts, c_ref, sems):
        copy.wait()


def edge_kernel(section, x_ref, h_ref, adj_ref, w_ref, c_ref, small_ref, pick_ref, agg_ref, z_ref, cross_ref, h_out):
    width = x_ref.shape[1]
    pick = pick_ref[section, 1]
    x = x_ref[...]
    adj = dot(pick, adj_ref[...]).astype(BF16)
    agg_ref[...] = dot(adj, x)
    xb = dot(pick, x).astype(BF16)
    z_ref[...] = dot(xb, w_ref[:width, :]) + small_ref[section, 0:1, :width]
    tile = c_ref.shape[0]
    cross = jnp.zeros((pick.shape[0], tile), F32)
    for b in range(c_ref.shape[1] // tile):
        lanes = slice(b * tile, (b + 1) * tile)
        cross = cross + dot(pick[:, lanes], c_ref[:, lanes])
    cross_ref[...] = cross.astype(BF16)
    h_out[...] = dot(pick, h_ref[...]).astype(BF16)


def send_kernel(section, recv_ref, agg_ref, z_ref, cross_ref, h_ref, w_ref, small_ref, sent_ref):
    width = h_ref.shape[1]
    agg = (agg_ref[...] + dot(cross_ref[...], recv_ref[...])).astype(BF16)
    z = z_ref[...] + dot(agg, w_ref[width:, :])
    h = stepped(h_ref[...], z)
    sent_ref[...] = normed(h.astype(F32), small_ref[section, 1:2, width : 2 * width])


def remote(c_ref, recv, i, block):
    tile = c_ref.shape[0]
    parts = []
    for b in range(block // tile):
        lanes = pl.ds(aligned(i * block + b * tile, tile), tile)
        parts.append(dot(c_ref[:, lanes], recv))
    return jnp.concatenate(parts, axis=0)


def even_kernel(section, x_ref, h_ref, adj_ref, recv_ref, w_ref, c_ref, small_ref, dep, h_out, x_out):
    nodes, width = x_ref.shape
    block = 256

    def even(i, carry):
        rows = pl.ds(aligned(i * block, block), block)
        agg = dot(adj_ref[rows, :], x_ref[...]) + remote(c_ref, recv_ref[...], i, block)
        z = dot(x_ref[rows, :], w_ref[:width, :]) + small_ref[section, 0:1, :width]
        z = z + dot(agg.astype(BF16), w_ref[width:, :])
        h = stepped(h_ref[rows, :], z)
        h_out[rows, :] = h
        x_out[rows, :] = normed(h.astype(F32), small_ref[section, 1:2, width : 2 * width])
        return carry

    lax.fori_loop(0, nodes // block, even, 0)


def odd_kernel(section, fetch, ids, dep, x_ref, adj_ref, small_ref, *refs):
    if fetch:
        z_out, w2_out, c_out, w_out, next_c_out, w1_ref, sems, next_sems = refs[-8:]
        cands, ahead = refs[: fetch], refs[fetch:-8]
    else:
        z_out, w2_out, c_out, w1_ref, sems = refs[-5:]
        cands = refs[:-5]
    nodes, width = x_ref.shape
    block = 256
    copies = fetch_layer(section, 1, ids, cands_of(cands), w1_ref, w2_out, c_out, sems)
    if fetch:
        parts = w_out.at[pl.ds(0, width), :], w_out.at[pl.ds(width, width), :]
        copies += fetch_layer(section + 1, 0, ids, cands_of(ahead), *parts, next_c_out, next_sems)
    copies[0].wait()
    copies[1].wait()

    def odd(i, carry):
        rows = pl.ds(aligned(i * block, block), block)
        agg = dot(adj_ref[rows, :], x_ref[...]).astype(BF16)
        z = dot(x_ref[rows, :], w1_ref[...]) + small_ref[section, 1:2, :width]
        z_out[rows, :] = z + dot(agg, w2_out[...])
        return carry

    lax.fori_loop(0, nodes // block, odd, 0)
    for copy in copies[2:]:
        copy.wait()


def finish_kernel(section, last, ids, recv_ref, z_ref, w2_ref, c_ref, h_ref, small_ref, pick_ref, *refs):
    nodes, width = h_ref.shape
    block = 256
    if last:
        ends, (h_out, *pays) = refs[:section], refs[section:]
        for k, end_ref in enumerate(ends):
            for r, pay_ref in enumerate(pays, 1):

                @pl.when(ids[0] == k ^ r)
                def _():
                    pay_ref[:nodes, :] = end_ref[...]

        for pay_ref in pays:
            pay_ref[nodes:, :] = jnp.zeros((pay_ref.shape[0] - nodes, width), BF16)
    else:
        h_out, x_out, sent_out = refs
    seen = dot(recv_ref[...], w2_ref[...]).astype(BF16)
    for i in range(nodes // block):
        rows = pl.ds(i * block, block)
        z = z_ref[rows, :] + remote(c_ref, seen, i, block)
        h = stepped(h_ref[rows, :], z)
        h_out[rows, :] = h
        if last:
            for r, pay_ref in enumerate(pays, 1):

                @pl.when(ids[0] == section ^ r)
                def _():
                    pay_ref[rows, :] = h
        else:
            x_out[rows, :] = normed(h.astype(F32), small_ref[section + 1, 0:1, width : 2 * width])
    if not last:
        sent_out[...] = dot(pick_ref[section + 1, 0], x_out[...]).astype(BF16)


def collect_kernel(ids, e0, e1, e2, e3, one_ref, two_ref, first_ref, second_ref, early_ref, later_ref, out_ref, sems):
    seg, core = ids[0], ids[1]
    rows = pl.ds(0, out_ref.shape[2])
    low, at_two, even = seg < 2, seg == 2, core == 0

    def both(a, b):
        return jnp.logical_and(a, b)

    odd = jnp.logical_not(even)
    own = [(seg == k, ref) for k, ref in enumerate((e0, e1, e2, e3))]
    beside = [
        (both(low, even), second_ref.at[rows, :]),
        (both(low, odd), first_ref.at[rows, :]),
        (jnp.logical_not(low), one_ref.at[rows, :]),
    ]
    above = [
        (both(at_two, even), later_ref.at[rows, :]),
        (both(at_two, odd), early_ref.at[rows, :]),
        (jnp.logical_not(at_two), two_ref.at[rows, :]),
    ]
    copies = [start_one(v, out_ref.at[0, seg ^ r], sems.at[r]) for r, v in enumerate((own, beside, above))]

    @pl.when(seg != 3)
    def _():
        crossed = [
            (both(low, even), first_ref.at[rows, :]),
            (both(low, odd), second_ref.at[rows, :]),
            (both(at_two, even), early_ref.at[rows, :]),
            (both(at_two, odd), later_ref.at[rows, :]),
        ]
        start_one(crossed, out_ref.at[0, seg ^ 3], sems.at[3]).wait()

    for copy in copies:
        copy.wait()


def collect_last_kernel(ids, three_ref, _, out_ref, sem):
    last = out_ref.shape[1] - 1

    @pl.when(ids[0] == last)
    def _():
        copy = pltpu.make_async_copy(three_ref, out_ref.at[0, last ^ 3], sem)
        copy.start()
        copy.wait()


def shards(features, weights, bias, gain, tile_val, tile_col, tile_count, cross_val, send_rows):
    sections = lax.axis_size("segment")
    doms = lax.axis_size("dom")
    seg = lax.axis_index("segment")
    core = lax.axis_index("dom") & 1
    steps, _, width = weights.shape
    nodes = features.shape[1]
    bound = send_rows.shape[1]
    nbits = doms.bit_length() - 1
    ids = jnp.stack([seg, core]).astype(jnp.int32)

    def moved(value, target, sources=range(sections)):
        pairs = []
        for s in sources:
            for d in range(doms):
                to = target(s, d)
                if to is not None:
                    pairs.append((s * doms + d, to[0] * doms + to[1]))
        return lax.ppermute(value, ("segment", "dom"), pairs)

    def near(s, d):
        return s ^ (1 + (d & 1)), d

    def far(s, d):
        return s ^ (2 - (d & 1)), d

    def sibling(s, d):
        return s, d ^ 1

    def across(r):
        return lambda s, d: (s ^ r, d)

    def exchange(sent, step):
        bit = step * (nbits - 1) // max(steps - 1, 1)
        return lax.ppermute(sent, "dom", [(i, i ^ 1 << bit) for i in range(doms)])

    mat = jax.ShapeDtypeStruct((nodes, width), BF16)
    mat32 = jax.ShapeDtypeStruct((nodes, width), F32)
    tall = jax.ShapeDtypeStruct((nodes + 32, width), BF16)
    edge = jax.ShapeDtypeStruct((bound, width), BF16)
    edge32 = jax.ShapeDtypeStruct((bound, width), F32)
    half = jax.ShapeDtypeStruct((width, width), BF16)
    both = jax.ShapeDtypeStruct((2 * width, width), BF16)
    load = jax.ShapeDtypeStruct((width + bound, width), BF16)
    picks = jax.ShapeDtypeStruct((sections, steps, bound, nodes), BF16)
    unit = 2 * nodes * width * width
    dmas = pltpu.SemaphoreType.DMA((2 + cross_val.shape[1],))

    own = call(
        payload_kernel,
        [load] * steps,
        [ANY, ANY],
        scratch=[pltpu.SemaphoreType.DMA((steps, 1 + cross_val.shape[1]))],
    )(lax.dynamic_slice_in_dim(weights, core * width, width, axis=1), cross_val)
    small = tie(jnp.concatenate([bias, gain, send_rows.astype(F32)], axis=1), own[0])
    smalls = [small] + [moved(small, across(r)) for r in range(1, sections)]
    inner, outer = (1, 2), (0, 3)
    a0, a1 = [moved(v, near) for v in own]
    (pay,) = select(ids, [a0, own[0]], [(inner, outer)])
    b0 = moved(pay, far)
    h, adj, x, sent, small, pick = call(
        first_kernel,
        (mat, jax.ShapeDtypeStruct((nodes, nodes), BF16), mat, edge, jax.ShapeDtypeStruct((sections,) + small.shape, F32), picks),
        [ANY, SM, SM, SM, HBM, VM] + [VM] * sections,
        scratch=[pltpu.SemaphoreType.DMA],
    )(own[0], ids, tile_col, tile_count, features, tile_val, *smalls)
    recv = exchange(sent, 0)

    (pay,) = select(ids, [a1, own[1]], [(inner, outer)], [pay, sent])
    b1 = moved(pay, far)
    issued = pay
    (pay,) = select(ids, [own[0], a0], [(inner, outer)], [pay])
    c0 = moved(pay, far)
    (pay,) = select(ids, [own[1], a1], [(inner, outer)], [pay])
    c1 = moved(pay, far)
    sa0 = moved(call(top_kernel, half, [ANY, VM])(issued, a0), sibling)
    sb0 = moved(call(top_kernel, half, [ANY, VM])(sent, b0), sibling)
    brought, swapped = [[a0, b0], [a1]], [[sa0, sb0], []]

    def candidates(p):
        return [weights, cross_val, *brought[p], *swapped[p]]

    def loaded(section, dep):
        cands = candidates(0)
        specs = [SM, ANY, HBM, HBM] + [ANY] * (len(cands) - 2)
        kernel = functools.partial(load_kernel, section)
        return call(kernel, (both, edge), specs, scratch=[dmas])(ids, dep, *cands)

    w, c = loaded(0, pay)

    ends = []
    last_segment = sections - 1
    for k in range(sections):
        last = k == sections - 1
        if k > 0:
            recv = exchange(sent, 0)
        if k == 1:
            c1 = tie(c1, x)
            w, c = loaded(1, c1)
        edges = call(
            functools.partial(edge_kernel, k),
            (edge32, edge32, jax.ShapeDtypeStruct((bound, bound), BF16), edge),
            [VM] * 7,
            flops=LOAD * unit / 4,
        )(x, h, adj, w, c, small, pick)
        sent = call(functools.partial(send_kernel, k), edge, [VM] * 7, flops=LOAD * unit / 4)(recv, *edges[:3], edges[3], w, small)
        recv2 = exchange(sent, 1)
        if k == 1:
            brought[1].append(c1)
            swapped[1].append(moved(brought[1][2], sibling))
        h, x = call(functools.partial(even_kernel, k), (mat, mat), [VM] * 7 + [ANY], flops=LOAD * unit)(
            x, h, adj, recv, w, c, small, sent
        )
        if k == 0:
            brought[1] = [tie(a1, sent), tie(b1, sent)]
            swapped[1] = [moved(v, sibling) for v in brought[1]]
        cands = candidates(1)
        ahead = candidates(0) if k in range(1, sections - 1) else []
        fetch = len(cands) if ahead else 0
        specs = [([HBM, HBM] + [ANY] * (len(v) - 2) if v else []) for v in (cands, ahead)]
        z, w2, c2, *loads = call(
            functools.partial(odd_kernel, k, fetch),
            (mat32, half, edge) + ((both, edge) if ahead else ()),
            [SM, ANY] + [VM] * 3 + specs[0] + specs[1],
            scratch=[pltpu.VMEM((width, width), BF16), dmas] + ([dmas] if ahead else []),
            flops=(20 if k > 1 else LOAD) * unit,
        )(ids, c0 if k == 0 else first_two[0] if last else x, x, adj, small, *cands, *ahead)
        if k == 0:
            brought[0].append(tie(c0, recv2, z))
            swapped[0].append(moved(brought[0][2], sibling))
        if k == 2:
            (pay,) = select(ids, ends, [[(1, 3), (0, 2)]], [x], extra=16)

            def crossing(parity):
                return lambda s, d: (s ^ (3 if s > 1 else 1), d) if (d & 1 == parity) == (s > 1) else None

            first_two = [moved(pay, crossing(parity)) for parity in range(2)]
            first_two[0] = tie(first_two[0], first_two[1])
        if last:
            (fresh,) = select(ids, ends[2:], [[(0, 1)]], [x], extra=16)
            early = moved(fresh, lambda s, d: (s ^ 2, d) if d & 1 else (s ^ 3, d) if s else None, [0, 1])
        out = call(
            functools.partial(finish_kernel, k, last),
            (mat, tall, tall) if last else (mat, mat, edge),
            [SM] + [VM] * 7 + ([VM] * len(ends) if last else []),
            flops=LOAD * unit,
        )(ids, recv2, z, w2, c2, h, small, pick, *(ends if last else []))
        ends.append(out[0])
        if not last:
            h, x, sent = out
        if ahead:
            w, c = loads
    hop = moved(ends[-1], near, [last_segment ^ 3])
    two = moved(out[2], across(2), [1, 2, 3])
    one = moved(out[1], across(1), [2, 3])

    pairs = []
    for d in range(doms):
        s, _ = near(last_segment ^ 3, d)
        pairs.append((s * doms + d, last_segment * doms + d))
    three = lax.ppermute(tie(hop, early), ("segment", "dom"), pairs)
    (pay,) = select(ids, [early, fresh], [[(3,), (0,)]])
    later = moved(pay, lambda s, d: (2, d) if (d & 1 == 1) == (s == 3) else None, [0, 3])
    whole = jax.ShapeDtypeStruct((1, sections, nodes, width), BF16)
    sems = [pltpu.SemaphoreType.DMA((sections,))]
    pieces = [*ends, one, two, *first_two, early, later]
    partly = call(collect_kernel, whole, [SM] + [ANY] * len(pieces), scratch=sems, out_specs=ANY)(ids, *pieces)
    return pl.pallas_call(
        collect_last_kernel,
        name="collect_last_kernel",
        out_shape=whole,
        in_specs=[SM] + [ANY] * 2,
        out_specs=ANY,
        scratch_shapes=[pltpu.SemaphoreType.DMA],
        input_output_aliases={2: 0},
        compiler_params=pltpu.CompilerParams(vmem_limit_bytes=2**20),
    )(ids, three, partly)


def solution(mesh):
    in_specs = (
        P(None, "dom", None),
        P("segment", None, None),
        P("segment", None),
        P("segment", None),
        P("dom", None, None, None),
        P("dom", None),
        P("dom"),
        P("segment", "dom", None, None),
        P("segment", "dom"),
    )
    out_specs = P("segment", None, "dom", None)
    return jax.shard_map(shards, mesh=mesh, in_specs=in_specs, out_specs=out_specs, check_vma=False)
```

```python
import functools

import jax
import jax.numpy as jnp
from jax import lax
from jax.experimental import pallas as pl
from jax.experimental.pallas import tpu as pltpu
from jax.sharding import PartitionSpec as P

F32 = jnp.float32
BF16 = jnp.bfloat16
VMEM_BYTES = 12 * 2**20
LOAD = 0.5
VM = pl.BlockSpec(memory_space=pltpu.VMEM)
SM = pl.BlockSpec(memory_space=pltpu.SMEM)
ANY = pl.BlockSpec(memory_space=pl.ANY)
HBM = pl.BlockSpec(memory_space=pltpu.HBM)


def call(body, outs, in_specs, scratch=(), out_specs=None, flops=0, vmem=VMEM_BYTES):
    if out_specs is None:
        out_specs = jax.tree.map(lambda _: VM, outs)
    inner = body.func if isinstance(body, functools.partial) else body
    return pl.pallas_call(
        body,
        name=inner.__name__,
        out_shape=outs,
        in_specs=in_specs,
        out_specs=out_specs,
        scratch_shapes=scratch,
        compiler_params=pltpu.CompilerParams(vmem_limit_bytes=vmem),
        cost_estimate=pl.CostEstimate(flops=int(flops), bytes_accessed=0, transcendentals=0),
    )


def dot(a, b):
    return jnp.dot(a, b, preferred_element_type=F32)


def aligned(start, unit):
    return start if isinstance(start, int) else pl.multiple_of(start, unit)


def normed(hf, gain):
    meansq = jnp.mean(hf * hf, axis=-1, keepdims=True)
    return (hf * lax.rsqrt(meansq + 1e-05) * gain).astype(BF16)


def stepped(h, z):
    half = 0.5 * z
    return (h.astype(F32) + half + half * jnp.tanh(half)).astype(BF16)


def start_one(choices, dst, sem):
    for condition, source in choices:

        @pl.when(condition)
        def _():
            pltpu.make_async_copy(source, dst, sem).start()

    return pltpu.make_async_copy(choices[0][1], dst, sem)


def source_of(seg, section, half):
    near, far = 1 + half, 2 - half
    via = seg ^ far
    passed = jnp.logical_or(via == 1, via == 2)
    second = jnp.where(passed, seg ^ 3, via)
    return jnp.where(seg == section, 0, jnp.where((seg ^ near) == section, 1, jnp.where(second == section, 2, 3)))


def fetch_half(seg, core, section, half, own, mine, theirs, dst, sem):
    width = dst.shape[1]
    source = source_of(seg, section, half)
    choices = [(source == 0, own.at[pl.ds(half * width, width), :])]
    for here, refs in ((core == half, mine), (core != half, theirs)):
        for i, ref in enumerate(refs):
            choices.append((jnp.logical_and(here, source == i + 1), ref.at[pl.ds(0, width), :]))
    return [start_one(choices, dst, sem)]


def fetch_cross(seg, core, section, own, mine, dst, sems):
    tile = dst.shape[0]
    width = dst.shape[1]
    blocks = own.shape[0]
    source = jnp.where(core == 0, source_of(seg, section, 0), source_of(seg, section, 1))
    for i, ref in enumerate(mine):

        @pl.when(source == i + 1)
        def _():
            for b in range(blocks):
                part = ref.at[pl.ds(width, tile), pl.ds(b * tile, tile)]
                pltpu.make_async_copy(part, dst.at[:, pl.ds(b * tile, tile)], sems.at[b]).start()

    @pl.when(source == 0)
    def _():
        for b in range(blocks):
            pltpu.make_async_copy(own.at[b], dst.at[:, pl.ds(b * tile, tile)], sems.at[b]).start()

    return [pltpu.make_async_copy(own.at[b], dst.at[:, pl.ds(b * tile, tile)], sems.at[b]) for b in range(blocks)]


def fetch_layer(section, step, ids, cands, top, bottom, cross, sems):
    own, own_cross, mine, theirs = cands
    seg, core = ids[0], ids[1]
    return (
        fetch_half(seg, core, section, 0, own.at[step], mine, theirs, top, sems.at[0])
        + fetch_half(seg, core, section, 1, own.at[step], mine, theirs, bottom, sems.at[1])
        + fetch_cross(seg, core, section, own_cross.at[step], mine, cross, sems.at[pl.ds(2, own_cross.shape[1])])
    )


def cands_of(refs):
    n = (len(refs) - 2) // 2
    return refs[0], refs[1], refs[2 : 2 + n], refs[2 + n :]


def first_kernel(dep, ids, cols, counts, feat_ref, tiles_ref, s0, s1, s2, s3, h_ref, adj_ref, x_ref, sent_ref, small_ref, pick_ref, sem):
    nblk, slots, tile, _ = tiles_ref.shape
    nodes, width = h_ref.shape
    seg = ids[0]
    copy = pltpu.make_async_copy(feat_ref.at[seg], h_ref, sem)
    copy.start()
    for r in range(nblk):
        for j in range(nblk):
            total = jnp.zeros((tile, tile), F32)
            for k in range(slots):
                used = jnp.logical_and(k < counts[r], cols[r, k] == j)
                total = total + jnp.where(used, tiles_ref[r, k].astype(F32), 0.0)
            adj_ref[r * tile : (r + 1) * tile, j * tile : (j + 1) * tile] = total.astype(BF16)
    for r, ref in enumerate((s0, s1, s2, s3)):
        small_ref[seg ^ r] = ref[...]
    sections, steps = small_ref.shape[:2]
    bound = small_ref.shape[2] - 2 * width
    for k in range(sections):
        for p in range(steps):
            rows = small_ref[k, p : p + 1, 2 * width :]
            index = lax.broadcasted_iota(jnp.int32, (nodes, bound), 0).astype(F32)
            pick_ref[k, p] = jnp.where(index == rows, 1.0, 0.0).T.astype(BF16)
    copy.wait()
    x = normed(h_ref[...].astype(F32), small_ref[0, 0:1, width : 2 * width])
    x_ref[...] = x
    sent_ref[...] = dot(pick_ref[0, 0], x).astype(BF16)


def payload_kernel(own, cross, *refs):
    outs, sems = refs[:-1], refs[-1]
    copies = []
    for p, out_ref in enumerate(outs):
        width = out_ref.shape[1]
        tile = cross.shape[-1]
        copies.append(pltpu.make_async_copy(own.at[p], out_ref.at[pl.ds(0, width), :], sems.at[p, 0]))
        for b in range(cross.shape[1]):
            dst = out_ref.at[pl.ds(width, tile), pl.ds(b * tile, tile)]
            copies.append(pltpu.make_async_copy(cross.at[p, b], dst, sems.at[p, b + 1]))
    for copy in copies:
        copy.start()
    for copy in copies:
        copy.wait()


def select_kernel(wanted, ids, *refs):
    count = len(wanted)
    outs, sources = refs[-count:], refs
    rows = sources[0].shape[0]
    for out_ref, rule in zip(outs, wanted):
        if out_ref.shape[0] > rows:
            out_ref[rows:, :] = jnp.zeros((out_ref.shape[0] - rows, out_ref.shape[1]), out_ref.dtype)
        for i, segments in enumerate(rule):
            here = functools.reduce(jnp.logical_or, [ids[0] == s for s in segments])

            @pl.when(here)
            def _():
                out_ref[:rows, :] = sources[i][...]


def select(ids, sources, wanted, deps=(), extra=0):
    rows, columns = sources[0].shape
    shape = jax.ShapeDtypeStruct((rows + extra, columns), sources[0].dtype)
    specs = [SM] + [VM] * len(sources) + [ANY] * len(deps)
    return call(functools.partial(select_kernel, wanted), [shape] * len(wanted), specs, vmem=8 * 2**20)(ids, *sources, *deps)


def tie(value, *deps):
    return pl.pallas_call(
        lambda *refs: None,
        name="tie",
        out_shape=jax.ShapeDtypeStruct(value.shape, value.dtype),
        in_specs=[ANY] * (1 + len(deps)),
        out_specs=ANY,
        input_output_aliases={0: 0},
        compiler_params=pltpu.CompilerParams(vmem_limit_bytes=2**20),
    )(value, *deps)


def top_kernel(dep, in_ref, out_ref):
    out_ref[...] = in_ref[: out_ref.shape[0], :]


def load_kernel(section, ids, dep, *refs):
    w_ref, c_ref, sems = refs[-3:]
    width = w_ref.shape[1]
    parts = w_ref.at[pl.ds(0, width), :], w_ref.at[pl.ds(width, width), :]
    for copy in fetch_layer(section, 0, ids, cands_of(refs[:-3]), *parts, c_ref, sems):
        copy.wait()


def edge_kernel(section, x_ref, h_ref, adj_ref, w_ref, c_ref, small_ref, pick_ref, agg_ref, z_ref, cross_ref, h_out):
    width = x_ref.shape[1]
    pick = pick_ref[section, 1]
    x = x_ref[...]
    adj = dot(pick, adj_ref[...]).astype(BF16)
    agg_ref[...] = dot(adj, x)
    xb = dot(pick, x).astype(BF16)
    z_ref[...] = dot(xb, w_ref[:width, :]) + small_ref[section, 0:1, :width]
    tile = c_ref.shape[0]
    cross = jnp.zeros((pick.shape[0], tile), F32)
    for b in range(c_ref.shape[1] // tile):
        lanes = slice(b * tile, (b + 1) * tile)
        cross = cross + dot(pick[:, lanes], c_ref[:, lanes])
    cross_ref[...] = cross.astype(BF16)
    h_out[...] = dot(pick, h_ref[...]).astype(BF16)


def send_kernel(section, recv_ref, agg_ref, z_ref, cross_ref, h_ref, w_ref, small_ref, sent_ref):
    width = h_ref.shape[1]
    agg = (agg_ref[...] + dot(cross_ref[...], recv_ref[...])).astype(BF16)
    z = z_ref[...] + dot(agg, w_ref[width:, :])
    h = stepped(h_ref[...], z)
    sent_ref[...] = normed(h.astype(F32), small_ref[section, 1:2, width : 2 * width])


def remote(c_ref, recv, i, block):
    tile = c_ref.shape[0]
    parts = []
    for b in range(block // tile):
        lanes = pl.ds(aligned(i * block + b * tile, tile), tile)
        parts.append(dot(c_ref[:, lanes], recv))
    return jnp.concatenate(parts, axis=0)


def even_kernel(section, x_ref, h_ref, adj_ref, recv_ref, w_ref, c_ref, small_ref, dep, h_out, x_out):
    nodes, width = x_ref.shape
    block = 256

    def even(i, carry):
        rows = pl.ds(aligned(i * block, block), block)
        agg = dot(adj_ref[rows, :], x_ref[...]) + remote(c_ref, recv_ref[...], i, block)
        z = dot(x_ref[rows, :], w_ref[:width, :]) + small_ref[section, 0:1, :width]
        z = z + dot(agg.astype(BF16), w_ref[width:, :])
        h = stepped(h_ref[rows, :], z)
        h_out[rows, :] = h
        x_out[rows, :] = normed(h.astype(F32), small_ref[section, 1:2, width : 2 * width])
        return carry

    lax.fori_loop(0, nodes // block, even, 0)


def odd_kernel(section, fetch, ids, dep, x_ref, adj_ref, small_ref, *refs):
    if fetch:
        z_out, w2_out, c_out, w_out, next_c_out, w1_ref, sems, next_sems = refs[-8:]
        cands, ahead = refs[: fetch], refs[fetch:-8]
    else:
        z_out, w2_out, c_out, w1_ref, sems = refs[-5:]
        cands = refs[:-5]
    nodes, width = x_ref.shape
    block = 256
    copies = fetch_layer(section, 1, ids, cands_of(cands), w1_ref, w2_out, c_out, sems)
    if fetch:
        parts = w_out.at[pl.ds(0, width), :], w_out.at[pl.ds(width, width), :]
        copies += fetch_layer(section + 1, 0, ids, cands_of(ahead), *parts, next_c_out, next_sems)
    copies[0].wait()
    copies[1].wait()

    def odd(i, carry):
        rows = pl.ds(aligned(i * block, block), block)
        agg = dot(adj_ref[rows, :], x_ref[...]).astype(BF16)
        z = dot(x_ref[rows, :], w1_ref[...]) + small_ref[section, 1:2, :width]
        z_out[rows, :] = z + dot(agg, w2_out[...])
        return carry

    lax.fori_loop(0, nodes // block, odd, 0)
    for copy in copies[2:]:
        copy.wait()


def finish_kernel(section, last, ids, recv_ref, z_ref, w2_ref, c_ref, h_ref, small_ref, pick_ref, *refs):
    nodes, width = h_ref.shape
    block = 256
    if last:
        ends, (h_out, *pays) = refs[:section], refs[section:]
        for k, end_ref in enumerate(ends):
            for r, pay_ref in enumerate(pays, 1):

                @pl.when(ids[0] == k ^ r)
                def _():
                    pay_ref[:nodes, :] = end_ref[...]

        for pay_ref in pays:
            pay_ref[nodes:, :] = jnp.zeros((pay_ref.shape[0] - nodes, width), BF16)
    else:
        h_out, x_out, sent_out = refs
    seen = dot(recv_ref[...], w2_ref[...]).astype(BF16)
    for i in range(nodes // block):
        rows = pl.ds(i * block, block)
        z = z_ref[rows, :] + remote(c_ref, seen, i, block)
        h = stepped(h_ref[rows, :], z)
        h_out[rows, :] = h
        if last:
            for r, pay_ref in enumerate(pays, 1):

                @pl.when(ids[0] == section ^ r)
                def _():
                    pay_ref[rows, :] = h
        else:
            x_out[rows, :] = normed(h.astype(F32), small_ref[section + 1, 0:1, width : 2 * width])
    if not last:
        sent_out[...] = dot(pick_ref[section + 1, 0], x_out[...]).astype(BF16)


def collect_early_kernel(ids, *refs):
    out_ref, sem = refs[-2:]
    start_one([(ids[0] == k, end) for k, end in enumerate(refs[:-2])], out_ref.at[0, ids[0]], sem).wait()


def collect_last_kernel(ids, one_ref, two_ref, three_ref, first_ref, early_ref, later_ref, _, out_ref, sems):
    last = out_ref.shape[1] - 1
    rows = pl.ds(0, out_ref.shape[2])
    copies = [
        pltpu.make_async_copy(ref.at[rows, :], out_ref.at[0, ids[0] ^ r], sems.at[r]) for r, ref in ((1, one_ref), (2, two_ref))
    ]
    for copy in copies:
        copy.start()
    choices = [
        (ids[0] == last, three_ref),
        (ids[0] < 2, first_ref.at[rows, :]),
        (jnp.logical_and(ids[0] == 2, ids[1] == 0), early_ref.at[rows, :]),
        (jnp.logical_and(ids[0] == 2, ids[1] != 0), later_ref.at[rows, :]),
    ]
    copies.append(start_one(choices, out_ref.at[0, ids[0] ^ 3], sems.at[3]))
    for copy in copies:
        copy.wait()


def shards(features, weights, bias, gain, tile_val, tile_col, tile_count, cross_val, send_rows):
    sections = lax.axis_size("segment")
    doms = lax.axis_size("dom")
    seg = lax.axis_index("segment")
    core = lax.axis_index("dom") & 1
    steps, _, width = weights.shape
    nodes = features.shape[1]
    bound = send_rows.shape[1]
    nbits = doms.bit_length() - 1
    ids = jnp.stack([seg, core]).astype(jnp.int32)

    def moved(value, target, sources=range(sections)):
        pairs = []
        for s in sources:
            for d in range(doms):
                t, e = target(s, d)
                pairs.append((s * doms + d, t * doms + e))
        return lax.ppermute(value, ("segment", "dom"), pairs)

    def near(s, d):
        return s ^ (1 + (d & 1)), d

    def far(s, d):
        return s ^ (2 - (d & 1)), d

    def sibling(s, d):
        return s, d ^ 1

    def across(r):
        return lambda s, d: (s ^ r, d)

    def exchange(sent, step):
        bit = step * (nbits - 1) // max(steps - 1, 1)
        return lax.ppermute(sent, "dom", [(i, i ^ 1 << bit) for i in range(doms)])

    mat = jax.ShapeDtypeStruct((nodes, width), BF16)
    mat32 = jax.ShapeDtypeStruct((nodes, width), F32)
    tall = jax.ShapeDtypeStruct((nodes + 32, width), BF16)
    edge = jax.ShapeDtypeStruct((bound, width), BF16)
    edge32 = jax.ShapeDtypeStruct((bound, width), F32)
    half = jax.ShapeDtypeStruct((width, width), BF16)
    both = jax.ShapeDtypeStruct((2 * width, width), BF16)
    load = jax.ShapeDtypeStruct((width + bound, width), BF16)
    picks = jax.ShapeDtypeStruct((sections, steps, bound, nodes), BF16)
    unit = 2 * nodes * width * width
    dmas = pltpu.SemaphoreType.DMA((2 + cross_val.shape[1],))

    own = call(
        payload_kernel,
        [load] * steps,
        [ANY, ANY],
        scratch=[pltpu.SemaphoreType.DMA((steps, 1 + cross_val.shape[1]))],
    )(lax.dynamic_slice_in_dim(weights, core * width, width, axis=1), cross_val)
    small = tie(jnp.concatenate([bias, gain, send_rows.astype(F32)], axis=1), own[0])
    smalls = [small] + [moved(small, across(r)) for r in range(1, sections)]
    inner, outer = (1, 2), (0, 3)
    a0, a1 = [moved(v, near) for v in own]
    (pay,) = select(ids, [a0, own[0]], [(inner, outer)])
    b0 = moved(pay, far)
    (pay,) = select(ids, [a1, own[1]], [(inner, outer)], [pay, *smalls[1:]])
    b1 = moved(pay, far)
    issued = pay
    (pay,) = select(ids, [own[0], a0], [(inner, outer)], [pay])
    c0 = moved(pay, far)
    (pay,) = select(ids, [own[1], a1], [(inner, outer)], [pay])
    c1 = moved(pay, far)
    h, adj, x, sent, small, pick = call(
        first_kernel,
        (mat, jax.ShapeDtypeStruct((nodes, nodes), BF16), mat, edge, jax.ShapeDtypeStruct((sections,) + small.shape, F32), picks),
        [ANY, SM, SM, SM, HBM, VM] + [VM] * sections,
        scratch=[pltpu.SemaphoreType.DMA],
    )(issued, ids, tile_col, tile_count, features, tile_val, *smalls)
    recv = exchange(sent, 0)

    sa0 = moved(call(top_kernel, half, [ANY, VM])(issued, a0), sibling)
    sb0 = moved(call(top_kernel, half, [ANY, VM])(issued, b0), sibling)
    brought, swapped = [[a0, b0], [a1]], [[sa0, sb0], []]

    def candidates(p):
        return [weights, cross_val, *brought[p], *swapped[p]]

    def loaded(section, dep):
        cands = candidates(0)
        specs = [SM, ANY, HBM, HBM] + [ANY] * (len(cands) - 2)
        kernel = functools.partial(load_kernel, section)
        return call(kernel, (both, edge), specs, scratch=[dmas])(ids, dep, *cands)

    w, c = loaded(0, pay)

    ends = []
    last_segment = sections - 1
    for k in range(sections):
        last = k == sections - 1
        if k > 0:
            recv = exchange(sent, 0)
        if k == 1:
            c1 = tie(c1, x)
            w, c = loaded(1, c1)
        edges = call(
            functools.partial(edge_kernel, k),
            (edge32, edge32, jax.ShapeDtypeStruct((bound, bound), BF16), edge),
            [VM] * 7,
            flops=LOAD * unit / 4,
        )(x, h, adj, w, c, small, pick)
        sent = call(functools.partial(send_kernel, k), edge, [VM] * 7, flops=LOAD * unit / 4)(recv, *edges[:3], edges[3], w, small)
        recv2 = exchange(sent, 1)
        if k == 1:
            brought[1].append(c1)
            swapped[1].append(moved(brought[1][2], sibling))
        h, x = call(functools.partial(even_kernel, k), (mat, mat), [VM] * 7 + [ANY], flops=LOAD * unit)(
            x, h, adj, recv, w, c, small, sent
        )
        if k == 0:
            brought[1] = [tie(a1, sent), tie(b1, sent)]
            swapped[1] = [moved(v, sibling) for v in brought[1]]
        cands = candidates(1)
        ahead = candidates(0) if k in range(1, sections - 1) else []
        fetch = len(cands) if ahead else 0
        specs = [([HBM, HBM] + [ANY] * (len(v) - 2) if v else []) for v in (cands, ahead)]
        z, w2, c2, *loads = call(
            functools.partial(odd_kernel, k, fetch),
            (mat32, half, edge) + ((both, edge) if ahead else ()),
            [SM, ANY] + [VM] * 3 + specs[0] + specs[1],
            scratch=[pltpu.VMEM((width, width), BF16), dmas] + ([dmas] if ahead else []),
            flops=(20 if k > 1 else LOAD) * unit,
        )(ids, c0 if k == 0 else first_two if last else x, x, adj, small, *cands, *ahead)
        if k == 0:
            brought[0].append(tie(c0, recv2, z))
            swapped[0].append(moved(brought[0][2], sibling))
        if k == 2:
            (pay,) = select(ids, ends, [[(j ^ 3,) for j in range(2)]], [x], extra=16)
            first_two = moved(pay, across(3), [j ^ 3 for j in range(2)])
        if last:
            (pay,) = select(ids, ends[2:], [[(2 ^ 3,)]], [x], extra=16)
            others = [2 ^ 3]
            early = moved(pay, lambda s, d: (s ^ (2 if d & 1 else 3), d), others)
        out = call(
            functools.partial(finish_kernel, k, last),
            (mat, tall, tall) if last else (mat, mat, edge),
            [SM] + [VM] * 7 + ([VM] * len(ends) if last else []),
            flops=LOAD * unit,
        )(ids, recv2, z, w2, c2, h, small, pick, *(ends if last else []))
        ends.append(out[0])
        if not last:
            h, x, sent = out
        if ahead:
            w, c = loads
    hop = moved(ends[-1], near, [last_segment ^ 3])
    two = moved(out[2], across(2))
    one = moved(out[1], across(1))
    def onward(value, between, sources, parity=None):
        pairs = []
        for s in sources:
            for d in range(doms):
                if parity is None or d & 1 == parity:
                    pairs.append((between(s, d) * doms + d, (s ^ 3) * doms + d))
        return lax.ppermute(value, ("segment", "dom"), pairs)

    three = onward(tie(hop, early), lambda s, d: near(s, d)[0], [last_segment ^ 3])
    later = onward(early, lambda s, d: s ^ 2, others, 1)
    whole = jax.ShapeDtypeStruct((1, sections, nodes, width), BF16)
    sems = [pltpu.SemaphoreType.DMA((sections,))]
    partly = call(
        collect_early_kernel, whole, [SM] + [ANY] * sections, scratch=[pltpu.SemaphoreType.DMA], out_specs=ANY
    )(ids, *ends)
    return pl.pallas_call(
        collect_last_kernel,
        name="collect_last_kernel",
        out_shape=whole,
        in_specs=[SM] + [ANY] * 7,
        out_specs=ANY,
        scratch_shapes=sems,
        input_output_aliases={7: 0},
        compiler_params=pltpu.CompilerParams(vmem_limit_bytes=2**20),
    )(ids, one, two, three, first_two, early, later, partly)


def solution(mesh):
    in_specs = (
        P(None, "dom", None),
        P("segment", None, None),
        P("segment", None),
        P("segment", None),
        P("dom", None, None, None),
        P("dom", None),
        P("dom"),
        P("segment", "dom", None, None),
        P("segment", "dom"),
    )
    out_specs = P("segment", None, "dom", None)
    return jax.shard_map(shards, mesh=mesh, in_specs=in_specs, out_specs=out_specs, check_vma=False)
```

```python
import functools

import jax
import jax.numpy as jnp
from jax import lax
from jax.experimental import pallas as pl
from jax.experimental.pallas import tpu as pltpu
from jax.sharding import PartitionSpec as P

F32 = jnp.float32
BF16 = jnp.bfloat16
VMEM_BYTES = 12 * 2**20
LOAD = 0.5
VM = pl.BlockSpec(memory_space=pltpu.VMEM)
SM = pl.BlockSpec(memory_space=pltpu.SMEM)
ANY = pl.BlockSpec(memory_space=pl.ANY)
HBM = pl.BlockSpec(memory_space=pltpu.HBM)


def call(body, outs, in_specs, scratch=(), out_specs=None, flops=0, vmem=VMEM_BYTES):
    if out_specs is None:
        out_specs = jax.tree.map(lambda _: VM, outs)
    inner = body.func if isinstance(body, functools.partial) else body
    return pl.pallas_call(
        body,
        name=inner.__name__,
        out_shape=outs,
        in_specs=in_specs,
        out_specs=out_specs,
        scratch_shapes=scratch,
        compiler_params=pltpu.CompilerParams(vmem_limit_bytes=vmem),
        cost_estimate=pl.CostEstimate(flops=int(flops), bytes_accessed=0, transcendentals=0),
    )


def position():
    return lax.axis_index("segment"), lax.axis_index("dom") & 1


def dot(a, b):
    return jnp.dot(a, b, preferred_element_type=F32)


def aligned(start, unit):
    return start if isinstance(start, int) else pl.multiple_of(start, unit)


def normed(hf, gain):
    meansq = jnp.mean(hf * hf, axis=-1, keepdims=True)
    return (hf * lax.rsqrt(meansq + 1e-05) * gain).astype(BF16)


def stepped(h, z):
    half = 0.5 * z
    return (h.astype(F32) + half + half * jnp.tanh(half)).astype(BF16)


def start_one(choices, dst, sem):
    for condition, source in choices:

        @pl.when(condition)
        def _():
            pltpu.make_async_copy(source, dst, sem).start()

    return pltpu.make_async_copy(choices[0][1], dst, sem)


def source_of(seg, section, half):
    near, far = 1 + half, 2 - half
    via = seg ^ far
    passed = jnp.logical_or(via == 1, via == 2)
    second = jnp.where(passed, seg ^ 3, via)
    return jnp.where(seg == section, 0, jnp.where((seg ^ near) == section, 1, jnp.where(second == section, 2, 3)))


def fetch_half(seg, core, section, half, own, mine, theirs, dst, sem):
    width = dst.shape[1]
    source = source_of(seg, section, half)
    choices = [(source == 0, own.at[pl.ds(half * width, width), :])]
    for here, refs in ((core == half, mine), (core != half, theirs)):
        for i, ref in enumerate(refs):
            choices.append((jnp.logical_and(here, source == i + 1), ref.at[pl.ds(0, width), :]))
    return [start_one(choices, dst, sem)]


def fetch_cross(seg, core, section, own, mine, dst, sems):
    tile = dst.shape[0]
    width = dst.shape[1]
    blocks = own.shape[0]
    source = jnp.where(core == 0, source_of(seg, section, 0), source_of(seg, section, 1))
    for i, ref in enumerate(mine):

        @pl.when(source == i + 1)
        def _():
            for b in range(blocks):
                part = ref.at[pl.ds(width, tile), pl.ds(b * tile, tile)]
                pltpu.make_async_copy(part, dst.at[:, pl.ds(b * tile, tile)], sems.at[b]).start()

    @pl.when(source == 0)
    def _():
        for b in range(blocks):
            pltpu.make_async_copy(own.at[b], dst.at[:, pl.ds(b * tile, tile)], sems.at[b]).start()

    return [pltpu.make_async_copy(own.at[b], dst.at[:, pl.ds(b * tile, tile)], sems.at[b]) for b in range(blocks)]


def fetch_layer(section, step, ids, cands, top, bottom, cross, sems):
    own, own_cross, mine, theirs = cands
    seg, core = ids[0], ids[1]
    return (
        fetch_half(seg, core, section, 0, own.at[step], mine, theirs, top, sems.at[0])
        + fetch_half(seg, core, section, 1, own.at[step], mine, theirs, bottom, sems.at[1])
        + fetch_cross(seg, core, section, own_cross.at[step], mine, cross, sems.at[pl.ds(2, own_cross.shape[1])])
    )


def cands_of(refs):
    n = (len(refs) - 2) // 2
    return refs[0], refs[1], refs[2 : 2 + n], refs[2 + n :]


def first_kernel(dep, cols, counts, feat_ref, tiles_ref, s0, s1, s2, s3, h_ref, adj_ref, x_ref, sent_ref, small_ref, pick_ref, sem):
    ids = position()
    nblk, slots, tile, _ = tiles_ref.shape
    nodes, width = h_ref.shape
    seg = ids[0]
    copy = pltpu.make_async_copy(feat_ref.at[seg], h_ref, sem)
    copy.start()
    for r in range(nblk):
        for j in range(nblk):
            total = jnp.zeros((tile, tile), F32)
            for k in range(slots):
                used = jnp.logical_and(k < counts[r], cols[r, k] == j)
                total = total + jnp.where(used, tiles_ref[r, k].astype(F32), 0.0)
            adj_ref[r * tile : (r + 1) * tile, j * tile : (j + 1) * tile] = total.astype(BF16)
    for r, ref in enumerate((s0, s1, s2, s3)):
        small_ref[seg ^ r] = ref[...]
    sections, steps = small_ref.shape[:2]
    bound = small_ref.shape[2] - 2 * width
    for k in range(sections):
        for p in range(steps):
            rows = small_ref[k, p : p + 1, 2 * width :]
            index = lax.broadcasted_iota(jnp.int32, (nodes, bound), 0).astype(F32)
            pick_ref[k, p] = jnp.where(index == rows, 1.0, 0.0).T.astype(BF16)
    copy.wait()
    x = normed(h_ref[...].astype(F32), small_ref[0, 0:1, width : 2 * width])
    x_ref[...] = x
    sent_ref[...] = dot(pick_ref[0, 0], x).astype(BF16)


def payload_kernel(own, cross, *refs):
    outs, sems = refs[:-1], refs[-1]
    copies = []
    for p, out_ref in enumerate(outs):
        width = out_ref.shape[1]
        tile = cross.shape[-1]
        copies.append(pltpu.make_async_copy(own.at[p], out_ref.at[pl.ds(0, width), :], sems.at[p, 0]))
        for b in range(cross.shape[1]):
            dst = out_ref.at[pl.ds(width, tile), pl.ds(b * tile, tile)]
            copies.append(pltpu.make_async_copy(cross.at[p, b], dst, sems.at[p, b + 1]))
    for copy in copies:
        copy.start()
    for copy in copies:
        copy.wait()


def select_kernel(wanted, *refs):
    ids = position()
    count = len(wanted)
    outs, sources = refs[-count:], refs
    rows = sources[0].shape[0]
    for out_ref, rule in zip(outs, wanted):
        if out_ref.shape[0] > rows:
            out_ref[rows:, :] = jnp.zeros((out_ref.shape[0] - rows, out_ref.shape[1]), out_ref.dtype)
        for i, segments in enumerate(rule):
            here = functools.reduce(jnp.logical_or, [ids[0] == s for s in segments])

            @pl.when(here)
            def _():
                out_ref[:rows, :] = sources[i][...]


def select(sources, wanted, deps=(), extra=0):
    rows, columns = sources[0].shape
    shape = jax.ShapeDtypeStruct((rows + extra, columns), sources[0].dtype)
    specs = [VM] * len(sources) + [ANY] * len(deps)
    return call(functools.partial(select_kernel, wanted), [shape] * len(wanted), specs, vmem=8 * 2**20)(*sources, *deps)


def tie(value, *deps):
    return pl.pallas_call(
        lambda *refs: None,
        name="tie",
        out_shape=jax.ShapeDtypeStruct(value.shape, value.dtype),
        in_specs=[ANY] * (1 + len(deps)),
        out_specs=ANY,
        input_output_aliases={0: 0},
        compiler_params=pltpu.CompilerParams(vmem_limit_bytes=2**20),
    )(value, *deps)


def top_kernel(dep, in_ref, out_ref):
    out_ref[...] = in_ref[: out_ref.shape[0], :]


def load_kernel(section, dep, *refs):
    ids = position()
    w_ref, c_ref, sems = refs[-3:]
    width = w_ref.shape[1]
    parts = w_ref.at[pl.ds(0, width), :], w_ref.at[pl.ds(width, width), :]
    for copy in fetch_layer(section, 0, ids, cands_of(refs[:-3]), *parts, c_ref, sems):
        copy.wait()


def edge_kernel(section, x_ref, h_ref, adj_ref, w_ref, c_ref, small_ref, pick_ref, agg_ref, z_ref, cross_ref, h_out):
    width = x_ref.shape[1]
    pick = pick_ref[section, 1]
    x = x_ref[...]
    adj = dot(pick, adj_ref[...]).astype(BF16)
    agg_ref[...] = dot(adj, x)
    xb = dot(pick, x).astype(BF16)
    z_ref[...] = dot(xb, w_ref[:width, :]) + small_ref[section, 0:1, :width]
    tile = c_ref.shape[0]
    cross = jnp.zeros((pick.shape[0], tile), F32)
    for b in range(c_ref.shape[1] // tile):
        lanes = slice(b * tile, (b + 1) * tile)
        cross = cross + dot(pick[:, lanes], c_ref[:, lanes])
    cross_ref[...] = cross.astype(BF16)
    h_out[...] = dot(pick, h_ref[...]).astype(BF16)


def send_kernel(section, recv_ref, agg_ref, z_ref, cross_ref, h_ref, w_ref, small_ref, sent_ref):
    width = h_ref.shape[1]
    agg = (agg_ref[...] + dot(cross_ref[...], recv_ref[...])).astype(BF16)
    z = z_ref[...] + dot(agg, w_ref[width:, :])
    h = stepped(h_ref[...], z)
    sent_ref[...] = normed(h.astype(F32), small_ref[section, 1:2, width : 2 * width])


def remote(c_ref, recv, i, block):
    tile = c_ref.shape[0]
    parts = []
    for b in range(block // tile):
        lanes = pl.ds(aligned(i * block + b * tile, tile), tile)
        parts.append(dot(c_ref[:, lanes], recv))
    return jnp.concatenate(parts, axis=0)


def even_kernel(section, x_ref, h_ref, adj_ref, recv_ref, w_ref, c_ref, small_ref, dep, h_out, x_out):
    nodes, width = x_ref.shape
    block = 256

    def even(i, carry):
        rows = pl.ds(aligned(i * block, block), block)
        agg = dot(adj_ref[rows, :], x_ref[...]) + remote(c_ref, recv_ref[...], i, block)
        z = dot(x_ref[rows, :], w_ref[:width, :]) + small_ref[section, 0:1, :width]
        z = z + dot(agg.astype(BF16), w_ref[width:, :])
        h = stepped(h_ref[rows, :], z)
        h_out[rows, :] = h
        x_out[rows, :] = normed(h.astype(F32), small_ref[section, 1:2, width : 2 * width])
        return carry

    lax.fori_loop(0, nodes // block, even, 0)


def odd_kernel(section, fetch, dep, x_ref, adj_ref, small_ref, *refs):
    ids = position()
    if fetch:
        z_out, w2_out, c_out, w_out, next_c_out, w1_ref, sems, next_sems = refs[-8:]
        cands, ahead = refs[: fetch], refs[fetch:-8]
    else:
        z_out, w2_out, c_out, w1_ref, sems = refs[-5:]
        cands = refs[:-5]
    nodes, width = x_ref.shape
    block = 256
    copies = fetch_layer(section, 1, ids, cands_of(cands), w1_ref, w2_out, c_out, sems)
    if fetch:
        parts = w_out.at[pl.ds(0, width), :], w_out.at[pl.ds(width, width), :]
        copies += fetch_layer(section + 1, 0, ids, cands_of(ahead), *parts, next_c_out, next_sems)
    copies[0].wait()
    copies[1].wait()

    def odd(i, carry):
        rows = pl.ds(aligned(i * block, block), block)
        agg = dot(adj_ref[rows, :], x_ref[...]).astype(BF16)
        z = dot(x_ref[rows, :], w1_ref[...]) + small_ref[section, 1:2, :width]
        z_out[rows, :] = z + dot(agg, w2_out[...])
        return carry

    lax.fori_loop(0, nodes // block, odd, 0)
    for copy in copies[2:]:
        copy.wait()


def finish_kernel(section, last, recv_ref, z_ref, w2_ref, c_ref, h_ref, small_ref, pick_ref, *refs):
    nodes, width = h_ref.shape
    block = 256
    ids = position()
    if last:
        ends, (h_out, *pays) = refs[:section], refs[section:]
        for k, end_ref in enumerate(ends):
            for r, pay_ref in enumerate(pays, 1):

                @pl.when(ids[0] == k ^ r)
                def _():
                    pay_ref[:nodes, :] = end_ref[...]

        for pay_ref in pays:
            pay_ref[nodes:, :] = jnp.zeros((pay_ref.shape[0] - nodes, width), BF16)
    else:
        h_out, x_out, sent_out = refs
    seen = dot(recv_ref[...], w2_ref[...]).astype(BF16)
    for i in range(nodes // block):
        rows = pl.ds(i * block, block)
        z = z_ref[rows, :] + remote(c_ref, seen, i, block)
        h = stepped(h_ref[rows, :], z)
        h_out[rows, :] = h
        if last:
            for r, pay_ref in enumerate(pays, 1):

                @pl.when(ids[0] == section ^ r)
                def _():
                    pay_ref[rows, :] = h
        else:
            x_out[rows, :] = normed(h.astype(F32), small_ref[section + 1, 0:1, width : 2 * width])
    if not last:
        sent_out[...] = dot(pick_ref[section + 1, 0], x_out[...]).astype(BF16)


def collect_early_kernel(*refs):
    ids = position()
    out_ref, sem = refs[-2:]
    start_one([(ids[0] == k, end) for k, end in enumerate(refs[:-2])], out_ref.at[0, ids[0]], sem).wait()


def collect_last_kernel(one_ref, two_ref, three_ref, first_ref, early_ref, later_ref, _, out_ref, sems):
    ids = position()
    last = out_ref.shape[1] - 1
    rows = pl.ds(0, out_ref.shape[2])
    copies = [
        pltpu.make_async_copy(ref.at[rows, :], out_ref.at[0, ids[0] ^ r], sems.at[r]) for r, ref in ((1, one_ref), (2, two_ref))
    ]
    for copy in copies:
        copy.start()
    choices = [
        (ids[0] == last, three_ref),
        (ids[0] < 2, first_ref.at[rows, :]),
        (jnp.logical_and(ids[0] == 2, ids[1] == 0), early_ref.at[rows, :]),
        (jnp.logical_and(ids[0] == 2, ids[1] != 0), later_ref.at[rows, :]),
    ]
    copies.append(start_one(choices, out_ref.at[0, ids[0] ^ 3], sems.at[3]))
    for copy in copies:
        copy.wait()


def shards(features, weights, bias, gain, tile_val, tile_col, tile_count, cross_val, send_rows):
    sections = lax.axis_size("segment")
    doms = lax.axis_size("dom")
    seg = lax.axis_index("segment")
    core = lax.axis_index("dom") & 1
    steps, _, width = weights.shape
    nodes = features.shape[1]
    bound = send_rows.shape[1]
    nbits = doms.bit_length() - 1

    def moved(value, target, sources=range(sections)):
        pairs = []
        for s in sources:
            for d in range(doms):
                t, e = target(s, d)
                pairs.append((s * doms + d, t * doms + e))
        return lax.ppermute(value, ("segment", "dom"), pairs)

    def near(s, d):
        return s ^ (1 + (d & 1)), d

    def far(s, d):
        return s ^ (2 - (d & 1)), d

    def sibling(s, d):
        return s, d ^ 1

    def across(r):
        return lambda s, d: (s ^ r, d)

    def exchange(sent, step):
        bit = step * (nbits - 1) // max(steps - 1, 1)
        return lax.ppermute(sent, "dom", [(i, i ^ 1 << bit) for i in range(doms)])

    mat = jax.ShapeDtypeStruct((nodes, width), BF16)
    mat32 = jax.ShapeDtypeStruct((nodes, width), F32)
    tall = jax.ShapeDtypeStruct((nodes + 32, width), BF16)
    edge = jax.ShapeDtypeStruct((bound, width), BF16)
    edge32 = jax.ShapeDtypeStruct((bound, width), F32)
    half = jax.ShapeDtypeStruct((width, width), BF16)
    both = jax.ShapeDtypeStruct((2 * width, width), BF16)
    load = jax.ShapeDtypeStruct((width + bound, width), BF16)
    picks = jax.ShapeDtypeStruct((sections, steps, bound, nodes), BF16)
    unit = 2 * nodes * width * width
    dmas = pltpu.SemaphoreType.DMA((2 + cross_val.shape[1],))

    own = call(
        payload_kernel,
        [load] * steps,
        [ANY, ANY],
        scratch=[pltpu.SemaphoreType.DMA((steps, 1 + cross_val.shape[1]))],
    )(lax.dynamic_slice_in_dim(weights, core * width, width, axis=1), cross_val)
    small = tie(jnp.concatenate([bias, gain, send_rows.astype(F32)], axis=1), own[0])
    smalls = [small] + [moved(small, across(r)) for r in range(1, sections)]
    inner, outer = (1, 2), (0, 3)
    a0, a1 = [moved(v, near) for v in own]
    (pay,) = select([a0, own[0]], [(inner, outer)])
    b0 = moved(pay, far)
    (pay,) = select([a1, own[1]], [(inner, outer)], [pay, *smalls[1:]])
    b1 = moved(pay, far)
    issued = pay
    (pay,) = select([own[0], a0], [(inner, outer)], [pay])
    c0 = moved(pay, far)
    (pay,) = select([own[1], a1], [(inner, outer)], [pay])
    c1 = moved(pay, far)
    h, adj, x, sent, small, pick = call(
        first_kernel,
        (mat, jax.ShapeDtypeStruct((nodes, nodes), BF16), mat, edge, jax.ShapeDtypeStruct((sections,) + small.shape, F32), picks),
        [ANY, SM, SM, HBM, VM] + [VM] * sections,
        scratch=[pltpu.SemaphoreType.DMA],
    )(issued, tile_col, tile_count, features, tile_val, *smalls)
    recv = exchange(sent, 0)

    sa0 = moved(call(top_kernel, half, [ANY, VM])(issued, a0), sibling)
    sb0 = moved(call(top_kernel, half, [ANY, VM])(issued, b0), sibling)
    brought, swapped = [[a0, b0], [a1]], [[sa0, sb0], []]

    def candidates(p):
        return [weights, cross_val, *brought[p], *swapped[p]]

    def loaded(section, dep):
        cands = candidates(0)
        specs = [ANY, HBM, HBM] + [ANY] * (len(cands) - 2)
        kernel = functools.partial(load_kernel, section)
        return call(kernel, (both, edge), specs, scratch=[dmas])(dep, *cands)

    w, c = loaded(0, pay)

    ends = []
    last_segment = sections - 1
    for k in range(sections):
        last = k == sections - 1
        if k > 0:
            recv = exchange(sent, 0)
        if k == 1:
            c1 = tie(c1, x)
            w, c = loaded(1, c1)
        edges = call(
            functools.partial(edge_kernel, k),
            (edge32, edge32, jax.ShapeDtypeStruct((bound, bound), BF16), edge),
            [VM] * 7,
            flops=LOAD * unit / 4,
        )(x, h, adj, w, c, small, pick)
        sent = call(functools.partial(send_kernel, k), edge, [VM] * 7, flops=LOAD * unit / 4)(recv, *edges[:3], edges[3], w, small)
        recv2 = exchange(sent, 1)
        if k == 1:
            brought[1].append(c1)
            swapped[1].append(moved(brought[1][2], sibling))
        h, x = call(functools.partial(even_kernel, k), (mat, mat), [VM] * 7 + [ANY], flops=LOAD * unit)(
            x, h, adj, recv, w, c, small, sent
        )
        if k == 0:
            brought[1] = [tie(a1, sent), tie(b1, sent)]
            swapped[1] = [moved(v, sibling) for v in brought[1]]
        cands = candidates(1)
        ahead = candidates(0) if k in range(1, sections - 1) else []
        fetch = len(cands) if ahead else 0
        specs = [([HBM, HBM] + [ANY] * (len(v) - 2) if v else []) for v in (cands, ahead)]
        z, w2, c2, *loads = call(
            functools.partial(odd_kernel, k, fetch),
            (mat32, half, edge) + ((both, edge) if ahead else ()),
            [ANY] + [VM] * 3 + specs[0] + specs[1],
            scratch=[pltpu.VMEM((width, width), BF16), dmas] + ([dmas] if ahead else []),
            flops=(20 if k > 1 else LOAD) * unit,
        )(c0 if k == 0 else first_two if last else x, x, adj, small, *cands, *ahead)
        if k == 0:
            brought[0].append(tie(c0, recv2, z))
            swapped[0].append(moved(brought[0][2], sibling))
        if k == 2:
            (pay,) = select(ends, [[(j ^ 3,) for j in range(2)]], [x], extra=16)
            first_two = moved(pay, across(3), [j ^ 3 for j in range(2)])
        if last:
            (pay,) = select(ends[2:], [[(2 ^ 3,)]], [x], extra=16)
            others = [2 ^ 3]
            early = moved(pay, lambda s, d: (s ^ (2 if d & 1 else 3), d), others)
        out = call(
            functools.partial(finish_kernel, k, last),
            (mat, tall, tall) if last else (mat, mat, edge),
            [VM] * 7 + ([VM] * len(ends) if last else []),
            flops=LOAD * unit,
        )(recv2, z, w2, c2, h, small, pick, *(ends if last else []))
        ends.append(out[0])
        if not last:
            h, x, sent = out
        if ahead:
            w, c = loads
    hop = moved(ends[-1], near, [last_segment ^ 3])
    two = moved(out[2], across(2))
    one = moved(out[1], across(1))
    def onward(value, between, sources, parity=None):
        pairs = []
        for s in sources:
            for d in range(doms):
                if parity is None or d & 1 == parity:
                    pairs.append((between(s, d) * doms + d, (s ^ 3) * doms + d))
        return lax.ppermute(value, ("segment", "dom"), pairs)

    three = onward(tie(hop, early), lambda s, d: near(s, d)[0], [last_segment ^ 3])
    later = onward(early, lambda s, d: s ^ 2, others, 1)
    whole = jax.ShapeDtypeStruct((1, sections, nodes, width), BF16)
    sems = [pltpu.SemaphoreType.DMA((sections,))]
    partly = call(
        collect_early_kernel, whole, [ANY] * sections, scratch=[pltpu.SemaphoreType.DMA], out_specs=ANY
    )(*ends)
    return pl.pallas_call(
        collect_last_kernel,
        name="collect_last_kernel",
        out_shape=whole,
        in_specs=[ANY] * 7,
        out_specs=ANY,
        scratch_shapes=sems,
        input_output_aliases={6: 0},
        compiler_params=pltpu.CompilerParams(vmem_limit_bytes=2**20),
    )(one, two, three, first_two, early, later, partly)


def solution(mesh):
    in_specs = (
        P(None, "dom", None),
        P("segment", None, None),
        P("segment", None),
        P("segment", None),
        P("dom", None, None, None),
        P("dom", None),
        P("dom"),
        P("segment", "dom", None, None),
        P("segment", "dom"),
    )
    out_specs = P("segment", None, "dom", None)
    return jax.shard_map(shards, mesh=mesh, in_specs=in_specs, out_specs=out_specs, check_vma=False)
```

```python
import functools

import jax
import jax.numpy as jnp
from jax import lax
from jax.experimental import pallas as pl
from jax.experimental.pallas import tpu as pltpu
from jax.sharding import PartitionSpec as P

F32 = jnp.float32
BF16 = jnp.bfloat16
VMEM_BYTES = 12 * 2**20
LOAD = 0.5
VM = pl.BlockSpec(memory_space=pltpu.VMEM)
SM = pl.BlockSpec(memory_space=pltpu.SMEM)
ANY = pl.BlockSpec(memory_space=pl.ANY)
HBM = pl.BlockSpec(memory_space=pltpu.HBM)


def call(body, outs, in_specs, scratch=(), out_specs=None, flops=0, vmem=VMEM_BYTES):
    if out_specs is None:
        out_specs = jax.tree.map(lambda _: VM, outs)
    inner = body.func if isinstance(body, functools.partial) else body
    return pl.pallas_call(
        body,
        name=inner.__name__,
        out_shape=outs,
        in_specs=in_specs,
        out_specs=out_specs,
        scratch_shapes=scratch,
        compiler_params=pltpu.CompilerParams(vmem_limit_bytes=vmem),
        cost_estimate=pl.CostEstimate(flops=int(flops), bytes_accessed=0, transcendentals=0),
    )


def position():
    return lax.axis_index("segment"), lax.axis_index("dom") & 1


def dot(a, b):
    return jnp.dot(a, b, preferred_element_type=F32)


def aligned(start, unit):
    return start if isinstance(start, int) else pl.multiple_of(start, unit)


def normed(hf, gain):
    meansq = jnp.mean(hf * hf, axis=-1, keepdims=True)
    return (hf * lax.rsqrt(meansq + 1e-05) * gain).astype(BF16)


def stepped(h, z):
    half = 0.5 * z
    return (h.astype(F32) + half + half * jnp.tanh(half)).astype(BF16)


def start_one(choices, dst, sem):
    for condition, source in choices:

        @pl.when(condition)
        def _():
            pltpu.make_async_copy(source, dst, sem).start()

    return pltpu.make_async_copy(choices[0][1], dst, sem)


def source_of(seg, section, half):
    near, far = 1 + half, 2 - half
    via = seg ^ far
    passed = jnp.logical_or(via == 1, via == 2)
    second = jnp.where(passed, seg ^ 3, via)
    return jnp.where(seg == section, 0, jnp.where((seg ^ near) == section, 1, jnp.where(second == section, 2, 3)))


def fetch_half(seg, core, section, half, own, mine, theirs, dst, sem):
    width = dst.shape[1]
    source = source_of(seg, section, half)
    choices = [(source == 0, own.at[pl.ds(half * width, width), :])]
    for here, refs in ((core == half, mine), (core != half, theirs)):
        for i, ref in enumerate(refs):
            choices.append((jnp.logical_and(here, source == i + 1), ref.at[pl.ds(0, width), :]))
    return [start_one(choices, dst, sem)]


def fetch_cross(seg, core, section, own, mine, dst, sems):
    tile = dst.shape[0]
    width = dst.shape[1]
    blocks = own.shape[0]
    source = jnp.where(core == 0, source_of(seg, section, 0), source_of(seg, section, 1))
    for i, ref in enumerate(mine):

        @pl.when(source == i + 1)
        def _():
            for b in range(blocks):
                part = ref.at[pl.ds(width, tile), pl.ds(b * tile, tile)]
                pltpu.make_async_copy(part, dst.at[:, pl.ds(b * tile, tile)], sems.at[b]).start()

    @pl.when(source == 0)
    def _():
        for b in range(blocks):
            pltpu.make_async_copy(own.at[b], dst.at[:, pl.ds(b * tile, tile)], sems.at[b]).start()

    return [pltpu.make_async_copy(own.at[b], dst.at[:, pl.ds(b * tile, tile)], sems.at[b]) for b in range(blocks)]


def fetch_layer(section, step, ids, cands, top, bottom, cross, sems):
    own, own_cross, mine, theirs = cands
    seg, core = ids[0], ids[1]
    return (
        fetch_half(seg, core, section, 0, own.at[step], mine, theirs, top, sems.at[0])
        + fetch_half(seg, core, section, 1, own.at[step], mine, theirs, bottom, sems.at[1])
        + fetch_cross(seg, core, section, own_cross.at[step], mine, cross, sems.at[pl.ds(2, own_cross.shape[1])])
    )


def cands_of(refs):
    n = (len(refs) - 2) // 2
    return refs[0], refs[1], refs[2 : 2 + n], refs[2 + n :]


def first_kernel(dep, cols, counts, feat_ref, tiles_ref, s0, s1, s2, s3, h_ref, adj_ref, x_ref, sent_ref, small_ref, pick_ref, sem):
    ids = position()
    nblk, slots, tile, _ = tiles_ref.shape
    nodes, width = h_ref.shape
    seg = ids[0]
    copy = pltpu.make_async_copy(feat_ref.at[seg], h_ref, sem)
    copy.start()
    for r in range(nblk):
        for j in range(nblk):
            total = jnp.zeros((tile, tile), F32)
            for k in range(slots):
                used = jnp.logical_and(k < counts[r], cols[r, k] == j)
                total = total + jnp.where(used, tiles_ref[r, k].astype(F32), 0.0)
            adj_ref[r * tile : (r + 1) * tile, j * tile : (j + 1) * tile] = total.astype(BF16)
    for r, ref in enumerate((s0, s1, s2, s3)):
        small_ref[seg ^ r] = ref[...]
    sections, steps = small_ref.shape[:2]
    bound = small_ref.shape[2] - 2 * width
    for k in range(sections):
        for p in range(steps):
            rows = small_ref[k, p : p + 1, 2 * width :]
            index = lax.broadcasted_iota(jnp.int32, (nodes, bound), 0).astype(F32)
            pick_ref[k, p] = jnp.where(index == rows, 1.0, 0.0).T.astype(BF16)
    copy.wait()
    x = normed(h_ref[...].astype(F32), small_ref[0, 0:1, width : 2 * width])
    x_ref[...] = x
    sent_ref[...] = dot(pick_ref[0, 0], x).astype(BF16)


def payload_kernel(own, cross, *refs):
    outs, sems = refs[:-1], refs[-1]
    copies = []
    for p, out_ref in enumerate(outs):
        width = out_ref.shape[1]
        tile = cross.shape[-1]
        copies.append(pltpu.make_async_copy(own.at[p], out_ref.at[pl.ds(0, width), :], sems.at[p, 0]))
        for b in range(cross.shape[1]):
            dst = out_ref.at[pl.ds(width, tile), pl.ds(b * tile, tile)]
            copies.append(pltpu.make_async_copy(cross.at[p, b], dst, sems.at[p, b + 1]))
    for copy in copies:
        copy.start()
    for copy in copies:
        copy.wait()


def select_kernel(wanted, *refs):
    ids = position()
    count = len(wanted)
    outs, sources = refs[-count:], refs
    rows = sources[0].shape[0]
    for out_ref, rule in zip(outs, wanted):
        if out_ref.shape[0] > rows:
            out_ref[rows:, :] = jnp.zeros((out_ref.shape[0] - rows, out_ref.shape[1]), out_ref.dtype)
        for i, segments in enumerate(rule):
            here = functools.reduce(jnp.logical_or, [ids[0] == s for s in segments])

            @pl.when(here)
            def _():
                out_ref[:rows, :] = sources[i][...]


def select(sources, wanted, deps=(), extra=0):
    rows, columns = sources[0].shape
    shape = jax.ShapeDtypeStruct((rows + extra, columns), sources[0].dtype)
    specs = [VM] * len(sources) + [ANY] * len(deps)
    return call(functools.partial(select_kernel, wanted), [shape] * len(wanted), specs, vmem=8 * 2**20)(*sources, *deps)


def tie(value, *deps):
    return pl.pallas_call(
        lambda *refs: None,
        name="tie",
        out_shape=jax.ShapeDtypeStruct(value.shape, value.dtype),
        in_specs=[ANY] * (1 + len(deps)),
        out_specs=ANY,
        input_output_aliases={0: 0},
        compiler_params=pltpu.CompilerParams(vmem_limit_bytes=2**20),
    )(value, *deps)


def top_kernel(dep, in_ref, out_ref):
    out_ref[...] = in_ref[: out_ref.shape[0], :]


def load_kernel(section, dep, *refs):
    ids = position()
    w_ref, c_ref, sems = refs[-3:]
    width = w_ref.shape[1]
    parts = w_ref.at[pl.ds(0, width), :], w_ref.at[pl.ds(width, width), :]
    for copy in fetch_layer(section, 0, ids, cands_of(refs[:-3]), *parts, c_ref, sems):
        copy.wait()


def edge_kernel(section, x_ref, h_ref, adj_ref, w_ref, c_ref, small_ref, pick_ref, agg_ref, z_ref, cross_ref, h_out):
    width = x_ref.shape[1]
    pick = pick_ref[section, 1]
    x = x_ref[...]
    adj = dot(pick, adj_ref[...]).astype(BF16)
    agg_ref[...] = dot(adj, x)
    xb = dot(pick, x).astype(BF16)
    z_ref[...] = dot(xb, w_ref[:width, :]) + small_ref[section, 0:1, :width]
    tile = c_ref.shape[0]
    cross = jnp.zeros((pick.shape[0], tile), F32)
    for b in range(c_ref.shape[1] // tile):
        lanes = slice(b * tile, (b + 1) * tile)
        cross = cross + dot(pick[:, lanes], c_ref[:, lanes])
    cross_ref[...] = cross.astype(BF16)
    h_out[...] = dot(pick, h_ref[...]).astype(BF16)


def send_kernel(section, recv_ref, agg_ref, z_ref, cross_ref, h_ref, w_ref, small_ref, sent_ref):
    width = h_ref.shape[1]
    agg = (agg_ref[...] + dot(cross_ref[...], recv_ref[...])).astype(BF16)
    z = z_ref[...] + dot(agg, w_ref[width:, :])
    h = stepped(h_ref[...], z)
    sent_ref[...] = normed(h.astype(F32), small_ref[section, 1:2, width : 2 * width])


def remote(c_ref, recv, i, block):
    tile = c_ref.shape[0]
    parts = []
    for b in range(block // tile):
        lanes = pl.ds(aligned(i * block + b * tile, tile), tile)
        parts.append(dot(c_ref[:, lanes], recv))
    return jnp.concatenate(parts, axis=0)


def even_kernel(section, x_ref, h_ref, adj_ref, recv_ref, w_ref, c_ref, small_ref, dep, h_out, x_out):
    nodes, width = x_ref.shape
    block = 256

    def even(i, carry):
        rows = pl.ds(aligned(i * block, block), block)
        agg = dot(adj_ref[rows, :], x_ref[...]) + remote(c_ref, recv_ref[...], i, block)
        z = dot(x_ref[rows, :], w_ref[:width, :]) + small_ref[section, 0:1, :width]
        z = z + dot(agg.astype(BF16), w_ref[width:, :])
        h = stepped(h_ref[rows, :], z)
        h_out[rows, :] = h
        x_out[rows, :] = normed(h.astype(F32), small_ref[section, 1:2, width : 2 * width])
        return carry

    lax.fori_loop(0, nodes // block, even, 0)


def odd_kernel(section, fetch, dep, x_ref, adj_ref, small_ref, *refs):
    ids = position()
    if fetch:
        z_out, w2_out, c_out, w_out, next_c_out, w1_ref, sems, next_sems = refs[-8:]
        cands, ahead = refs[: fetch], refs[fetch:-8]
    else:
        z_out, w2_out, c_out, w1_ref, sems = refs[-5:]
        cands = refs[:-5]
    nodes, width = x_ref.shape
    block = 256
    copies = fetch_layer(section, 1, ids, cands_of(cands), w1_ref, w2_out, c_out, sems)
    if fetch:
        parts = w_out.at[pl.ds(0, width), :], w_out.at[pl.ds(width, width), :]
        copies += fetch_layer(section + 1, 0, ids, cands_of(ahead), *parts, next_c_out, next_sems)
    copies[0].wait()
    copies[1].wait()

    def odd(i, carry):
        rows = pl.ds(aligned(i * block, block), block)
        agg = dot(adj_ref[rows, :], x_ref[...]).astype(BF16)
        z = dot(x_ref[rows, :], w1_ref[...]) + small_ref[section, 1:2, :width]
        z_out[rows, :] = z + dot(agg, w2_out[...])
        return carry

    lax.fori_loop(0, nodes // block, odd, 0)
    for copy in copies[2:]:
        copy.wait()


def finish_kernel(section, last, recv_ref, z_ref, w2_ref, c_ref, h_ref, small_ref, pick_ref, *refs):
    nodes, width = h_ref.shape
    block = 256
    ids = position()
    if last:
        ends, (h_out, *pays) = refs[:section], refs[section:]
        for k, end_ref in enumerate(ends):
            for r, pay_ref in enumerate(pays, 1):

                @pl.when(ids[0] == k ^ r)
                def _():
                    pay_ref[:nodes, :] = end_ref[...]

        for pay_ref in pays:
            pay_ref[nodes:, :] = jnp.zeros((pay_ref.shape[0] - nodes, width), BF16)
    else:
        h_out, x_out, sent_out = refs
    seen = dot(recv_ref[...], w2_ref[...]).astype(BF16)
    for i in range(nodes // block):
        rows = pl.ds(i * block, block)
        z = z_ref[rows, :] + remote(c_ref, seen, i, block)
        h = stepped(h_ref[rows, :], z)
        h_out[rows, :] = h
        if last:
            for r, pay_ref in enumerate(pays, 1):

                @pl.when(ids[0] == section ^ r)
                def _():
                    pay_ref[rows, :] = h
        else:
            x_out[rows, :] = normed(h.astype(F32), small_ref[section + 1, 0:1, width : 2 * width])
    if not last:
        sent_out[...] = dot(pick_ref[section + 1, 0], x_out[...]).astype(BF16)


def collect_early_kernel(*refs):
    ids = position()
    out_ref, sem = refs[-2:]
    start_one([(ids[0] == k, end) for k, end in enumerate(refs[:-2])], out_ref.at[0, ids[0]], sem).wait()


def collect_last_kernel(one_ref, two_ref, three_ref, first_ref, early_ref, later_ref, _, out_ref, sems):
    ids = position()
    last = out_ref.shape[1] - 1
    rows = pl.ds(0, out_ref.shape[2])
    copies = [
        pltpu.make_async_copy(ref.at[rows, :], out_ref.at[0, ids[0] ^ r], sems.at[r]) for r, ref in ((1, one_ref), (2, two_ref))
    ]
    for copy in copies:
        copy.start()
    choices = [
        (ids[0] == last, three_ref),
        (ids[0] < 2, first_ref.at[rows, :]),
        (jnp.logical_and(ids[0] == 2, ids[1] == 0), early_ref.at[rows, :]),
        (jnp.logical_and(ids[0] == 2, ids[1] != 0), later_ref.at[rows, :]),
    ]
    copies.append(start_one(choices, out_ref.at[0, ids[0] ^ 3], sems.at[3]))
    for copy in copies:
        copy.wait()


def shards(features, weights, bias, gain, tile_val, tile_col, tile_count, cross_val, send_rows):
    sections = lax.axis_size("segment")
    doms = lax.axis_size("dom")
    seg = lax.axis_index("segment")
    core = lax.axis_index("dom") & 1
    steps, _, width = weights.shape
    nodes = features.shape[1]
    bound = send_rows.shape[1]
    nbits = doms.bit_length() - 1

    def moved(value, target, sources=range(sections)):
        pairs = []
        for s in sources:
            for d in range(doms):
                t, e = target(s, d)
                pairs.append((s * doms + d, t * doms + e))
        return lax.ppermute(value, ("segment", "dom"), pairs)

    def near(s, d):
        return s ^ (1 + (d & 1)), d

    def far(s, d):
        return s ^ (2 - (d & 1)), d

    def sibling(s, d):
        return s, d ^ 1

    def across(r):
        return lambda s, d: (s ^ r, d)

    def exchange(sent, step):
        bit = step * (nbits - 1) // max(steps - 1, 1)
        return lax.ppermute(sent, "dom", [(i, i ^ 1 << bit) for i in range(doms)])

    mat = jax.ShapeDtypeStruct((nodes, width), BF16)
    mat32 = jax.ShapeDtypeStruct((nodes, width), F32)
    tall = jax.ShapeDtypeStruct((nodes + 32, width), BF16)
    edge = jax.ShapeDtypeStruct((bound, width), BF16)
    edge32 = jax.ShapeDtypeStruct((bound, width), F32)
    half = jax.ShapeDtypeStruct((width, width), BF16)
    both = jax.ShapeDtypeStruct((2 * width, width), BF16)
    load = jax.ShapeDtypeStruct((width + bound, width), BF16)
    picks = jax.ShapeDtypeStruct((sections, steps, bound, nodes), BF16)
    unit = 2 * nodes * width * width
    dmas = pltpu.SemaphoreType.DMA((2 + cross_val.shape[1],))

    own = call(
        payload_kernel,
        [load] * steps,
        [ANY, ANY],
        scratch=[pltpu.SemaphoreType.DMA((steps, 1 + cross_val.shape[1]))],
    )(lax.dynamic_slice_in_dim(weights, core * width, width, axis=1), cross_val)
    small = tie(jnp.concatenate([bias, gain, send_rows.astype(F32)], axis=1), own[0])
    smalls = [small] + [moved(small, across(r)) for r in range(1, sections)]
    inner, outer = (1, 2), (0, 3)
    a0, a1 = [moved(v, near) for v in own]
    (pay,) = select([a0, own[0]], [(inner, outer)])
    b0 = moved(pay, far)
    (pay,) = select([a1, own[1]], [(inner, outer)], [pay, *smalls[1:]])
    b1 = moved(pay, far)
    issued = pay
    (pay,) = select([own[0], a0], [(inner, outer)], [pay])
    c0 = moved(pay, far)
    (pay,) = select([own[1], a1], [(inner, outer)], [pay])
    c1 = moved(pay, far)
    h, adj, x, sent, small, pick = call(
        first_kernel,
        (mat, jax.ShapeDtypeStruct((nodes, nodes), BF16), mat, edge, jax.ShapeDtypeStruct((sections,) + small.shape, F32), picks),
        [ANY, SM, SM, HBM, VM] + [VM] * sections,
        scratch=[pltpu.SemaphoreType.DMA],
    )(issued, tile_col, tile_count, features, tile_val, *smalls)
    recv = exchange(sent, 0)

    sa0 = moved(call(top_kernel, half, [ANY, VM])(issued, a0), sibling)
    sb0 = moved(call(top_kernel, half, [ANY, VM])(issued, b0), sibling)
    brought, swapped = [[a0, b0], [a1]], [[sa0, sb0], []]

    def candidates(p):
        return [weights, cross_val, *brought[p], *swapped[p]]

    def loaded(section, dep):
        cands = candidates(0)
        specs = [ANY, HBM, HBM] + [ANY] * (len(cands) - 2)
        kernel = functools.partial(load_kernel, section)
        return call(kernel, (both, edge), specs, scratch=[dmas])(dep, *cands)

    w, c = loaded(0, pay)

    ends = []
    last_segment = sections - 1
    for k in range(sections):
        last = k == sections - 1
        if k > 0:
            recv = exchange(sent, 0)
        if k == 1:
            w, c = loaded(1, x)
        edges = call(
            functools.partial(edge_kernel, k),
            (edge32, edge32, jax.ShapeDtypeStruct((bound, bound), BF16), edge),
            [VM] * 7,
            flops=LOAD * unit / 4,
        )(x, h, adj, w, c, small, pick)
        sent = call(functools.partial(send_kernel, k), edge, [VM] * 7, flops=LOAD * unit / 4)(recv, *edges[:3], edges[3], w, small)
        recv2 = exchange(sent, 1)
        if k == 1:
            brought[1].append(tie(c1, sent))
            swapped[1].append(moved(brought[1][2], sibling))
        h, x = call(functools.partial(even_kernel, k), (mat, mat), [VM] * 7 + [ANY], flops=LOAD * unit)(
            x, h, adj, recv, w, c, small, sent
        )
        if k == 0:
            brought[1] = [tie(a1, sent), tie(b1, sent)]
            swapped[1] = [moved(v, sibling) for v in brought[1]]
        cands = candidates(1)
        ahead = candidates(0) if k in range(1, sections - 1) else []
        fetch = len(cands) if ahead else 0
        specs = [([HBM, HBM] + [ANY] * (len(v) - 2) if v else []) for v in (cands, ahead)]
        z, w2, c2, *loads = call(
            functools.partial(odd_kernel, k, fetch),
            (mat32, half, edge) + ((both, edge) if ahead else ()),
            [ANY] + [VM] * 3 + specs[0] + specs[1],
            scratch=[pltpu.VMEM((width, width), BF16), dmas] + ([dmas] if ahead else []),
            flops=(20 if k > 1 else LOAD) * unit,
        )(c0 if k == 0 else first_two if last else x, x, adj, small, *cands, *ahead)
        if k == 0:
            brought[0].append(tie(c0, recv2, z))
            swapped[0].append(moved(call(top_kernel, half, [ANY, VM])(z, brought[0][2]), sibling))
        if k == 2:
            (pay,) = select(ends, [[(j ^ 3,) for j in range(2)]], [x], extra=16)
            first_two = moved(pay, across(3), [j ^ 3 for j in range(2)])
        if last:
            (pay,) = select(ends[2:], [[(2 ^ 3,)]], [x], extra=16)
            others = [2 ^ 3]
            early = moved(pay, lambda s, d: (s ^ (2 if d & 1 else 3), d), others)
        out = call(
            functools.partial(finish_kernel, k, last),
            (mat, tall, tall) if last else (mat, mat, edge),
            [VM] * 7 + ([VM] * len(ends) if last else []),
            flops=LOAD * unit,
        )(recv2, z, w2, c2, h, small, pick, *(ends if last else []))
        ends.append(out[0])
        if not last:
            h, x, sent = out
        if ahead:
            w, c = loads
    hop = moved(ends[-1], near, [last_segment ^ 3])
    two = moved(out[2], across(2))
    one = moved(out[1], across(1))
    def onward(value, between, sources, parity=None):
        pairs = []
        for s in sources:
            for d in range(doms):
                if parity is None or d & 1 == parity:
                    pairs.append((between(s, d) * doms + d, (s ^ 3) * doms + d))
        return lax.ppermute(value, ("segment", "dom"), pairs)

    three = onward(tie(hop, early), lambda s, d: near(s, d)[0], [last_segment ^ 3])
    later = onward(early, lambda s, d: s ^ 2, others, 1)
    whole = jax.ShapeDtypeStruct((1, sections, nodes, width), BF16)
    sems = [pltpu.SemaphoreType.DMA((sections,))]
    partly = call(
        collect_early_kernel, whole, [ANY] * sections, scratch=[pltpu.SemaphoreType.DMA], out_specs=ANY
    )(*ends)
    return pl.pallas_call(
        collect_last_kernel,
        name="collect_last_kernel",
        out_shape=whole,
        in_specs=[ANY] * 7,
        out_specs=ANY,
        scratch_shapes=sems,
        input_output_aliases={6: 0},
        compiler_params=pltpu.CompilerParams(vmem_limit_bytes=2**20),
    )(one, two, three, first_two, early, later, partly)


def solution(mesh):
    in_specs = (
        P(None, "dom", None),
        P("segment", None, None),
        P("segment", None),
        P("segment", None),
        P("dom", None, None, None),
        P("dom", None),
        P("dom"),
        P("segment", "dom", None, None),
        P("segment", "dom"),
    )
    out_specs = P("segment", None, "dom", None)
    return jax.shard_map(shards, mesh=mesh, in_specs=in_specs, out_specs=out_specs, check_vma=False)
```

```python
import functools

import jax
import jax.numpy as jnp
from jax import lax
from jax.experimental import pallas as pl
from jax.experimental.pallas import tpu as pltpu
from jax.sharding import PartitionSpec as P

F32 = jnp.float32
BF16 = jnp.bfloat16
VMEM_BYTES = 12 * 2**20
LOAD = 0.5
VM = pl.BlockSpec(memory_space=pltpu.VMEM)
SM = pl.BlockSpec(memory_space=pltpu.SMEM)
ANY = pl.BlockSpec(memory_space=pl.ANY)
HBM = pl.BlockSpec(memory_space=pltpu.HBM)


def call(body, outs, in_specs, scratch=(), out_specs=None, flops=0, vmem=VMEM_BYTES):
    if out_specs is None:
        out_specs = jax.tree.map(lambda _: VM, outs)
    inner = body.func if isinstance(body, functools.partial) else body
    return pl.pallas_call(
        body,
        name=inner.__name__,
        out_shape=outs,
        in_specs=in_specs,
        out_specs=out_specs,
        scratch_shapes=scratch,
        compiler_params=pltpu.CompilerParams(vmem_limit_bytes=vmem),
        cost_estimate=pl.CostEstimate(flops=int(flops), bytes_accessed=0, transcendentals=0),
    )


def position():
    return lax.axis_index("segment"), lax.axis_index("dom") & 1


def dot(a, b):
    return jnp.dot(a, b, preferred_element_type=F32)


def aligned(start, unit):
    return start if isinstance(start, int) else pl.multiple_of(start, unit)


def normed(hf, gain):
    meansq = jnp.mean(hf * hf, axis=-1, keepdims=True)
    return (hf * lax.rsqrt(meansq + 1e-05) * gain).astype(BF16)


def stepped(h, z):
    half = 0.5 * z
    return (h.astype(F32) + half + half * jnp.tanh(half)).astype(BF16)


def start_one(choices, dst, sem):
    for condition, source in choices:

        @pl.when(condition)
        def _():
            pltpu.make_async_copy(source, dst, sem).start()

    return pltpu.make_async_copy(choices[0][1], dst, sem)


def source_of(seg, section, half):
    near, far = 1 + half, 2 - half
    via = seg ^ far
    passed = jnp.logical_or(via == 1, via == 2)
    second = jnp.where(passed, seg ^ 3, via)
    return jnp.where(seg == section, 0, jnp.where((seg ^ near) == section, 1, jnp.where(second == section, 2, 3)))


def fetch_half(seg, core, section, half, own, mine, theirs, dst, sem):
    width = dst.shape[1]
    source = source_of(seg, section, half)
    choices = [(source == 0, own.at[pl.ds(half * width, width), :])]
    for here, refs in ((core == half, mine), (core != half, theirs)):
        for i, ref in enumerate(refs):
            choices.append((jnp.logical_and(here, source == i + 1), ref.at[pl.ds(0, width), :]))
    return [start_one(choices, dst, sem)]


def fetch_cross(seg, core, section, own, mine, dst, sems):
    tile = dst.shape[0]
    width = dst.shape[1]
    blocks = own.shape[0]
    source = jnp.where(core == 0, source_of(seg, section, 0), source_of(seg, section, 1))
    for i, ref in enumerate(mine):

        @pl.when(source == i + 1)
        def _():
            for b in range(blocks):
                part = ref.at[pl.ds(width, tile), pl.ds(b * tile, tile)]
                pltpu.make_async_copy(part, dst.at[:, pl.ds(b * tile, tile)], sems.at[b]).start()

    @pl.when(source == 0)
    def _():
        for b in range(blocks):
            pltpu.make_async_copy(own.at[b], dst.at[:, pl.ds(b * tile, tile)], sems.at[b]).start()

    return [pltpu.make_async_copy(own.at[b], dst.at[:, pl.ds(b * tile, tile)], sems.at[b]) for b in range(blocks)]


def fetch_layer(section, step, ids, cands, top, bottom, cross, sems):
    own, own_cross, mine, theirs = cands
    seg, core = ids[0], ids[1]
    return (
        fetch_half(seg, core, section, 0, own.at[step], mine, theirs, top, sems.at[0])
        + fetch_half(seg, core, section, 1, own.at[step], mine, theirs, bottom, sems.at[1])
        + fetch_cross(seg, core, section, own_cross.at[step], mine, cross, sems.at[pl.ds(2, own_cross.shape[1])])
    )


def cands_of(refs):
    n = (len(refs) - 2) // 2
    return refs[0], refs[1], refs[2 : 2 + n], refs[2 + n :]


def first_kernel(dep, cols, counts, feat_ref, tiles_ref, s0, s1, s2, s3, h_ref, adj_ref, x_ref, sent_ref, small_ref, pick_ref, sem):
    ids = position()
    nblk, slots, tile, _ = tiles_ref.shape
    nodes, width = h_ref.shape
    seg = ids[0]
    copy = pltpu.make_async_copy(feat_ref.at[seg], h_ref, sem)
    copy.start()
    for r in range(nblk):
        for j in range(nblk):
            total = jnp.zeros((tile, tile), F32)
            for k in range(slots):
                used = jnp.logical_and(k < counts[r], cols[r, k] == j)
                total = total + jnp.where(used, tiles_ref[r, k].astype(F32), 0.0)
            adj_ref[r * tile : (r + 1) * tile, j * tile : (j + 1) * tile] = total.astype(BF16)
    for r, ref in enumerate((s0, s1, s2, s3)):
        small_ref[seg ^ r] = ref[...]
    sections, steps = small_ref.shape[:2]
    bound = small_ref.shape[2] - 2 * width
    for k in range(sections):
        for p in range(steps):
            rows = small_ref[k, p : p + 1, 2 * width :]
            index = lax.broadcasted_iota(jnp.int32, (nodes, bound), 0).astype(F32)
            pick_ref[k, p] = jnp.where(index == rows, 1.0, 0.0).T.astype(BF16)
    copy.wait()
    x = normed(h_ref[...].astype(F32), small_ref[0, 0:1, width : 2 * width])
    x_ref[...] = x
    sent_ref[...] = dot(pick_ref[0, 0], x).astype(BF16)


def payload_kernel(own, cross, *refs):
    outs, sems = refs[:-1], refs[-1]
    copies = []
    for p, out_ref in enumerate(outs):
        width = out_ref.shape[1]
        tile = cross.shape[-1]
        copies.append(pltpu.make_async_copy(own.at[p], out_ref.at[pl.ds(0, width), :], sems.at[p, 0]))
        for b in range(cross.shape[1]):
            dst = out_ref.at[pl.ds(width, tile), pl.ds(b * tile, tile)]
            copies.append(pltpu.make_async_copy(cross.at[p, b], dst, sems.at[p, b + 1]))
    for copy in copies:
        copy.start()
    for copy in copies:
        copy.wait()


def select_kernel(wanted, *refs):
    ids = position()
    count = len(wanted)
    outs, sources = refs[-count:], refs
    rows = sources[0].shape[0]
    for out_ref, rule in zip(outs, wanted):
        if out_ref.shape[0] > rows:
            out_ref[rows:, :] = jnp.zeros((out_ref.shape[0] - rows, out_ref.shape[1]), out_ref.dtype)
        for i, segments in enumerate(rule):
            here = functools.reduce(jnp.logical_or, [ids[0] == s for s in segments])

            @pl.when(here)
            def _():
                out_ref[:rows, :] = sources[i][...]


def select(sources, wanted, deps=(), extra=0):
    rows, columns = sources[0].shape
    shape = jax.ShapeDtypeStruct((rows + extra, columns), sources[0].dtype)
    specs = [VM] * len(sources) + [ANY] * len(deps)
    return call(functools.partial(select_kernel, wanted), [shape] * len(wanted), specs, vmem=8 * 2**20)(*sources, *deps)


def tie(value, *deps):
    return pl.pallas_call(
        lambda *refs: None,
        name="tie",
        out_shape=jax.ShapeDtypeStruct(value.shape, value.dtype),
        in_specs=[ANY] * (1 + len(deps)),
        out_specs=ANY,
        input_output_aliases={0: 0},
        compiler_params=pltpu.CompilerParams(vmem_limit_bytes=2**20),
    )(value, *deps)


def top_kernel(dep, in_ref, out_ref):
    out_ref[...] = in_ref[: out_ref.shape[0], :]


def load_kernel(section, dep, *refs):
    ids = position()
    w_ref, c_ref, sems = refs[-3:]
    width = w_ref.shape[1]
    parts = w_ref.at[pl.ds(0, width), :], w_ref.at[pl.ds(width, width), :]
    for copy in fetch_layer(section, 0, ids, cands_of(refs[:-3]), *parts, c_ref, sems):
        copy.wait()


def edge_kernel(section, x_ref, h_ref, adj_ref, w_ref, c_ref, small_ref, pick_ref, agg_ref, z_ref, cross_ref, h_out):
    width = x_ref.shape[1]
    pick = pick_ref[section, 1]
    x = x_ref[...]
    adj = dot(pick, adj_ref[...]).astype(BF16)
    agg_ref[...] = dot(adj, x)
    xb = dot(pick, x).astype(BF16)
    z_ref[...] = dot(xb, w_ref[:width, :]) + small_ref[section, 0:1, :width]
    tile = c_ref.shape[0]
    cross = jnp.zeros((pick.shape[0], tile), F32)
    for b in range(c_ref.shape[1] // tile):
        lanes = slice(b * tile, (b + 1) * tile)
        cross = cross + dot(pick[:, lanes], c_ref[:, lanes])
    cross_ref[...] = cross.astype(BF16)
    h_out[...] = dot(pick, h_ref[...]).astype(BF16)


def send_kernel(section, recv_ref, agg_ref, z_ref, cross_ref, h_ref, w_ref, small_ref, sent_ref):
    width = h_ref.shape[1]
    agg = (agg_ref[...] + dot(cross_ref[...], recv_ref[...])).astype(BF16)
    z = z_ref[...] + dot(agg, w_ref[width:, :])
    h = stepped(h_ref[...], z)
    sent_ref[...] = normed(h.astype(F32), small_ref[section, 1:2, width : 2 * width])


def remote(c_ref, recv, i, block):
    tile = c_ref.shape[0]
    parts = []
    for b in range(block // tile):
        lanes = pl.ds(aligned(i * block + b * tile, tile), tile)
        parts.append(dot(c_ref[:, lanes], recv))
    return jnp.concatenate(parts, axis=0)


def even_kernel(section, x_ref, h_ref, adj_ref, recv_ref, w_ref, c_ref, small_ref, dep, h_out, x_out):
    nodes, width = x_ref.shape
    block = 256

    def even(i, carry):
        rows = pl.ds(aligned(i * block, block), block)
        agg = dot(adj_ref[rows, :], x_ref[...]) + remote(c_ref, recv_ref[...], i, block)
        z = dot(x_ref[rows, :], w_ref[:width, :]) + small_ref[section, 0:1, :width]
        z = z + dot(agg.astype(BF16), w_ref[width:, :])
        h = stepped(h_ref[rows, :], z)
        h_out[rows, :] = h
        x_out[rows, :] = normed(h.astype(F32), small_ref[section, 1:2, width : 2 * width])
        return carry

    lax.fori_loop(0, nodes // block, even, 0)


def odd_kernel(section, fetch, dep, x_ref, adj_ref, small_ref, *refs):
    ids = position()
    if fetch:
        z_out, w2_out, c_out, w_out, next_c_out, w1_ref, sems, next_sems = refs[-8:]
        cands, ahead = refs[: fetch], refs[fetch:-8]
    else:
        z_out, w2_out, c_out, w1_ref, sems = refs[-5:]
        cands = refs[:-5]
    nodes, width = x_ref.shape
    block = 256
    copies = fetch_layer(section, 1, ids, cands_of(cands), w1_ref, w2_out, c_out, sems)
    if fetch:
        parts = w_out.at[pl.ds(0, width), :], w_out.at[pl.ds(width, width), :]
        copies += fetch_layer(section + 1, 0, ids, cands_of(ahead), *parts, next_c_out, next_sems)
    copies[0].wait()
    copies[1].wait()

    def odd(i, carry):
        rows = pl.ds(aligned(i * block, block), block)
        agg = dot(adj_ref[rows, :], x_ref[...]).astype(BF16)
        z = dot(x_ref[rows, :], w1_ref[...]) + small_ref[section, 1:2, :width]
        z_out[rows, :] = z + dot(agg, w2_out[...])
        return carry

    lax.fori_loop(0, nodes // block, odd, 0)
    for copy in copies[2:]:
        copy.wait()


def finish_kernel(section, last, recv_ref, z_ref, w2_ref, c_ref, h_ref, small_ref, pick_ref, *refs):
    nodes, width = h_ref.shape
    block = 256
    ids = position()
    if last:
        ends, (h_out, *pays) = refs[:section], refs[section:]
        for k, end_ref in enumerate(ends):
            for r, pay_ref in enumerate(pays, 1):

                @pl.when(ids[0] == k ^ r)
                def _():
                    pay_ref[:nodes, :] = end_ref[...]

        for pay_ref in pays:
            pay_ref[nodes:, :] = jnp.zeros((pay_ref.shape[0] - nodes, width), BF16)
    else:
        h_out, x_out, sent_out = refs
    seen = dot(recv_ref[...], w2_ref[...]).astype(BF16)
    for i in range(nodes // block):
        rows = pl.ds(i * block, block)
        z = z_ref[rows, :] + remote(c_ref, seen, i, block)
        h = stepped(h_ref[rows, :], z)
        h_out[rows, :] = h
        if last:
            for r, pay_ref in enumerate(pays, 1):

                @pl.when(ids[0] == section ^ r)
                def _():
                    pay_ref[rows, :] = h
        else:
            x_out[rows, :] = normed(h.astype(F32), small_ref[section + 1, 0:1, width : 2 * width])
    if not last:
        sent_out[...] = dot(pick_ref[section + 1, 0], x_out[...]).astype(BF16)


def collect_early_kernel(*refs):
    ids = position()
    out_ref, sem = refs[-2:]
    start_one([(ids[0] == k, end) for k, end in enumerate(refs[:-2])], out_ref.at[0, ids[0]], sem).wait()


def collect_last_kernel(one_ref, two_ref, three_ref, first_ref, early_ref, later_ref, _, out_ref, sems):
    ids = position()
    last = out_ref.shape[1] - 1
    rows = pl.ds(0, out_ref.shape[2])
    copies = [
        pltpu.make_async_copy(ref.at[rows, :], out_ref.at[0, ids[0] ^ r], sems.at[r]) for r, ref in ((1, one_ref), (2, two_ref))
    ]
    for copy in copies:
        copy.start()
    choices = [
        (ids[0] == last, three_ref),
        (ids[0] < 2, first_ref.at[rows, :]),
        (jnp.logical_and(ids[0] == 2, ids[1] == 0), early_ref.at[rows, :]),
        (jnp.logical_and(ids[0] == 2, ids[1] != 0), later_ref.at[rows, :]),
    ]
    copies.append(start_one(choices, out_ref.at[0, ids[0] ^ 3], sems.at[3]))
    for copy in copies:
        copy.wait()


def shards(features, weights, bias, gain, tile_val, tile_col, tile_count, cross_val, send_rows):
    sections = lax.axis_size("segment")
    doms = lax.axis_size("dom")
    seg = lax.axis_index("segment")
    core = lax.axis_index("dom") & 1
    steps, _, width = weights.shape
    nodes = features.shape[1]
    bound = send_rows.shape[1]
    nbits = doms.bit_length() - 1

    def moved(value, target, sources=range(sections)):
        pairs = []
        for s in sources:
            for d in range(doms):
                t, e = target(s, d)
                pairs.append((s * doms + d, t * doms + e))
        return lax.ppermute(value, ("segment", "dom"), pairs)

    def near(s, d):
        return s ^ (1 + (d & 1)), d

    def far(s, d):
        return s ^ (2 - (d & 1)), d

    def sibling(s, d):
        return s, d ^ 1

    def across(r):
        return lambda s, d: (s ^ r, d)

    def exchange(sent, step):
        bit = step * (nbits - 1) // max(steps - 1, 1)
        return lax.ppermute(sent, "dom", [(i, i ^ 1 << bit) for i in range(doms)])

    mat = jax.ShapeDtypeStruct((nodes, width), BF16)
    mat32 = jax.ShapeDtypeStruct((nodes, width), F32)
    tall = jax.ShapeDtypeStruct((nodes + 16, width), BF16)
    edge = jax.ShapeDtypeStruct((bound, width), BF16)
    edge32 = jax.ShapeDtypeStruct((bound, width), F32)
    half = jax.ShapeDtypeStruct((width, width), BF16)
    both = jax.ShapeDtypeStruct((2 * width, width), BF16)
    load = jax.ShapeDtypeStruct((width + bound, width), BF16)
    picks = jax.ShapeDtypeStruct((sections, steps, bound, nodes), BF16)
    unit = 2 * nodes * width * width
    dmas = pltpu.SemaphoreType.DMA((2 + cross_val.shape[1],))

    own = call(
        payload_kernel,
        [load] * steps,
        [ANY, ANY],
        scratch=[pltpu.SemaphoreType.DMA((steps, 1 + cross_val.shape[1]))],
    )(lax.dynamic_slice_in_dim(weights, core * width, width, axis=1), cross_val)
    small = tie(jnp.concatenate([bias, gain, send_rows.astype(F32)], axis=1), own[0])
    smalls = [small] + [moved(small, across(r)) for r in range(1, sections)]
    inner, outer = (1, 2), (0, 3)
    a0, a1 = [moved(v, near) for v in own]
    (pay,) = select([a0, own[0]], [(inner, outer)])
    b0 = moved(pay, far)
    (pay,) = select([a1, own[1]], [(inner, outer)], [pay, *smalls[1:]])
    b1 = moved(pay, far)
    issued = pay
    (pay,) = select([own[0], a0], [(inner, outer)], [pay])
    c0 = moved(pay, far)
    (pay,) = select([own[1], a1], [(inner, outer)], [pay])
    c1 = moved(pay, far)
    h, adj, x, sent, small, pick = call(
        first_kernel,
        (mat, jax.ShapeDtypeStruct((nodes, nodes), BF16), mat, edge, jax.ShapeDtypeStruct((sections,) + small.shape, F32), picks),
        [ANY, SM, SM, HBM, VM] + [VM] * sections,
        scratch=[pltpu.SemaphoreType.DMA],
    )(issued, tile_col, tile_count, features, tile_val, *smalls)
    recv = exchange(sent, 0)

    sa0 = moved(call(top_kernel, half, [ANY, VM])(issued, a0), sibling)
    sb0 = moved(call(top_kernel, half, [ANY, VM])(issued, b0), sibling)
    brought, swapped = [[a0, b0], [a1]], [[sa0, sb0], []]

    def candidates(p):
        return [weights, cross_val, *brought[p], *swapped[p]]

    def loaded(section, dep):
        cands = candidates(0)
        specs = [ANY, HBM, HBM] + [ANY] * (len(cands) - 2)
        kernel = functools.partial(load_kernel, section)
        return call(kernel, (both, edge), specs, scratch=[dmas])(dep, *cands)

    w, c = loaded(0, pay)

    ends = []
    last_segment = sections - 1
    for k in range(sections):
        last = k == sections - 1
        if k > 0:
            recv = exchange(sent, 0)
        if k == 1:
            w, c = loaded(1, x)
        edges = call(
            functools.partial(edge_kernel, k),
            (edge32, edge32, jax.ShapeDtypeStruct((bound, bound), BF16), edge),
            [VM] * 7,
            flops=LOAD * unit / 4,
        )(x, h, adj, w, c, small, pick)
        sent = call(functools.partial(send_kernel, k), edge, [VM] * 7, flops=LOAD * unit / 4)(recv, *edges[:3], edges[3], w, small)
        recv2 = exchange(sent, 1)
        if k == 1:
            brought[1].append(tie(c1, sent))
            swapped[1].append(moved(call(top_kernel, half, [ANY, VM])(sent, brought[1][2]), sibling))
        h, x = call(functools.partial(even_kernel, k), (mat, mat), [VM] * 7 + [ANY], flops=LOAD * unit)(
            x, h, adj, recv, w, c, small, sent
        )
        if k == 0:
            brought[1] = [tie(a1, sent), tie(b1, sent)]
            swapped[1] = [moved(brought[1][0], sibling), moved(call(top_kernel, half, [ANY, VM])(sent, brought[1][1]), sibling)]
        cands = candidates(1)
        ahead = candidates(0) if k in range(1, sections - 1) else []
        fetch = len(cands) if ahead else 0
        specs = [([HBM, HBM] + [ANY] * (len(v) - 2) if v else []) for v in (cands, ahead)]
        z, w2, c2, *loads = call(
            functools.partial(odd_kernel, k, fetch),
            (mat32, half, edge) + ((both, edge) if ahead else ()),
            [ANY] + [VM] * 3 + specs[0] + specs[1],
            scratch=[pltpu.VMEM((width, width), BF16), dmas] + ([dmas] if ahead else []),
            flops=(20 if k > 1 else LOAD) * unit,
        )(c0 if k == 0 else first_two if last else x, x, adj, small, *cands, *ahead)
        if k == 0:
            brought[0].append(tie(c0, recv2, z))
            swapped[0].append(moved(call(top_kernel, half, [ANY, VM])(z, brought[0][2]), sibling))
        if k == 2:
            (pay,) = select(ends, [[(j ^ 3,) for j in range(2)]], [x])
            first_two = moved(pay, across(3), [j ^ 3 for j in range(2)])
        if last:
            (pay,) = select(ends[2:], [[(2 ^ 3,)]], [x], extra=16)
            others = [2 ^ 3]
            early = moved(pay, lambda s, d: (s ^ (2 if d & 1 else 3), d), others)
        out = call(
            functools.partial(finish_kernel, k, last),
            (mat, tall, tall) if last else (mat, mat, edge),
            [VM] * 7 + ([VM] * len(ends) if last else []),
            flops=LOAD * unit,
        )(recv2, z, w2, c2, h, small, pick, *(ends if last else []))
        ends.append(out[0])
        if not last:
            h, x, sent = out
        if ahead:
            w, c = loads
    hop = moved(ends[-1], near, [last_segment ^ 3])
    two = moved(out[2], across(2))
    one = moved(out[1], across(1))
    def onward(value, between, sources, parity=None):
        pairs = []
        for s in sources:
            for d in range(doms):
                if parity is None or d & 1 == parity:
                    pairs.append((between(s, d) * doms + d, (s ^ 3) * doms + d))
        return lax.ppermute(value, ("segment", "dom"), pairs)

    three = onward(tie(hop, early), lambda s, d: near(s, d)[0], [last_segment ^ 3])
    later = onward(early, lambda s, d: s ^ 2, others, 1)
    whole = jax.ShapeDtypeStruct((1, sections, nodes, width), BF16)
    sems = [pltpu.SemaphoreType.DMA((sections,))]
    partly = call(
        collect_early_kernel, whole, [ANY] * sections, scratch=[pltpu.SemaphoreType.DMA], out_specs=ANY
    )(*ends)
    return pl.pallas_call(
        collect_last_kernel,
        name="collect_last_kernel",
        out_shape=whole,
        in_specs=[ANY] * 7,
        out_specs=ANY,
        scratch_shapes=sems,
        input_output_aliases={6: 0},
        compiler_params=pltpu.CompilerParams(vmem_limit_bytes=2**20),
    )(one, two, three, first_two, early, later, partly)


def solution(mesh):
    in_specs = (
        P(None, "dom", None),
        P("segment", None, None),
        P("segment", None),
        P("segment", None),
        P("dom", None, None, None),
        P("dom", None),
        P("dom"),
        P("segment", "dom", None, None),
        P("segment", "dom"),
    )
    out_specs = P("segment", None, "dom", None)
    return jax.shard_map(shards, mesh=mesh, in_specs=in_specs, out_specs=out_specs, check_vma=False)
```

```python
import functools

import jax
import jax.numpy as jnp
from jax import lax
from jax.experimental import pallas as pl
from jax.experimental.pallas import tpu as pltpu
from jax.sharding import PartitionSpec as P

F32 = jnp.float32
BF16 = jnp.bfloat16
VMEM_BYTES = 12 * 2**20
LOAD = 0.5
VM = pl.BlockSpec(memory_space=pltpu.VMEM)
SM = pl.BlockSpec(memory_space=pltpu.SMEM)
ANY = pl.BlockSpec(memory_space=pl.ANY)
HBM = pl.BlockSpec(memory_space=pltpu.HBM)


def call(body, outs, in_specs, scratch=(), out_specs=None, flops=0, vmem=VMEM_BYTES):
    if out_specs is None:
        out_specs = jax.tree.map(lambda _: VM, outs)
    inner = body.func if isinstance(body, functools.partial) else body
    return pl.pallas_call(
        body,
        name=inner.__name__,
        out_shape=outs,
        in_specs=in_specs,
        out_specs=out_specs,
        scratch_shapes=scratch,
        compiler_params=pltpu.CompilerParams(vmem_limit_bytes=vmem),
        cost_estimate=pl.CostEstimate(flops=int(flops), bytes_accessed=0, transcendentals=0),
    )


def position():
    return lax.axis_index("segment"), lax.axis_index("dom") & 1


def dot(a, b):
    return jnp.dot(a, b, preferred_element_type=F32)


def aligned(start, unit):
    return start if isinstance(start, int) else pl.multiple_of(start, unit)


def normed(hf, gain):
    meansq = jnp.mean(hf * hf, axis=-1, keepdims=True)
    return (hf * lax.rsqrt(meansq + 1e-05) * gain).astype(BF16)


def stepped(h, z):
    half = 0.5 * z
    return (h.astype(F32) + half + half * jnp.tanh(half)).astype(BF16)


def start_one(choices, dst, sem):
    for condition, source in choices:

        @pl.when(condition)
        def _():
            pltpu.make_async_copy(source, dst, sem).start()

    return pltpu.make_async_copy(choices[0][1], dst, sem)


def source_of(seg, section, half):
    near, far = 1 + half, 2 - half
    via = seg ^ far
    passed = jnp.logical_or(via == 1, via == 2)
    second = jnp.where(passed, seg ^ 3, via)
    return jnp.where(seg == section, 0, jnp.where((seg ^ near) == section, 1, jnp.where(second == section, 2, 3)))


def fetch_half(seg, core, section, half, own, mine, theirs, dst, sem):
    width = dst.shape[1]
    source = source_of(seg, section, half)
    choices = [(source == 0, own.at[pl.ds(half * width, width), :])]
    for here, refs in ((core == half, mine), (core != half, theirs)):
        for i, ref in enumerate(refs):
            choices.append((jnp.logical_and(here, source == i + 1), ref.at[pl.ds(0, width), :]))
    return [start_one(choices, dst, sem)]


def fetch_cross(seg, core, section, own, mine, dst, sems):
    tile = dst.shape[0]
    width = dst.shape[1]
    blocks = own.shape[0]
    source = jnp.where(core == 0, source_of(seg, section, 0), source_of(seg, section, 1))
    for i, ref in enumerate(mine):

        @pl.when(source == i + 1)
        def _():
            for b in range(blocks):
                part = ref.at[pl.ds(width, tile), pl.ds(b * tile, tile)]
                pltpu.make_async_copy(part, dst.at[:, pl.ds(b * tile, tile)], sems.at[b]).start()

    @pl.when(source == 0)
    def _():
        for b in range(blocks):
            pltpu.make_async_copy(own.at[b], dst.at[:, pl.ds(b * tile, tile)], sems.at[b]).start()

    return [pltpu.make_async_copy(own.at[b], dst.at[:, pl.ds(b * tile, tile)], sems.at[b]) for b in range(blocks)]


def fetch_layer(section, step, ids, cands, top, bottom, cross, sems):
    own, own_cross, mine, theirs = cands
    seg, core = ids[0], ids[1]
    return (
        fetch_half(seg, core, section, 0, own.at[step], mine, theirs, top, sems.at[0])
        + fetch_half(seg, core, section, 1, own.at[step], mine, theirs, bottom, sems.at[1])
        + fetch_cross(seg, core, section, own_cross.at[step], mine, cross, sems.at[pl.ds(2, own_cross.shape[1])])
    )


def cands_of(refs):
    n = (len(refs) - 2) // 2
    return refs[0], refs[1], refs[2 : 2 + n], refs[2 + n :]


def first_kernel(dep, cols, counts, feat_ref, tiles_ref, s0, s1, s2, s3, h_ref, adj_ref, x_ref, sent_ref, small_ref, pick_ref, sem):
    ids = position()
    nblk, slots, tile, _ = tiles_ref.shape
    nodes, width = h_ref.shape
    seg = ids[0]
    copy = pltpu.make_async_copy(feat_ref.at[seg], h_ref, sem)
    copy.start()
    for r in range(nblk):
        for j in range(nblk):
            total = jnp.zeros((tile, tile), F32)
            for k in range(slots):
                used = jnp.logical_and(k < counts[r], cols[r, k] == j)
                total = total + jnp.where(used, tiles_ref[r, k].astype(F32), 0.0)
            adj_ref[r * tile : (r + 1) * tile, j * tile : (j + 1) * tile] = total.astype(BF16)
    for r, ref in enumerate((s0, s1, s2, s3)):
        small_ref[seg ^ r] = ref[...]
    sections, steps = small_ref.shape[:2]
    bound = small_ref.shape[2] - 2 * width
    for k in range(sections):
        for p in range(steps):
            rows = small_ref[k, p : p + 1, 2 * width :]
            index = lax.broadcasted_iota(jnp.int32, (nodes, bound), 0).astype(F32)
            pick_ref[k, p] = jnp.where(index == rows, 1.0, 0.0).T.astype(BF16)
    copy.wait()
    x = normed(h_ref[...].astype(F32), small_ref[0, 0:1, width : 2 * width])
    x_ref[...] = x
    sent_ref[...] = dot(pick_ref[0, 0], x).astype(BF16)


def payload_kernel(own, cross, *refs):
    outs, sems = refs[:-1], refs[-1]
    copies = []
    for p, out_ref in enumerate(outs):
        width = out_ref.shape[1]
        tile = cross.shape[-1]
        copies.append(pltpu.make_async_copy(own.at[p], out_ref.at[pl.ds(0, width), :], sems.at[p, 0]))
        for b in range(cross.shape[1]):
            dst = out_ref.at[pl.ds(width, tile), pl.ds(b * tile, tile)]
            copies.append(pltpu.make_async_copy(cross.at[p, b], dst, sems.at[p, b + 1]))
    for copy in copies:
        copy.start()
    for copy in copies:
        copy.wait()


def select_kernel(wanted, *refs):
    ids = position()
    count = len(wanted)
    outs, sources = refs[-count:], refs
    rows = sources[0].shape[0]
    for out_ref, rule in zip(outs, wanted):
        if out_ref.shape[0] > rows:
            out_ref[rows:, :] = jnp.zeros((out_ref.shape[0] - rows, out_ref.shape[1]), out_ref.dtype)
        for i, segments in enumerate(rule):
            here = functools.reduce(jnp.logical_or, [ids[0] == s for s in segments])

            @pl.when(here)
            def _():
                out_ref[:rows, :] = sources[i][...]


def select(sources, wanted, deps=(), extra=0):
    rows, columns = sources[0].shape
    shape = jax.ShapeDtypeStruct((rows + extra, columns), sources[0].dtype)
    specs = [VM] * len(sources) + [ANY] * len(deps)
    return call(functools.partial(select_kernel, wanted), [shape] * len(wanted), specs, vmem=8 * 2**20)(*sources, *deps)


def tie(value, *deps):
    return pl.pallas_call(
        lambda *refs: None,
        name="tie",
        out_shape=jax.ShapeDtypeStruct(value.shape, value.dtype),
        in_specs=[ANY] * (1 + len(deps)),
        out_specs=ANY,
        input_output_aliases={0: 0},
        compiler_params=pltpu.CompilerParams(vmem_limit_bytes=2**20),
    )(value, *deps)


def top_kernel(dep, in_ref, out_ref):
    out_ref[...] = in_ref[: out_ref.shape[0], :]


def load_kernel(section, dep, *refs):
    ids = position()
    w_ref, c_ref, sems = refs[-3:]
    width = w_ref.shape[1]
    parts = w_ref.at[pl.ds(0, width), :], w_ref.at[pl.ds(width, width), :]
    for copy in fetch_layer(section, 0, ids, cands_of(refs[:-3]), *parts, c_ref, sems):
        copy.wait()


def edge_kernel(section, x_ref, h_ref, adj_ref, w_ref, c_ref, small_ref, pick_ref, agg_ref, z_ref, cross_ref, h_out):
    width = x_ref.shape[1]
    pick = pick_ref[section, 1]
    x = x_ref[...]
    adj = dot(pick, adj_ref[...]).astype(BF16)
    agg_ref[...] = dot(adj, x)
    xb = dot(pick, x).astype(BF16)
    z_ref[...] = dot(xb, w_ref[:width, :]) + small_ref[section, 0:1, :width]
    tile = c_ref.shape[0]
    cross = jnp.zeros((pick.shape[0], tile), F32)
    for b in range(c_ref.shape[1] // tile):
        lanes = slice(b * tile, (b + 1) * tile)
        cross = cross + dot(pick[:, lanes], c_ref[:, lanes])
    cross_ref[...] = cross.astype(BF16)
    h_out[...] = dot(pick, h_ref[...]).astype(BF16)


def send_kernel(section, recv_ref, agg_ref, z_ref, cross_ref, h_ref, w_ref, small_ref, sent_ref):
    width = h_ref.shape[1]
    agg = (agg_ref[...] + dot(cross_ref[...], recv_ref[...])).astype(BF16)
    z = z_ref[...] + dot(agg, w_ref[width:, :])
    h = stepped(h_ref[...], z)
    sent_ref[...] = normed(h.astype(F32), small_ref[section, 1:2, width : 2 * width])


def remote(c_ref, recv, i, block):
    tile = c_ref.shape[0]
    parts = []
    for b in range(block // tile):
        lanes = pl.ds(aligned(i * block + b * tile, tile), tile)
        parts.append(dot(c_ref[:, lanes], recv))
    return jnp.concatenate(parts, axis=0)


def even_kernel(section, x_ref, h_ref, adj_ref, recv_ref, w_ref, c_ref, small_ref, dep, h_out, x_out):
    nodes, width = x_ref.shape
    block = 256

    def even(i, carry):
        rows = pl.ds(aligned(i * block, block), block)
        agg = dot(adj_ref[rows, :], x_ref[...]) + remote(c_ref, recv_ref[...], i, block)
        z = dot(x_ref[rows, :], w_ref[:width, :]) + small_ref[section, 0:1, :width]
        z = z + dot(agg.astype(BF16), w_ref[width:, :])
        h = stepped(h_ref[rows, :], z)
        h_out[rows, :] = h
        x_out[rows, :] = normed(h.astype(F32), small_ref[section, 1:2, width : 2 * width])
        return carry

    lax.fori_loop(0, nodes // block, even, 0)


def odd_kernel(section, fetch, dep, x_ref, adj_ref, small_ref, *refs):
    ids = position()
    if fetch:
        z_out, w2_out, c_out, w_out, next_c_out, w1_ref, sems, next_sems = refs[-8:]
        cands, ahead = refs[: fetch], refs[fetch:-8]
    else:
        z_out, w2_out, c_out, w1_ref, sems = refs[-5:]
        cands = refs[:-5]
    nodes, width = x_ref.shape
    block = 256
    copies = fetch_layer(section, 1, ids, cands_of(cands), w1_ref, w2_out, c_out, sems)
    if fetch:
        parts = w_out.at[pl.ds(0, width), :], w_out.at[pl.ds(width, width), :]
        copies += fetch_layer(section + 1, 0, ids, cands_of(ahead), *parts, next_c_out, next_sems)
    copies[0].wait()
    copies[1].wait()

    def odd(i, carry):
        rows = pl.ds(aligned(i * block, block), block)
        agg = dot(adj_ref[rows, :], x_ref[...]).astype(BF16)
        z = dot(x_ref[rows, :], w1_ref[...]) + small_ref[section, 1:2, :width]
        z_out[rows, :] = z + dot(agg, w2_out[...])
        return carry

    lax.fori_loop(0, nodes // block, odd, 0)
    for copy in copies[2:]:
        copy.wait()


def finish_kernel(section, last, recv_ref, z_ref, w2_ref, c_ref, h_ref, small_ref, pick_ref, *refs):
    nodes, width = h_ref.shape
    block = 256
    ids = position()
    if last:
        ends, (h_out, *pays) = refs[:section], refs[section:]
        for k, end_ref in enumerate(ends):
            for r, pay_ref in enumerate(pays, 1):

                @pl.when(ids[0] == k ^ r)
                def _():
                    pay_ref[:nodes, :] = end_ref[...]

        for pay_ref in pays:
            pay_ref[nodes:, :] = jnp.zeros((pay_ref.shape[0] - nodes, width), BF16)
    else:
        h_out, x_out, sent_out = refs
    seen = dot(recv_ref[...], w2_ref[...]).astype(BF16)
    for i in range(nodes // block):
        rows = pl.ds(i * block, block)
        z = z_ref[rows, :] + remote(c_ref, seen, i, block)
        h = stepped(h_ref[rows, :], z)
        h_out[rows, :] = h
        if last:
            for r, pay_ref in enumerate(pays, 1):

                @pl.when(ids[0] == section ^ r)
                def _():
                    pay_ref[rows, :] = h
        else:
            x_out[rows, :] = normed(h.astype(F32), small_ref[section + 1, 0:1, width : 2 * width])
    if not last:
        sent_out[...] = dot(pick_ref[section + 1, 0], x_out[...]).astype(BF16)


def collect_early_kernel(*refs):
    ids = position()
    out_ref, sem = refs[-2:]
    start_one([(ids[0] == k, end) for k, end in enumerate(refs[:-2])], out_ref.at[0, ids[0]], sem).wait()


def collect_last_kernel(one_ref, two_ref, three_ref, first_ref, early_ref, later_ref, _, out_ref, sems):
    ids = position()
    last = out_ref.shape[1] - 1
    rows = pl.ds(0, out_ref.shape[2])
    copies = [
        pltpu.make_async_copy(ref.at[rows, :], out_ref.at[0, ids[0] ^ r], sems.at[r]) for r, ref in ((1, one_ref), (2, two_ref))
    ]
    for copy in copies:
        copy.start()
    choices = [
        (ids[0] == last, three_ref),
        (ids[0] < 2, first_ref.at[rows, :]),
        (jnp.logical_and(ids[0] == 2, ids[1] == 0), early_ref.at[rows, :]),
        (jnp.logical_and(ids[0] == 2, ids[1] != 0), later_ref.at[rows, :]),
    ]
    copies.append(start_one(choices, out_ref.at[0, ids[0] ^ 3], sems.at[3]))
    for copy in copies:
        copy.wait()


def shards(features, weights, bias, gain, tile_val, tile_col, tile_count, cross_val, send_rows):
    sections = lax.axis_size("segment")
    doms = lax.axis_size("dom")
    seg = lax.axis_index("segment")
    core = lax.axis_index("dom") & 1
    steps, _, width = weights.shape
    nodes = features.shape[1]
    bound = send_rows.shape[1]
    nbits = doms.bit_length() - 1

    def moved(value, target, sources=range(sections)):
        pairs = []
        for s in sources:
            for d in range(doms):
                t, e = target(s, d)
                pairs.append((s * doms + d, t * doms + e))
        return lax.ppermute(value, ("segment", "dom"), pairs)

    def near(s, d):
        return s ^ (1 + (d & 1)), d

    def far(s, d):
        return s ^ (2 - (d & 1)), d

    def sibling(s, d):
        return s, d ^ 1

    def across(r):
        return lambda s, d: (s ^ r, d)

    def exchange(sent, step):
        bit = step * (nbits - 1) // max(steps - 1, 1)
        return lax.ppermute(sent, "dom", [(i, i ^ 1 << bit) for i in range(doms)])

    mat = jax.ShapeDtypeStruct((nodes, width), BF16)
    mat32 = jax.ShapeDtypeStruct((nodes, width), F32)
    tall = jax.ShapeDtypeStruct((nodes + 16, width), BF16)
    edge = jax.ShapeDtypeStruct((bound, width), BF16)
    edge32 = jax.ShapeDtypeStruct((bound, width), F32)
    half = jax.ShapeDtypeStruct((width, width), BF16)
    both = jax.ShapeDtypeStruct((2 * width, width), BF16)
    load = jax.ShapeDtypeStruct((width + bound, width), BF16)
    picks = jax.ShapeDtypeStruct((sections, steps, bound, nodes), BF16)
    unit = 2 * nodes * width * width
    dmas = pltpu.SemaphoreType.DMA((2 + cross_val.shape[1],))

    own = call(
        payload_kernel,
        [load] * steps,
        [ANY, ANY],
        scratch=[pltpu.SemaphoreType.DMA((steps, 1 + cross_val.shape[1]))],
    )(lax.dynamic_slice_in_dim(weights, core * width, width, axis=1), cross_val)
    small = tie(jnp.concatenate([bias, gain, send_rows.astype(F32)], axis=1), own[0])
    smalls = [small] + [moved(small, across(r)) for r in range(1, sections)]
    inner, outer = (1, 2), (0, 3)
    a0, a1 = [moved(v, near) for v in own]
    (pay,) = select([a0, own[0]], [(inner, outer)])
    b0 = moved(pay, far)
    (pay,) = select([a1, own[1]], [(inner, outer)], [pay, *smalls[1:]])
    b1 = moved(pay, far)
    issued = pay
    (pay,) = select([own[0], a0], [(inner, outer)], [pay])
    c0 = moved(pay, far)
    (pay,) = select([own[1], a1], [(inner, outer)], [pay])
    c1 = moved(pay, far)
    h, adj, x, sent, small, pick = call(
        first_kernel,
        (mat, jax.ShapeDtypeStruct((nodes, nodes), BF16), mat, edge, jax.ShapeDtypeStruct((sections,) + small.shape, F32), picks),
        [ANY, SM, SM, HBM, VM] + [VM] * sections,
        scratch=[pltpu.SemaphoreType.DMA],
    )(issued, tile_col, tile_count, features, tile_val, *smalls)
    recv = exchange(sent, 0)

    sa0 = moved(call(top_kernel, half, [ANY, VM])(issued, a0), sibling)
    sb0 = moved(call(top_kernel, half, [ANY, VM])(issued, b0), sibling)
    brought, swapped = [[a0, b0], [a1]], [[sa0, sb0], []]

    def candidates(p):
        return [weights, cross_val, *brought[p], *swapped[p]]

    def loaded(section, dep):
        cands = candidates(0)
        specs = [ANY, HBM, HBM] + [ANY] * (len(cands) - 2)
        kernel = functools.partial(load_kernel, section)
        return call(kernel, (both, edge), specs, scratch=[dmas])(dep, *cands)

    w, c = loaded(0, pay)

    ends = []
    last_segment = sections - 1
    for k in range(sections):
        last = k == sections - 1
        if k > 0:
            recv = exchange(sent, 0)
        if k == 1:
            w, c = loaded(1, x)
        edges = call(
            functools.partial(edge_kernel, k),
            (edge32, edge32, jax.ShapeDtypeStruct((bound, bound), BF16), edge),
            [VM] * 7,
            flops=LOAD * unit / 4,
        )(x, h, adj, w, c, small, pick)
        sent = call(functools.partial(send_kernel, k), edge, [VM] * 7, flops=LOAD * unit / 4)(recv, *edges[:3], edges[3], w, small)
        recv2 = exchange(sent, 1)
        if k == 1:
            brought[1].append(tie(c1, sent))
            swapped[1].append(moved(brought[1][2], sibling))
        h, x = call(functools.partial(even_kernel, k), (mat, mat), [VM] * 7 + [ANY], flops=LOAD * unit)(
            x, h, adj, recv, w, c, small, sent
        )
        if k == 0:
            brought[1] = [tie(a1, sent), tie(b1, sent)]
            swapped[1] = [moved(v, sibling) for v in brought[1]]
        cands = candidates(1)
        ahead = candidates(0) if k in range(1, sections - 1) else []
        fetch = len(cands) if ahead else 0
        specs = [([HBM, HBM] + [ANY] * (len(v) - 2) if v else []) for v in (cands, ahead)]
        z, w2, c2, *loads = call(
            functools.partial(odd_kernel, k, fetch),
            (mat32, half, edge) + ((both, edge) if ahead else ()),
            [ANY] + [VM] * 3 + specs[0] + specs[1],
            scratch=[pltpu.VMEM((width, width), BF16), dmas] + ([dmas] if ahead else []),
            flops=(20 if k > 1 else LOAD) * unit,
        )(c0 if k == 0 else first_two if last else x, x, adj, small, *cands, *ahead)
        if k == 0:
            brought[0].append(tie(c0, recv2, z))
            swapped[0].append(moved(call(top_kernel, half, [ANY, VM])(z, brought[0][2]), sibling))
        if k == 2:
            (pay,) = select(ends, [[(j ^ 3,) for j in range(2)]], [x])
            first_two = moved(pay, across(3), [j ^ 3 for j in range(2)])
        if last:
            (pay,) = select(ends[2:], [[(2 ^ 3,)]], [x], extra=16)
            others = [2 ^ 3]
            early = moved(pay, lambda s, d: (s ^ (2 if d & 1 else 3), d), others)
        out = call(
            functools.partial(finish_kernel, k, last),
            (mat, tall, tall) if last else (mat, mat, edge),
            [VM] * 7 + ([VM] * len(ends) if last else []),
            flops=LOAD * unit,
        )(recv2, z, w2, c2, h, small, pick, *(ends if last else []))
        ends.append(out[0])
        if not last:
            h, x, sent = out
        if ahead:
            w, c = loads
    hop = moved(ends[-1], near, [last_segment ^ 3])
    two = moved(out[2], across(2))
    one = moved(out[1], across(1))
    def onward(value, between, sources, parity=None):
        pairs = []
        for s in sources:
            for d in range(doms):
                if parity is None or d & 1 == parity:
                    pairs.append((between(s, d) * doms + d, (s ^ 3) * doms + d))
        return lax.ppermute(value, ("segment", "dom"), pairs)

    three = onward(tie(hop, early), lambda s, d: near(s, d)[0], [last_segment ^ 3])
    later = onward(early, lambda s, d: s ^ 2, others, 1)
    whole = jax.ShapeDtypeStruct((1, sections, nodes, width), BF16)
    sems = [pltpu.SemaphoreType.DMA((sections,))]
    partly = call(
        collect_early_kernel, whole, [ANY] * sections, scratch=[pltpu.SemaphoreType.DMA], out_specs=ANY
    )(*ends)
    return pl.pallas_call(
        collect_last_kernel,
        name="collect_last_kernel",
        out_shape=whole,
        in_specs=[ANY] * 7,
        out_specs=ANY,
        scratch_shapes=sems,
        input_output_aliases={6: 0},
        compiler_params=pltpu.CompilerParams(vmem_limit_bytes=2**20),
    )(one, two, three, first_two, early, later, partly)


def solution(mesh):
    in_specs = (
        P(None, "dom", None),
        P("segment", None, None),
        P("segment", None),
        P("segment", None),
        P("dom", None, None, None),
        P("dom", None),
        P("dom"),
        P("segment", "dom", None, None),
        P("segment", "dom"),
    )
    out_specs = P("segment", None, "dom", None)
    return jax.shard_map(shards, mesh=mesh, in_specs=in_specs, out_specs=out_specs, check_vma=False)
```
